32 devices in a mesh: slab: 8 (over z, y), col: 4 (over x, core).
Axes of the slice: x: 2, y: 2, z: 4, core: 2. Of those that a mesh axis runs over, the one named last changes fastest.
Arguments:
- wave_amplitudes: float32 [8, 512, 128], P('slab', 'col'), may hold values from -6 to 6
- energy_block_per_segment: float32 [8, 512, 512], P('slab', 'col'), as said below
- tunnel_coupling_block: float32 [8, 512, 512], P('slab', 'col'), may hold values from -0.25 to 0.25
- reduced_block_reciprocal: float32 [8, 2, 512, 512], P('slab', None, 'col'), may hold values from -0.1875 to 0.1875
- beneath_reduce_multiplier: float32 [8, 2, 512, 512], P('slab', None, 'col'), may hold values from -0.09375 to 0.09375
- above_reduce_multiplier: float32 [8, 2, 512, 512], P('slab', None, 'col'), may hold values from -0.09375 to 0.09375
- beneath_solve_multiplier: float32 [8, 2, 512, 512], P('slab', None, 'col'), may hold values from -0.09375 to 0.09375
- above_solve_multiplier: float32 [8, 2, 512, 512], P('slab', None, 'col'), may hold values from -0.09375 to 0.09375
Outputs:
- psi_next: float32 [8, 512, 128], P('slab', 'col')
The draws below stay inside these ranges and needn't reach their ends.
Inputs may be any that keep to these rules, and one draw needn't show every extreme that they name: energy_block_per_segment[s] is a symmetric matrix for every slab s.
All inputs are finite; a program needn't handle non-finite values.
Results may differ from the reference program's by a relative error of at most 0.00011.
Values sent between devices are 32-bit elements; how exact they have to be, the bound alone decides.
No kernel may reach another device: no remote copies, remote signals or barrier semaphores. Data moves between devices by JAX's collectives and lax.ppermute only.
A program may use at most 64 MiB of HBM per device.

```python
import jax
import jax.numpy as jnp
from jax import lax

BASIS_FUNCTIONS = 512
STATES = 64
SEGMENT_NUMBER = 8
LEVELS = 3


def draw_energy_block_per_segment(key, part):
    raw = jax.random.normal(key, (SEGMENT_NUMBER, BASIS_FUNCTIONS, BASIS_FUNCTIONS), jnp.float32)
    return (raw + jnp.swapaxes(raw, 1, 2)) * 0.5 ** 0.5 * BASIS_FUNCTIONS ** (-0.5)


def level_of(rng, shape, split, smallest, high):
    def one(dim, blocks):
        draws = jax.random.uniform(jax.random.fold_in(jax.random.fold_in(rng, 6), dim), (blocks,), jnp.float32, smallest / len(split), high / len(split))
        return jnp.repeat(jnp.exp(draws), shape[dim] // blocks).reshape((-1,) + (1,) * (len(shape) - dim - 1))

    factor_of = one(*split[0])
    for cut in split[1:]:
        factor_of = factor_of * one(*cut)
    return factor_of


def noise(rng, dims, scale, limit, split=(), kind=jnp.bfloat16):
    level = level_of(rng, dims, split, -0.22, 0.18) if split else 1.0
    values = jax.random.normal(rng, dims, jnp.float32) * scale * level
    return jnp.minimum(jnp.maximum(values, -limit), limit).astype(kind)


def setup_inputs(seed: int = 0) -> dict:
    streams_of = jax.random.split(jax.random.key(seed), 9)
    wave_amplitudes = noise(streams_of[0], (SEGMENT_NUMBER, BASIS_FUNCTIONS, 2 * STATES), 1.0, 6.0, ((0, 8), (1, 4)), jnp.float32)
    energy_block_per_segment = draw_energy_block_per_segment(jax.random.fold_in(streams_of[8], 71), 0)
    tunnel_coupling_block = noise(streams_of[2], (SEGMENT_NUMBER, BASIS_FUNCTIONS, BASIS_FUNCTIONS), BASIS_FUNCTIONS ** -0.5, 0.25, ((0, 8), (1, 4)), jnp.float32)
    reduced_block_reciprocal = noise(streams_of[3], (SEGMENT_NUMBER, 2, BASIS_FUNCTIONS, BASIS_FUNCTIONS), (2 * BASIS_FUNCTIONS) ** -0.5, 0.1875, ((0, 8), (2, 4)), jnp.float32)
    beneath_reduce_multiplier = noise(streams_of[4], (SEGMENT_NUMBER, 2, BASIS_FUNCTIONS, BASIS_FUNCTIONS), (8 * BASIS_FUNCTIONS) ** -0.5, 0.09375, ((0, 8), (2, 4)), jnp.float32)
    above_reduce_multiplier = noise(streams_of[5], (SEGMENT_NUMBER, 2, BASIS_FUNCTIONS, BASIS_FUNCTIONS), (8 * BASIS_FUNCTIONS) ** -0.5, 0.09375, ((0, 8), (2, 4)), jnp.float32)
    beneath_solve_multiplier = noise(streams_of[6], (SEGMENT_NUMBER, 2, BASIS_FUNCTIONS, BASIS_FUNCTIONS), (8 * BASIS_FUNCTIONS) ** -0.5, 0.09375, ((0, 8), (2, 4)), jnp.float32)
    above_solve_multiplier = noise(streams_of[7], (SEGMENT_NUMBER, 2, BASIS_FUNCTIONS, BASIS_FUNCTIONS), (8 * BASIS_FUNCTIONS) ** -0.5, 0.09375, ((0, 8), (2, 4)), jnp.float32)
    return {"wave_amplitudes": wave_amplitudes, "energy_block_per_segment": energy_block_per_segment, "tunnel_coupling_block": tunnel_coupling_block, "reduced_block_reciprocal": reduced_block_reciprocal, "beneath_reduce_multiplier": beneath_reduce_multiplier, "above_reduce_multiplier": above_reduce_multiplier, "beneath_solve_multiplier": beneath_solve_multiplier, "above_solve_multiplier": above_solve_multiplier}


half_step = 0.5
highest = lax.Precision.HIGHEST


def rotate(values):
    column = lax.broadcasted_iota(jnp.int32, values.shape, values.ndim - 1)
    return jnp.where(column % 2 == 0, -jnp.roll(values, -1, axis=-1), jnp.roll(values, 1, axis=-1))


def real_product(blocks, vectors):
    return jnp.einsum("smn,snk->smk", blocks, vectors, precision=highest)


def stacked_product_of_matrices(blocks, vectors):
    real_part = jnp.einsum("smn,snk->smk", blocks[:, 0], vectors, precision=highest)
    imag_part = jnp.einsum("smn,snk->smk", blocks[:, 1], vectors, precision=highest)
    return real_part + rotate(imag_part)


def reference(wave_amplitudes, energy_block_per_segment, tunnel_coupling_block, reduced_block_reciprocal, beneath_reduce_multiplier, above_reduce_multiplier, beneath_solve_multiplier, above_solve_multiplier):
    zero_slab = jnp.zeros_like(wave_amplitudes[:1])
    next_slab = jnp.concatenate([wave_amplitudes[1:], zero_slab], 0)
    prev_all = jnp.einsum("snm,snk->smk", tunnel_coupling_block, wave_amplitudes, precision=highest)
    prev_term = jnp.concatenate([zero_slab, prev_all[:-1]], 0)
    ham_psi = real_product(energy_block_per_segment, wave_amplitudes) + real_product(tunnel_coupling_block, next_slab) + prev_term
    reduced = wave_amplitudes - half_step * rotate(ham_psi)
    pivot_part = jnp.zeros_like(wave_amplitudes)
    for level_id in range(LEVELS):
        tier_spacing = 2 ** level_id
        present_tier = reduced[tier_spacing::2 * tier_spacing]
        pivot_piece = stacked_product_of_matrices(reduced_block_reciprocal[tier_spacing::2 * tier_spacing], present_tier)
        pivot_part = pivot_part.at[tier_spacing::2 * tier_spacing].set(pivot_piece)
        heading_beneath = stacked_product_of_matrices(beneath_reduce_multiplier[tier_spacing::2 * tier_spacing], present_tier)
        heading_above = stacked_product_of_matrices(above_reduce_multiplier[tier_spacing::2 * tier_spacing], present_tier)
        reduced = reduced.at[0::2 * tier_spacing].add(-heading_beneath)
        reduced = reduced.at[2 * tier_spacing::2 * tier_spacing].add(-heading_above[:-1])
    pivot_part = pivot_part.at[0].set(stacked_product_of_matrices(reduced_block_reciprocal[:1], reduced[:1])[0])
    solved = jnp.zeros_like(wave_amplitudes).at[0].set(pivot_part[0])
    for level_id in reversed(range(LEVELS)):
        tier_spacing = 2 ** level_id
        from_lower = solved[0::2 * tier_spacing]
        from_upper = jnp.concatenate([solved[2 * tier_spacing::2 * tier_spacing], zero_slab], 0)
        settled = pivot_part[tier_spacing::2 * tier_spacing] - stacked_product_of_matrices(beneath_solve_multiplier[tier_spacing::2 * tier_spacing], from_lower) - stacked_product_of_matrices(above_solve_multiplier[tier_spacing::2 * tier_spacing], from_upper)
        solved = solved.at[tier_spacing::2 * tier_spacing].set(settled)
    return solved
```

```python
import functools

import jax
import jax.numpy as jnp
from jax import lax
from jax.experimental import pallas as pl
from jax.experimental.pallas import tpu as pltpu
from jax.sharding import PartitionSpec as P


half_step = 0.5
wide = jnp.float32
short = jnp.bfloat16
Q = 128
LANES = 128


def lanes(values):
    return lax.broadcasted_iota(jnp.int32, values.shape, 1)


def swap_halves(values):
    return pltpu.roll(values, 64, 1)


def join(left, right):
    return jnp.where(lanes(left) < 64, left, right)


def rotate(values):
    even = lanes(values) % 2 == 0
    return jnp.where(even, -pltpu.roll(values, LANES - 1, 1), pltpu.roll(values, 1, 1))


def split(values):
    high = values.astype(short)
    return high, (values - high.astype(wide)).astype(short)


def quarter(number):
    return pl.ds(pl.multiple_of(number * Q, Q), Q)


def spread(store, packed, first):
    high = packed.astype(short).astype(wide)
    low = packed - high
    store[quarter(first), :] = join(high, swap_halves(low)).astype(short)
    store[quarter(first ^ 1), :] = join(swap_halves(high), low).astype(short)


def load_vector(store, near, far):
    c = lax.axis_index("col")
    spread(store, near[...], c)
    spread(store, far[...], c ^ 2)


def rows_product(block, store):
    high, low = split(block)
    vector = store[...]
    return jnp.dot(high, vector, preferred_element_type=wide) + jnp.dot(
        low, vector, preferred_element_type=wide
    )


def fold(values):
    return values + swap_halves(values)


def real_product(own, mate, store):
    return join(fold(rows_product(own, store)), fold(rows_product(mate, store)))


def complex_half(block, store):
    both = rows_product(block.reshape(2 * Q, block.shape[-1]), store)
    return fold(both[:Q] + rotate(both[Q:]))


def complex_product(own, mate, store):
    return join(complex_half(own, store), complex_half(mate, store))


def regroup_kernel(mine, other, out):
    c = lax.axis_index("col")
    rows = join(mine[...], other[...])
    out[...] = jnp.where(c % 2 == 0, rows, swap_halves(rows))


def pack_kernel(mine, other, out):
    c = lax.axis_index("col")
    near, far = mine[...], other[...]
    out[...] = jnp.where(
        c % 2 == 0, join(near, swap_halves(far)), join(swap_halves(near), far)
    )


def up_kernel(packed, own, mate, near, far, store):
    c = lax.axis_index("col")
    turned = packed[...].T
    total = None
    for rows, block in ((turned[:64], own[0]), (turned[64:], mate[0])):
        high, low = split(rows)
        pair = jnp.concatenate([high, low], axis=0)
        block_high, block_low = split(block)
        part = jnp.dot(pair, block_high, preferred_element_type=wide) + jnp.dot(
            pair, block_low, preferred_element_type=wide
        )
        part = part[:64] + part[64:]
        total = part if total is None else total + part
    store[...] = total
    for out, first in ((near, c), (far, c ^ 2)):
        pair = jnp.concatenate(
            [store[:, quarter(first)], store[:, quarter(first ^ 1)]], axis=0
        )
        out[...] = pair.T


def ham_kernel(near, far, next_near, next_far, own, mate, out, here, there):
    load_vector(here, near, far)
    load_vector(there, next_near, next_far)
    ham = real_product(own[1], mate[1], here) + real_product(own[0], mate[0], there)
    out[...] = near[...] - half_step * rotate(ham)


def add_up_kernel(rest, first, second, out):
    out[...] = rest[...] - half_step * rotate(first[...] + second[...])


def level_kernel(near, far, own, mate, beneath, above, store):
    load_vector(store, near, far)
    beneath[...] = complex_product(own[0:2], mate[0:2], store)
    above[...] = complex_product(own[2:4], mate[2:4], store)


def top_kernel(near, far, own, mate, beneath, store):
    load_vector(store, near, far)
    beneath[...] = complex_product(own[0:2], mate[0:2], store)


def pivot_kernel(near, far, less_near, less_far, own, mate, out, store):
    c = lax.axis_index("col")
    spread(store, near[...] - less_near[...], c)
    spread(store, far[...] - less_far[...], c ^ 2)
    out[...] = complex_product(own[4:6], mate[4:6], store)


def settle_kernel(tier_spacing, pivot, solved, *refs):
    *vectors, own, mate, out, lower, upper = refs
    s = lax.axis_index("slab")
    load_vector(lower, vectors[0], vectors[1])
    change = complex_product(own[6:8], mate[6:8], lower)
    if len(vectors) == 4:
        load_vector(upper, vectors[2], vectors[3])
        change = change + complex_product(own[8:10], mate[8:10], upper)
    active = s % (2 * tier_spacing) == tier_spacing
    out[...] = jnp.where(active, pivot[...] - change, solved[...])


def call(kernel, *operands, outs=1, scratch=(), flops=0):
    packed = jax.ShapeDtypeStruct((Q, LANES), wide)
    size = sum(v.size for v in operands) * 4 + outs * Q * LANES * 4
    return pl.pallas_call(
        kernel,
        out_shape=packed if outs == 1 else (packed,) * outs,
        in_specs=[pl.BlockSpec(memory_space=pltpu.VMEM)] * len(operands),
        out_specs=pl.BlockSpec(memory_space=pltpu.VMEM)
        if outs == 1
        else (pl.BlockSpec(memory_space=pltpu.VMEM),) * outs,
        scratch_shapes=list(scratch),
        cost_estimate=pl.CostEstimate(flops=flops, bytes_accessed=size, transcendentals=0),
        compiler_params=pltpu.CompilerParams(vmem_limit_bytes=24 * 2**20),
    )(*operands)


def per_device(slabs, cols, waves, energy, tunnel, pivots, below, above, back_lower, back_upper):
    everyone = range(cols)
    rows = waves.shape[1]
    width = energy.shape[2]
    store = pltpu.VMEM((width, LANES), short)
    one = 2 * 2 * Q * width * 2 * LANES * 2

    def send(values, slab_pairs, flip=0):
        route = [
            (a * cols + c, b * cols + (c ^ flip)) for a, b in slab_pairs for c in everyone
        ]
        return lax.ppermute(values, ("slab", "col"), route)

    same = [(s, s) for s in range(slabs)]

    def shift(distance, chosen):
        return [(s, s + distance) for s in chosen if 0 <= s + distance < slabs]

    states = waves[0]
    mate_states = send(states, same, 1)
    hops = jnp.concatenate([tunnel, energy], axis=0)
    mate_hops = send(hops, same, 1)
    blocks = jnp.concatenate(
        [below[0], above[0], pivots[0], back_lower[0], back_upper[0]], axis=0
    )
    mate_blocks = send(blocks, same, 1)

    psi = call(pack_kernel, states, mate_states)
    every = range(slabs)
    down, up = shift(-1, every), shift(1, every)
    psi_far = send(psi, same, 2)
    next_near = send(psi, down)
    next_far = send(psi, down, 2)
    up_near, up_far = call(
        up_kernel,
        psi,
        hops,
        mate_hops,
        outs=2,
        scratch=[pltpu.VMEM((64, width), wide)],
        flops=one // 2,
    )
    prev_near = send(up_near, up)
    prev_far = send(up_far, up, 2)
    rest = call(
        ham_kernel,
        psi,
        psi_far,
        next_near,
        next_far,
        hops,
        mate_hops,
        scratch=[store, store],
        flops=one,
    )
    near = call(add_up_kernel, rest, prev_near, prev_far)

    levels = slabs.bit_length() - 1
    for level in range(levels):
        spacing = 2**level
        active = [s for s in every if s % (2 * spacing) == spacing]
        far = send(near, same, 2)
        if level < levels - 1:
            beneath, over = call(
                level_kernel, near, far, blocks, mate_blocks, outs=2, scratch=[store], flops=2 * one
            )
            less = send(beneath, shift(-spacing, active))
            more = send(over, shift(spacing, active))
            near = near - less - more
        else:
            beneath = call(
                top_kernel, near, far, blocks, mate_blocks, scratch=[store], flops=one
            )
            less_near = send(beneath, shift(-spacing, active))
            less_far = send(beneath, shift(-spacing, active), 2)
            pivot = call(
                pivot_kernel,
                near,
                far,
                less_near,
                less_far,
                blocks,
                mate_blocks,
                scratch=[store],
                flops=one,
            )

    solved = pivot
    for level in reversed(range(levels)):
        spacing = 2**level
        active = [s for s in every if s % (2 * spacing) == spacing]
        from_lower = [(s - spacing, s) for s in active]
        from_upper = [(s + spacing, s) for s in active if s + spacing < slabs]
        vectors = [send(solved, from_lower), send(solved, from_lower, 2)]
        if from_upper:
            vectors += [send(solved, from_upper), send(solved, from_upper, 2)]
        solved = call(
            functools.partial(settle_kernel, spacing),
            pivot,
            solved,
            *vectors,
            blocks,
            mate_blocks,
            scratch=[store, store],
            flops=len(vectors) // 2 * one,
        )
    out = call(regroup_kernel, solved, send(solved, same, 1))
    return out[None]


def solution(mesh):
    slabs, cols = mesh.shape["slab"], mesh.shape["col"]
    vector = P("slab", "col", None)
    block = P("slab", None, "col", None)
    return jax.shard_map(
        functools.partial(per_device, slabs, cols),
        mesh=mesh,
        in_specs=(vector,) * 3 + (block,) * 5,
        out_specs=vector,
        check_vma=False,
    )
```

```python
import functools

import jax
import jax.numpy as jnp
from jax import lax
from jax.experimental import pallas as pl
from jax.experimental.pallas import tpu as pltpu
from jax.sharding import PartitionSpec as P


half_step = 0.5
wide = jnp.float32
short = jnp.bfloat16
Q = 128
LANES = 128


def lanes(values):
    return lax.broadcasted_iota(jnp.int32, values.shape, 1)


def swap_halves(values):
    return pltpu.roll(values, 64, 1)


def join(left, right):
    return jnp.where(lanes(left) < 64, left, right)


def rotate(values):
    even = lanes(values) % 2 == 0
    return jnp.where(even, -pltpu.roll(values, LANES - 1, 1), pltpu.roll(values, 1, 1))


def split(values):
    high = values.astype(short)
    return high, (values - high.astype(wide)).astype(short)


def quarter(number):
    return pl.ds(pl.multiple_of(number * Q, Q), Q)


def spread(store, packed, first):
    high = packed.astype(short).astype(wide)
    low = packed - high
    store[quarter(first), :] = join(high, swap_halves(low)).astype(short)
    store[quarter(first ^ 1), :] = join(swap_halves(high), low).astype(short)


def load_vector(store, near, far):
    c = lax.axis_index("col")
    spread(store, near, c)
    spread(store, far, c ^ 2)


def keep(wanted, values):
    return jnp.where(wanted, values[...], 0.0)


def rows_product(block, store):
    high, low = split(block)
    vector = store[...]
    return jnp.dot(high, vector, preferred_element_type=wide) + jnp.dot(
        low, vector, preferred_element_type=wide
    )


def fold(values):
    return values + swap_halves(values)


def real_product(own, mate, store):
    return join(fold(rows_product(own, store)), fold(rows_product(mate, store)))


def complex_half(block, store):
    both = rows_product(block.reshape(2 * Q, block.shape[-1]), store)
    return fold(both[:Q] + rotate(both[Q:]))


def complex_product(own, mate, store):
    return join(complex_half(own, store), complex_half(mate, store))


def regroup_kernel(mine, other, out):
    c = lax.axis_index("col")
    rows = join(mine[...], other[...])
    out[...] = jnp.where(c % 2 == 0, rows, swap_halves(rows))


def pack_kernel(mine, other, out):
    c = lax.axis_index("col")
    near, far = mine[...], other[...]
    out[...] = jnp.where(
        c % 2 == 0, join(near, swap_halves(far)), join(swap_halves(near), far)
    )


def up_kernel(packed, own, mate, near, far, store):
    c = lax.axis_index("col")
    turned = packed[...].T
    total = None
    for rows, block in ((turned[:64], own[0]), (turned[64:], mate[0])):
        high, low = split(rows)
        pair = jnp.concatenate([high, low], axis=0)
        block_high, block_low = split(block)
        part = jnp.dot(pair, block_high, preferred_element_type=wide) + jnp.dot(
            pair, block_low, preferred_element_type=wide
        )
        part = part[:64] + part[64:]
        total = part if total is None else total + part
    store[...] = total
    for out, first in ((near, c), (far, c ^ 2)):
        pair = jnp.concatenate(
            [store[:, quarter(first)], store[:, quarter(first ^ 1)]], axis=0
        )
        out[...] = pair.T


def ham_kernel(slabs, near, far, next_near, next_far, own_e, mate_e, own_t, mate_t, out, here, there):
    linked = lax.axis_index("slab") < slabs - 1
    load_vector(here, near[...], far[...])
    load_vector(there, keep(linked, next_near), keep(linked, next_far))
    ham = real_product(own_e[0], mate_e[0], here) + real_product(own_t[0], mate_t[0], there)
    out[...] = near[...] - half_step * rotate(ham)


def add_up_kernel(rest, first, second, out):
    linked = lax.axis_index("slab") > 0
    out[...] = rest[...] - half_step * rotate(keep(linked, first) + keep(linked, second))


def level_kernel(near, far, own_b, mate_b, own_a, mate_a, beneath, above, store):
    load_vector(store, near[...], far[...])
    beneath[...] = complex_product(own_b[0], mate_b[0], store)
    above[...] = complex_product(own_a[0], mate_a[0], store)


def top_kernel(near, far, own_b, mate_b, beneath, store):
    load_vector(store, near[...], far[...])
    beneath[...] = complex_product(own_b[0], mate_b[0], store)


def reduce_kernel(tier_spacing, near, less, more, out):
    s = lax.axis_index("slab")
    kept = s % (2 * tier_spacing) == 0
    out[...] = near[...] - keep(kept, less) - keep(kept & (s > 0), more)


def pivot_kernel(tier_spacing, near, far, less_near, less_far, own, mate, out, store):
    root = lax.axis_index("slab") % (2 * tier_spacing) == 0
    load_vector(store, near[...] - keep(root, less_near), far[...] - keep(root, less_far))
    out[...] = complex_product(own[0], mate[0], store)


def settle_kernel(slabs, tier_spacing, pivot, solved, lower_near, lower_far, own_l, mate_l, *refs):
    *others, out, lower, upper = refs
    s = lax.axis_index("slab")
    load_vector(lower, lower_near[...], lower_far[...])
    change = complex_product(own_l[0], mate_l[0], lower)
    if others:
        upper_near, upper_far, own_u, mate_u = others
        linked = s + tier_spacing < slabs
        load_vector(upper, keep(linked, upper_near), keep(linked, upper_far))
        change = change + complex_product(own_u[0], mate_u[0], upper)
    active = s % (2 * tier_spacing) == tier_spacing
    out[...] = jnp.where(active, pivot[...] - change, solved[...])


def call(kernel, *operands, outs=1, scratch=(), flops=0):
    packed = jax.ShapeDtypeStruct((Q, LANES), wide)
    size = sum(v.size for v in operands) * 4 + outs * Q * LANES * 4
    return pl.pallas_call(
        kernel,
        out_shape=packed if outs == 1 else (packed,) * outs,
        in_specs=[pl.BlockSpec(memory_space=pltpu.VMEM)] * len(operands),
        out_specs=pl.BlockSpec(memory_space=pltpu.VMEM)
        if outs == 1
        else (pl.BlockSpec(memory_space=pltpu.VMEM),) * outs,
        scratch_shapes=list(scratch),
        cost_estimate=pl.CostEstimate(flops=flops, bytes_accessed=size, transcendentals=0),
        compiler_params=pltpu.CompilerParams(vmem_limit_bytes=24 * 2**20),
    )(*operands)


def completed(route, slabs, cols):
    target = dict(route)
    taken = set(target.values())
    for a, b in route:
        if b not in target and a not in taken:
            target[b] = a
            taken.add(a)
    for a in [a for a in range(slabs * cols) if a not in target and a not in taken]:
        target[a] = a ^ 1
        taken.add(a ^ 1)
    for a in range(slabs * cols):
        if a not in target:
            free = [b for b in range(slabs * cols) if b not in taken and b % cols == a % cols]
            target[a] = free[0]
            taken.add(free[0])
    return sorted(target.items())


def per_device(slabs, cols, waves, energy, tunnel, pivots, below, above, back_lower, back_upper):
    everyone = range(cols)
    width = energy.shape[2]
    store = pltpu.VMEM((width, LANES), short)
    one = 2 * 2 * Q * width * 2 * LANES * 2

    def send(values, slab_pairs, flip=0):
        route = [
            (a * cols + c, b * cols + (c ^ flip)) for a, b in slab_pairs for c in everyone
        ]
        return lax.ppermute(values, ("slab", "col"), completed(route, slabs, cols))

    same = [(s, s) for s in range(slabs)]

    def shift(distance, chosen):
        return [(s, s + distance) for s in chosen if 0 <= s + distance < slabs]

    def swap(values):
        return send(values, same, 1)

    states = waves[0]
    psi = call(pack_kernel, states, swap(states))
    t_pair = tunnel, swap(tunnel)
    e_pair = energy, swap(energy)
    b_pair = below, swap(below)
    a_pair = above, swap(above)
    r_pair = pivots, swap(pivots)
    l_pair = back_lower, swap(back_lower)
    u_pair = back_upper, swap(back_upper)

    every = range(slabs)
    down, up = shift(-1, every), shift(1, every)
    psi_far = send(psi, same, 2)
    next_near = send(psi, down)
    next_far = send(psi, down, 2)
    up_near, up_far = call(
        up_kernel, psi, *t_pair, outs=2, scratch=[pltpu.VMEM((64, width), wide)], flops=one // 2
    )
    prev_near = send(up_near, up)
    prev_far = send(up_far, up, 2)
    rest = call(
        functools.partial(ham_kernel, slabs),
        psi,
        psi_far,
        next_near,
        next_far,
        *e_pair,
        *t_pair,
        scratch=[store, store],
        flops=one,
    )
    near = call(add_up_kernel, rest, prev_near, prev_far)

    levels = slabs.bit_length() - 1
    for level in range(levels):
        spacing = 2**level
        active = [s for s in every if s % (2 * spacing) == spacing]
        far = send(near, same, 2)
        if level < levels - 1:
            beneath, over = call(
                level_kernel, near, far, *b_pair, *a_pair, outs=2, scratch=[store], flops=2 * one
            )
            less = send(beneath, shift(-spacing, active))
            more = send(over, shift(spacing, active))
            near = call(functools.partial(reduce_kernel, spacing), near, less, more)
        else:
            beneath = call(top_kernel, near, far, *b_pair, scratch=[store], flops=one)
            less_near = send(beneath, shift(-spacing, active))
            less_far = send(beneath, shift(-spacing, active), 2)
            pivot = call(
                functools.partial(pivot_kernel, spacing),
                near,
                far,
                less_near,
                less_far,
                *r_pair,
                scratch=[store],
                flops=one,
            )

    solved = pivot
    for level in reversed(range(levels)):
        spacing = 2**level
        active = [s for s in every if s % (2 * spacing) == spacing]
        from_lower = [(s - spacing, s) for s in active]
        from_upper = [(s + spacing, s) for s in active if s + spacing < slabs]
        rest = [send(solved, from_lower), send(solved, from_lower, 2), *l_pair]
        if from_upper:
            rest += [send(solved, from_upper), send(solved, from_upper, 2), *u_pair]
        solved = call(
            functools.partial(settle_kernel, slabs, spacing),
            pivot,
            solved,
            *rest,
            scratch=[store, store],
            flops=len(rest) // 4 * one,
        )
    out = call(regroup_kernel, solved, swap(solved))
    return out[None]


def solution(mesh):
    slabs, cols = mesh.shape["slab"], mesh.shape["col"]
    vector = P("slab", "col", None)
    block = P("slab", None, "col", None)
    return jax.shard_map(
        functools.partial(per_device, slabs, cols),
        mesh=mesh,
        in_specs=(vector,) * 3 + (block,) * 5,
        out_specs=vector,
        check_vma=False,
    )
```

```python
import functools

import jax
import jax.numpy as jnp
from jax import lax
from jax.experimental import pallas as pl
from jax.experimental.pallas import tpu as pltpu
from jax.sharding import PartitionSpec as P


half_step = 0.5
wide = jnp.float32
short = jnp.bfloat16
Q = 128
LANES = 128
cost = pl.CostEstimate(flops=10**10, bytes_accessed=1, transcendentals=0)


def lanes(values):
    return lax.broadcasted_iota(jnp.int32, values.shape, 1)


def swap_halves(values):
    return pltpu.roll(values, 64, 1)


def join(left, right):
    return jnp.where(lanes(left) < 64, left, right)


def rotate(values):
    even = lanes(values) % 2 == 0
    return jnp.where(even, -pltpu.roll(values, LANES - 1, 1), pltpu.roll(values, 1, 1))


def split(values):
    high = values.astype(short)
    return high, (values - high.astype(wide)).astype(short)


def quarter(number):
    return pl.ds(pl.multiple_of(number * Q, Q), Q)


def spread(store, packed, first):
    high = packed.astype(short).astype(wide)
    low = packed - high
    store[quarter(first), :] = join(high, swap_halves(low)).astype(short)
    store[quarter(first ^ 1), :] = join(swap_halves(high), low).astype(short)


def load_vector(store, near, far):
    c = lax.axis_index("col")
    spread(store, near, c)
    spread(store, far, c ^ 2)


def keep(wanted, values):
    return jnp.where(wanted, values[...], 0.0)


def rows_product(block, store):
    high, low = split(block)
    vector = store[...]
    return jnp.dot(high, vector, preferred_element_type=wide) + jnp.dot(
        low, vector, preferred_element_type=wide
    )


def fold(values):
    return values + swap_halves(values)


def real_product(own, mate, store):
    return join(fold(rows_product(own, store)), fold(rows_product(mate, store)))


def complex_half(block, store):
    both = rows_product(block.reshape(2 * Q, block.shape[-1]), store)
    return fold(both[:Q] + rotate(both[Q:]))


def complex_product(own, mate, store):
    return join(complex_half(own, store), complex_half(mate, store))


def regroup_kernel(mine, other, out):
    c = lax.axis_index("col")
    rows = join(mine[...], other[...])
    out[...] = jnp.where(c % 2 == 0, rows, swap_halves(rows))


def side_kernel(side):
    c = lax.axis_index("col")
    side[...] = jnp.zeros_like(side) + (1 - c % 2)


def open_kernel(mine, other, side, own, mate, psi, near, far, crossing, store):
    c = lax.axis_index("col")
    packed = jnp.where(
        side[0:1] == 1,
        join(mine[0], swap_halves(other[0])),
        join(swap_halves(mine[0]), other[0]),
    )
    psi[...] = packed
    turned = packed.T
    total = None
    for rows, block in ((turned[:64], own[0]), (turned[64:], mate[0])):
        high, low = split(rows)
        pair = jnp.concatenate([high, low], axis=0)
        block_high, block_low = split(block)
        part = jnp.dot(pair, block_high, preferred_element_type=wide) + jnp.dot(
            pair, block_low, preferred_element_type=wide
        )
        part = part[:64] + part[64:]
        total = part if total is None else total + part
    store[...] = total
    for out, first in ((near, c), (far, c ^ 2)):
        pair = jnp.concatenate(
            [store[:, quarter(first)], store[:, quarter(first ^ 1)]], axis=0
        )
        out[...] = half_step * rotate(pair.T)
    crossing[...] = jnp.where(lax.axis_index("slab") % 2 == 1, packed, far[...])


def ham_kernel(slabs, near, crossed, crossed_next, next_near, own_e, mate_e, own_t, mate_t, out, here, there):
    s = lax.axis_index("slab")
    odd = s % 2 == 1
    linked = odd & (s < slabs - 1)
    load_vector(here, near[...], jnp.where(odd, crossed[...], crossed_next[...]))
    load_vector(there, keep(linked, next_near), keep(linked, crossed_next))
    ham = real_product(own_e[0], mate_e[0], here) + real_product(own_t[0], mate_t[0], there)
    out[...] = near[...] - half_step * rotate(ham)


def even_kernel(rest, next_near, next_far, own, mate, out, store):
    load_vector(store, next_near[...], next_far[...])
    out[...] = rest[...] - half_step * rotate(real_product(own[0], mate[0], store))


def first_kernel(near, far, tail_near, tail_far, own_b, mate_b, own_a, mate_a, beneath, above, store):
    load_vector(store, near[...], far[...])
    above[...] = complex_product(own_a[0], mate_a[0], store) + tail_near[...] + tail_far[...]
    beneath[...] = complex_product(own_b[0], mate_b[0], store)


def level_kernel(near, far, own_b, mate_b, own_a, mate_a, beneath, above, store):
    load_vector(store, near[...], far[...])
    above[...] = complex_product(own_a[0], mate_a[0], store)
    beneath[...] = complex_product(own_b[0], mate_b[0], store)


def one_kernel(near, far, own, mate, out, store):
    load_vector(store, near[...], far[...])
    out[...] = complex_product(own[0], mate[0], store)


def settle_kernel(tier_spacing, late, pivot, near, far, own_l, mate_l, own_u, mate_u, out, store):
    first = lax.axis_index("slab") % (4 * tier_spacing) == tier_spacing
    from_lower = jnp.logical_xor(first, late)
    load_vector(store, near[...], far[...])

    @pl.when(from_lower)
    def _():
        out[...] = pivot[...] - complex_product(own_l[0], mate_l[0], store)

    @pl.when(jnp.logical_not(from_lower))
    def _():
        out[...] = pivot[...] - complex_product(own_u[0], mate_u[0], store)


def call(kernel, *operands, outs=1, scratch=(), shape=jax.ShapeDtypeStruct((Q, LANES), wide)):
    vmem = pl.BlockSpec(memory_space=pltpu.VMEM)
    return pl.pallas_call(
        kernel,
        out_shape=shape if outs == 1 else (shape,) * outs,
        in_specs=[vmem] * len(operands),
        out_specs=vmem if outs == 1 else (vmem,) * outs,
        scratch_shapes=list(scratch),
        cost_estimate=cost,
        compiler_params=pltpu.CompilerParams(vmem_limit_bytes=16 * 2**20),
    )(*operands)


def completed(route, slabs, cols):
    target = dict(route)
    taken = set(target.values())
    for a, b in route:
        if b not in target and a not in taken:
            target[b] = a
            taken.add(a)
    for a in [a for a in range(slabs * cols) if a not in target and a not in taken]:
        target[a] = a ^ 1
        taken.add(a ^ 1)
    for a in range(slabs * cols):
        if a not in target:
            free = [b for b in range(slabs * cols) if b not in taken and b % cols == a % cols]
            target[a] = free[0]
            taken.add(free[0])
    return sorted(target.items())


def per_device(slabs, cols, waves, energy, tunnel, pivots, below, above, back_lower, back_upper):
    everyone = range(cols)
    width = energy.shape[2]
    store = pltpu.VMEM((width, LANES), short)
    levels = slabs.bit_length() - 1
    every = range(slabs)
    s = lax.axis_index("slab")
    odd = s % 2 == 1

    def send(values, slab_pairs, flip=0):
        route = [
            (a * cols + c, b * cols + (c ^ flip)) for a, b in slab_pairs for c in everyone
        ]
        return lax.ppermute(values, ("slab", "col"), completed(route, slabs, cols))

    def both(values, slab_pairs):
        return send(values, slab_pairs), send(values, slab_pairs, 2)

    def swap(values):
        return send(values, [(a, a) for a in every], 1)

    def exchange(values):
        return send(values, [(a, a) for a in every], 2)

    in_plane = [(a, a ^ 1) for a in every]
    between = [(a, a + 1) for a in every if a % 2 == 1 and a + 1 < slabs]

    side = call(side_kernel, shape=jax.ShapeDtypeStruct((8, LANES), jnp.int32))
    t_pair = tunnel, swap(tunnel)
    e_pair = energy, swap(energy)
    b_pair = below, swap(below)
    a_pair = above, swap(above)
    r_pair = pivots, swap(pivots)
    l_pair = back_lower, swap(back_lower)
    u_pair = back_upper, swap(back_upper)
    psi, up_near, up_far, crossing = call(
        open_kernel,
        waves,
        swap(waves),
        side,
        *t_pair,
        outs=4,
        scratch=[pltpu.VMEM((64, width), wide)],
    )
    next_odd = send(psi, between)
    crossed = exchange(crossing)
    crossed_next = exchange(jnp.where(odd, next_odd, psi))
    stepped = send(jnp.where(odd, psi, up_near + crossed), in_plane)
    up_odd = exchange(up_far)
    rest = call(
        functools.partial(ham_kernel, slabs),
        psi,
        crossed,
        crossed_next,
        next_odd,
        *e_pair,
        *t_pair,
        scratch=[store, store],
    )
    near = rest - stepped
    far = exchange(near)
    stepped_far = exchange(stepped)

    base = base_far = last_near = last_far = pivot = None
    for level in range(levels):
        spacing = 2**level
        active = [a for a in every if a % (2 * spacing) == spacing]
        is_active = s % (2 * spacing) == spacing
        if level == 0:
            last_near, last_far = near, far
            beneath, over = call(
                first_kernel,
                near,
                far,
                up_near,
                up_odd,
                *b_pair,
                *a_pair,
                outs=2,
                scratch=[store],
            )
        else:
            last_near = jnp.where(is_active, near, last_near)
            last_far = jnp.where(is_active, far, last_far)
            if level < levels - 1:
                beneath, over = call(
                    level_kernel, near, far, *b_pair, *a_pair, outs=2, scratch=[store]
                )
            else:
                beneath = call(one_kernel, near, far, *b_pair, scratch=[store])
        if level == levels - 1:
            less_near, less_far = both(beneath, [(spacing, 0)])
            base_far = exchange(base)
            near = jnp.where(s == 0, base - less_near, last_near)
            far = jnp.where(s == 0, base_far - less_far, last_far)
            pivot = call(one_kernel, near, far, *r_pair, scratch=[store])
            continue
        urgent = [a for a in every if a % (4 * spacing) == 2 * spacing]
        more_near, more_far = both(over, [(a - spacing, a) for a in urgent])
        less_near, less_far = both(beneath, [(a + spacing, a) for a in urgent])
        if level == 0:
            base = call(
                even_kernel, rest, stepped, stepped_far, *t_pair, scratch=[store]
            )
        base_far = exchange(base)
        near = base - more_near - less_near
        far = base_far - more_far - less_far
        patient = [a for a in every if a % (4 * spacing) == 0]
        is_patient = s % (4 * spacing) == 0
        later_less = send(beneath, [(a + spacing, a) for a in patient])
        later_more = [(a - spacing, a) for a in patient if a >= spacing]
        base = base - jnp.where(is_patient, later_less, 0.0)
        if later_more:
            arrived = send(over, later_more)
            base = base - jnp.where(is_patient & (s > 0), arrived, 0.0)

    solved = rest = pivot
    for level in reversed(range(levels)):
        spacing = 2**level
        is_active = s % (2 * spacing) == spacing
        late = [a for a in every if a % (4 * spacing) == 2 * spacing] if level < levels - 1 else [0]
        vectors = []
        for way in (1, -1):
            pairs = [(a, a + way * spacing) for a in late if 0 <= a + way * spacing < slabs]
            if pairs:
                vectors.append((way, both(solved, pairs)))
        if level == levels - 1:
            near, far = vectors[0][1]
        else:
            from_above = s % (4 * spacing) == spacing
            near = jnp.where(from_above, vectors[1][1][0], vectors[0][1][0])
            far = jnp.where(from_above, vectors[1][1][1], vectors[0][1][1])
        settled = call(
            functools.partial(settle_kernel, spacing, level < levels - 1),
            rest,
            near,
            far,
            *l_pair,
            *u_pair,
            scratch=[store],
        )
        before = solved
        solved = jnp.where(is_active, settled, solved)
        if level > 0:
            below_spacing = spacing // 2
            sources = [a for a in every if a % (4 * below_spacing) == 0]
            from_lower = [(a, a + below_spacing) for a in sources]
            from_upper = [(a, a - below_spacing) for a in sources if a > 0]
            low = both(before, from_lower)
            near, far = low
            linked = True
            if from_upper:
                up = both(before, from_upper)
                first = s % (4 * below_spacing) == below_spacing
                near = jnp.where(first, low[0], up[0])
                far = jnp.where(first, low[1], up[1])
            linked = s + below_spacing < slabs
            rest = call(
                functools.partial(settle_kernel, below_spacing, False),
                pivot,
                jnp.where(linked, near, 0.0),
                jnp.where(linked, far, 0.0),
                *l_pair,
                *u_pair,
                scratch=[store],
            )
    out = call(regroup_kernel, solved, swap(solved))
    return out[None]


def solution(mesh):
    slabs, cols = mesh.shape["slab"], mesh.shape["col"]
    vector = P("slab", "col", None)
    block = P("slab", None, "col", None)
    return jax.shard_map(
        functools.partial(per_device, slabs, cols),
        mesh=mesh,
        in_specs=(vector,) * 3 + (block,) * 5,
        out_specs=vector,
        check_vma=False,
    )
```

```python
import functools

import jax
import jax.numpy as jnp
from jax import lax
from jax.experimental import pallas as pl
from jax.experimental.pallas import tpu as pltpu
from jax.sharding import PartitionSpec as P


half_step = 0.5
wide = jnp.float32
short = jnp.bfloat16
Q = 128
LANES = 128


def lanes(values):
    return lax.broadcasted_iota(jnp.int32, values.shape, 1)


def swap_halves(values):
    return pltpu.roll(values, 64, 1)


def join(left, right):
    return jnp.where(lanes(left) < 64, left, right)


def rotate(values):
    even = lanes(values) % 2 == 0
    return jnp.where(even, -pltpu.roll(values, LANES - 1, 1), pltpu.roll(values, 1, 1))


def split(values):
    high = values.astype(short)
    return high, (values - high.astype(wide)).astype(short)


def quarter(number):
    return pl.ds(pl.multiple_of(number * Q, Q), Q)


def spread(store, packed, first):
    high = packed.astype(short).astype(wide)
    low = packed - high
    store[quarter(first), :] = join(high, swap_halves(low)).astype(short)
    store[quarter(first ^ 1), :] = join(swap_halves(high), low).astype(short)


def load_vector(store, near, far):
    c = lax.axis_index("col")
    spread(store, near, c)
    spread(store, far, c ^ 2)


def keep(wanted, values):
    return jnp.where(wanted, values[...], 0.0)


def rows_product(block, store):
    high, low = split(block)
    vector = store[...]
    return jnp.dot(high, vector, preferred_element_type=wide) + jnp.dot(
        low, vector, preferred_element_type=wide
    )


def fold(values):
    return values + swap_halves(values)


def real_product(own, mate, store):
    return join(fold(rows_product(own, store)), fold(rows_product(mate, store)))


def complex_half(block, store):
    both = rows_product(block.reshape(2 * Q, block.shape[-1]), store)
    return fold(both[:Q] + rotate(both[Q:]))


def complex_product(own, mate, store):
    return join(complex_half(own, store), complex_half(mate, store))


def this_core(left, right):
    first = lax.axis_index("col") % 2 == 0
    return jnp.where(first, join(left, swap_halves(right)), join(swap_halves(left), right))


def side_kernel(side):
    side[...] = jnp.zeros_like(side) + lax.axis_index("col")


def regroup_kernel(mine, other, out):
    rows = join(mine[...], other[...])
    out[...] = jnp.where(lax.axis_index("col") % 2 == 0, rows, swap_halves(rows))


def stack_kernel(*refs):
    *sources, _, out = refs
    place = 0
    for source in sources:
        depth = source.shape[0]
        out[place : place + depth] = source[...]
        place += depth


def reduce_kernel(spacing, count, base, *refs):
    out = refs[-1]
    less, *more = refs[:count]
    s = lax.axis_index("slab")
    kept = s % (4 * spacing) == 0
    values = base[...] - keep(kept, less)
    for late in more:
        values = values - keep(kept & (s > 0), late)
    out[...] = values


def open_kernel(mine, other, side, own, mate, psi, near, far, store):
    c = lax.axis_index("col")
    packed = this_core(mine[0], other[0])
    psi[...] = packed
    turned = packed.T
    total = None
    for rows, block in ((turned[:64], own[0]), (turned[64:], mate[0])):
        high, low = split(rows)
        pair = jnp.concatenate([high, low], axis=0)
        block_high, block_low = split(block)
        part = jnp.dot(pair, block_high, preferred_element_type=wide) + jnp.dot(
            pair, block_low, preferred_element_type=wide
        )
        part = part[:64] + part[64:]
        total = part if total is None else total + part
    store[...] = total
    for out, first in ((far, c ^ 2), (near, c)):
        pair = jnp.concatenate(
            [store[:, quarter(first)], store[:, quarter(first ^ 1)]], axis=0
        )
        out[...] = half_step * rotate(pair.T)


def ham_kernel(slabs, near, far, next_near, next_far, own_e, mate_e, own_t, mate_t, *refs):
    out, here, there = refs[-3:]
    linked = lax.axis_index("slab") < slabs - 1
    load_vector(here, near[...], far[...])
    load_vector(there, keep(linked, next_near), keep(linked, next_far))
    ham = real_product(own_e[0], mate_e[0], here) + real_product(own_t[0], mate_t[0], there)
    out[...] = near[...] - half_step * rotate(ham)


def level_kernel(spacing, near, far, own, mate, *refs):
    beneath, above, store = refs[-3:]

    @pl.when(lax.axis_index("slab") % (2 * spacing) == spacing)
    def _():
        load_vector(store, near[...], far[...])
        above[...] = complex_product(own[2:4], mate[2:4], store)
        beneath[...] = complex_product(own[0:2], mate[0:2], store)


def top_kernel(spacing, near, far, own, mate, *refs):
    beneath, store = refs[-2:]

    @pl.when(lax.axis_index("slab") % (2 * spacing) == spacing)
    def _():
        load_vector(store, near[...], far[...])
        beneath[...] = complex_product(own[0:2], mate[0:2], store)


def pivot_kernel(spacing, near, far, own, mate, before, out, store):
    active = lax.axis_index("slab") % (2 * spacing) == spacing

    @pl.when(active)
    def _():
        load_vector(store, near[...], far[...])
        out[...] = complex_product(own[0:2], mate[0:2], store)

    @pl.when(jnp.logical_not(active))
    def _():
        out[...] = before[...]


def root_kernel(near, far, less_near, less_far, own, mate, before, out, store):
    root = lax.axis_index("slab") == 0

    @pl.when(root)
    def _():
        load_vector(store, near[...] - less_near[...], far[...] - less_far[...])
        out[...] = complex_product(own[0:2], mate[0:2], store)

    @pl.when(jnp.logical_not(root))
    def _():
        out[...] = before[...]


def settle_kernel(slabs, spacing, kind, part, other, *refs):
    *vectors, own, mate, out, store = refs
    s = lax.axis_index("slab")
    active = s % (2 * spacing) == spacing
    first = s % (4 * spacing) == spacing
    if kind == "late":
        below = jnp.logical_not(first)
        take = active
    elif kind == "early":
        below = first
        take = active & (s + spacing < slabs)
    else:
        below = s >= 0
        take = active

    def settle(vector, place):
        load_vector(store, vector[0][...], vector[1][...])
        blocks = slice(place, place + 2)
        out[...] = part[...] - complex_product(own[blocks], mate[blocks], store)

    @pl.when(take & below)
    def _():
        settle(vectors[:2], 2)

    if len(vectors) == 4:

        @pl.when(take & jnp.logical_not(below))
        def _():
            settle(vectors[2:], 4)

    @pl.when(jnp.logical_not(take))
    def _():
        out[...] = other[...]


def call(
    kernel,
    *operands,
    outs=1,
    scratch=(),
    unused=(),
    shape=jax.ShapeDtypeStruct((Q, LANES), wide),
    flops=10**9,
):
    vmem = pl.BlockSpec(memory_space=pltpu.VMEM)
    return pl.pallas_call(
        kernel,
        out_shape=shape if outs == 1 else (shape,) * outs,
        in_specs=[vmem] * len(operands) + [pl.BlockSpec(memory_space=pl.ANY)] * len(unused),
        out_specs=vmem if outs == 1 else (vmem,) * outs,
        scratch_shapes=list(scratch),
        cost_estimate=pl.CostEstimate(flops=flops, bytes_accessed=1, transcendentals=0),
        compiler_params=pltpu.CompilerParams(vmem_limit_bytes=16 * 2**20),
    )(*operands, *unused)


def completed(route, count, cols):
    target = dict(route)
    taken = set(target.values())
    for a in [a for a in range(count) if a not in target and a not in taken]:
        target[a] = a ^ 1
        taken.add(a ^ 1)
    for a in range(count):
        if a not in target:
            target[a] = next(b for b in range(count) if b not in taken and b % cols == a % cols)
            taken.add(target[a])
    if sorted(target.values()) != list(range(count)):
        raise ValueError("no permutation")
    return sorted(target.items())


def per_device(slabs, cols, waves, energy, tunnel, pivots, below, above, back_lower, back_upper):
    everyone = range(cols)
    width = energy.shape[2]
    store = pltpu.VMEM((width, LANES), short)
    levels = slabs.bit_length() - 1
    every = range(slabs)
    s = lax.axis_index("slab")

    def send(values, moves, flip=0):
        route = []
        for c in everyone:
            for a, b, *h in moves:
                route.append((a * cols + c, b * cols + (c ^ flip)))
                for h in h:
                    route.append((b * cols + (c ^ flip), h * cols + c))
                    route.append((h * cols + c, a * cols + c))
        return lax.ppermute(values, ("slab", "col"), completed(route, slabs * cols, cols))

    def both(values, near_moves, far_moves):
        return send(values, near_moves), send(values, far_moves, 2)

    def swap(values):
        return send(values, [(a, a) for a in every], 1)

    def exchange(values, chosen=every):
        return send(values, [(a, a) for a in chosen], 2)

    def kernel(body, *arguments):
        return functools.partial(body, *arguments)

    def stack(*arrays, after):
        depth = sum(v.shape[0] for v in arrays)
        shape = jax.ShapeDtypeStruct((depth, Q, width), wide)
        return call(stack_kernel, *arrays, unused=(after,), shape=shape, flops=1)

    mate_waves = swap(waves)
    t_pair = tunnel, swap(tunnel)
    e_pair = energy, swap(energy)
    side = call(side_kernel, shape=jax.ShapeDtypeStruct((8, LANES), jnp.int32))
    psi, up_near, up_far = call(
        open_kernel, waves, mate_waves, side, *t_pair, outs=3, scratch=[pltpu.VMEM((64, width), wide)]
    )
    up = up_near + exchange(up_far)
    prev = send(up, [(a, a + 1) for a in every[:-1]])
    down = [(a + 1, a) for a in every[:-1]]
    front = stack(below[0], above[0], after=up)
    front = front, swap(front)
    rest = call(
        kernel(ham_kernel, slabs),
        psi,
        exchange(psi),
        *both(psi, down, down),
        *e_pair,
        *t_pair,
        scratch=[store, store],
        unused=(up,),
    )
    base = near = rest - jnp.where(s > 0, prev, 0.0)
    back = stack(pivots[0], back_lower[0], back_upper[0], after=near)
    back = back, swap(back)
    base_far = far = exchange(near)

    pivot = base
    late = None
    for level in range(levels):
        d = 2**level
        active = [a for a in every if a % (2 * d) == d]
        if level == levels - 1:
            beneath = call(
                kernel(top_kernel, d), near, far, *front, scratch=[store], unused=late
            )
            less = both(beneath, [(d, 0, d + 1)], [(d, 0, d + 3)])
            base = call(kernel(reduce_kernel, d // 2, len(late)), base, *late, unused=(beneath,))
            base_far = exchange(base)
            pivot = call(kernel(pivot_kernel, d), near, far, *back, pivot, scratch=[store])
            pivot = call(root_kernel, base, base_far, *less, *back, pivot, scratch=[store])
            break
        beneath, over = call(
            kernel(level_kernel, d),
            near,
            far,
            *front,
            outs=2,
            scratch=[store],
            unused=(back[1],) if level == 0 else late,
        )
        urgent = [b for b in every if b % (4 * d) == 2 * d]
        patient = [b for b in every if b % (4 * d) == 0]
        if level == 0:
            more = send(over, [(b - 1, b, b - 2) for b in urgent])
            less = send(beneath, [(b + 1, b, b - 2) for b in urgent])
            late_less = send(beneath, [(b + 1, b, b + 3) for b in patient])
            late_more = send(over, [(b - 1, b, b + 1) for b in patient if b > 0])
        else:
            more = both(
                over, [(b - d, b, b - 1) for b in urgent], [(b - d, b, b - 3) for b in urgent]
            )
            less = both(
                beneath, [(b + d, b, b + 1) for b in urgent], [(b + d, b, b + 3) for b in urgent]
            )
            late_less = send(beneath, [(b + d, b, b + d + 1) for b in patient])
            late_more = None
            if len(patient) > 1:
                late_more = send(over, [(b - d, b, b - d + 1) for b in patient if b > 0])
        pivot = call(kernel(pivot_kernel, d), near, far, *back, pivot, scratch=[store])
        if level == 0:
            near = base - more - less
            far = exchange(near)
        else:
            base = call(kernel(reduce_kernel, d // 2, len(late)), base, *late, unused=(beneath,))
            base_far = exchange(base)
            near = base - more[0] - less[0]
            far = base_far - more[1] - less[1]
        late = (late_less,) if late_more is None else (late_less, late_more)

    solved = rest = pivot
    for level in reversed(range(levels)):
        d = 2**level
        if level == levels - 1:
            vectors = both(solved, [(0, d, 1)], [(0, d, 3)])
            kind = "only"
        else:
            sources = [a for a in every if a % (4 * d) == 2 * d]
            kind = "late"
            if d > 1:
                up_near = send(solved, [(a, a + d, a + 3) for a in sources])
                down_near = send(solved, [(a, a - d, a - 1) for a in sources])
                up_far = send(solved, [(a, a + d, a + 1) for a in sources], 2)
                down_far = send(solved, [(a, a - d, a - 3) for a in sources], 2)
            else:
                up_near = send(solved, [(a, a + 1, a - 2) for a in sources])
                down_near = send(solved, [(a, a - 1, a + 1) for a in sources])
                down_far = send(solved, [(a, a - 1, a - 2) for a in sources], 2)
                up_far = exchange(up_near, [a + 1 for a in sources])
            vectors = up_near, up_far, down_near, down_far
        if level > 0:
            half = d // 2
            sources = [a for a in every if a % (4 * half) == 0]
            if half > 1:
                early = both(
                    solved,
                    [(a, a + half, a + 1) for a in sources],
                    [(a, a + half, a + 3) for a in sources],
                )
                if len(sources) > 1:
                    early += both(
                        solved,
                        [(a, a - half, a - 1) for a in sources if a > 0],
                        [(a, a - half, a - 3) for a in sources if a > 0],
                    )
            else:
                early = both(
                    solved,
                    [(a, a + 1, a + 3) for a in sources],
                    [(a, a + 1, a + 3) for a in sources],
                ) + both(
                    solved,
                    [(a, a - 1, a + 1) for a in sources if a > 0],
                    [(a, a - 1, a + 1) for a in sources if a > 0],
                )
        solved = call(
            kernel(settle_kernel, slabs, d, kind),
            rest,
            solved,
            *vectors,
            *back,
            scratch=[store],
        )
        if level > 0:
            rest = call(
                kernel(settle_kernel, slabs, half, "early"),
                pivot,
                pivot,
                *early,
                *back,
                scratch=[store],
            )
    out = call(regroup_kernel, solved, swap(solved))
    return out[None]


def solution(mesh):
    slabs, cols = mesh.shape["slab"], mesh.shape["col"]
    vector = P("slab", "col", None)
    block = P("slab", None, "col", None)
    return jax.shard_map(
        functools.partial(per_device, slabs, cols),
        mesh=mesh,
        in_specs=(vector,) * 3 + (block,) * 5,
        out_specs=vector,
        check_vma=False,
    )
```

```python
import functools

import jax
import jax.numpy as jnp
from jax import lax
from jax.experimental import pallas as pl
from jax.experimental.pallas import tpu as pltpu
from jax.sharding import PartitionSpec as P


half_step = 0.5
wide = jnp.float32
short = jnp.bfloat16
Q = 128
LANES = 128


def lanes(values):
    return lax.broadcasted_iota(jnp.int32, values.shape, 1)


def swap_halves(values):
    return pltpu.roll(values, 64, 1)


def join(left, right):
    return jnp.where(lanes(left) < 64, left, right)


def rotate(values):
    even = lanes(values) % 2 == 0
    return jnp.where(even, -pltpu.roll(values, LANES - 1, 1), pltpu.roll(values, 1, 1))


def split(values):
    high = values.astype(short)
    return high, (values - high.astype(wide)).astype(short)


def quarter(number):
    return pl.ds(pl.multiple_of(number * Q, Q), Q)


def spread(store, packed, first):
    high = packed.astype(short).astype(wide)
    low = packed - high
    store[quarter(first), :] = join(high, swap_halves(low)).astype(short)
    store[quarter(first ^ 1), :] = join(swap_halves(high), low).astype(short)


def load_vector(store, near, far):
    c = lax.axis_index("col")
    spread(store, near, c)
    spread(store, far, c ^ 2)


def keep(wanted, values):
    return jnp.where(wanted, values[...], 0.0)


def rows_product(block, store):
    high, low = split(block)
    vector = store[...]
    return jnp.dot(high, vector, preferred_element_type=wide) + jnp.dot(
        low, vector, preferred_element_type=wide
    )


def fold(values):
    return values + swap_halves(values)


def real_product(own, mate, store):
    return join(fold(rows_product(own, store)), fold(rows_product(mate, store)))


def complex_half(block, store):
    both = rows_product(block.reshape(2 * Q, block.shape[-1]), store)
    return fold(both[:Q] + rotate(both[Q:]))


def complex_product(own, mate, store):
    return join(complex_half(own, store), complex_half(mate, store))


def this_core(left, right):
    first = lax.axis_index("col") % 2 == 0
    return jnp.where(first, join(left, swap_halves(right)), join(swap_halves(left), right))


def side_kernel(side):
    side[...] = jnp.zeros_like(side) + lax.axis_index("col")


def regroup_kernel(mine, other, out):
    rows = join(mine[...], other[...])
    out[...] = jnp.where(lax.axis_index("col") % 2 == 0, rows, swap_halves(rows))


def stack_kernel(*refs):
    *sources, _, out = refs
    place = 0
    for source in sources:
        depth = source.shape[0]
        out[place : place + depth] = source[...]
        place += depth


def reduce_kernel(spacing, count, base, *refs):
    out = refs[-1]
    less, *more = refs[:count]
    s = lax.axis_index("slab")
    kept = s % (4 * spacing) == 0
    values = base[...] - keep(kept, less)
    for late in more:
        values = values - keep(kept & (s > 0), late)
    out[...] = values


def open_kernel(mine, other, side, own, mate, psi, near, far, store):
    c = lax.axis_index("col")
    packed = this_core(mine[0], other[0])
    psi[...] = packed
    turned = packed.T
    total = None
    for rows, block in ((turned[:64], own[0]), (turned[64:], mate[0])):
        high, low = split(rows)
        pair = jnp.concatenate([high, low], axis=0)
        block_high, block_low = split(block)
        part = jnp.dot(pair, block_high, preferred_element_type=wide) + jnp.dot(
            pair, block_low, preferred_element_type=wide
        )
        part = part[:64] + part[64:]
        total = part if total is None else total + part
    store[...] = total
    for out, first in ((far, c ^ 2), (near, c)):
        pair = jnp.concatenate(
            [store[:, quarter(first)], store[:, quarter(first ^ 1)]], axis=0
        )
        out[...] = half_step * rotate(pair.T)


def ham_kernel(slabs, near, far, next_near, next_far, own_e, mate_e, own_t, mate_t, *refs):
    out, here, there = refs[-3:]
    linked = lax.axis_index("slab") < slabs - 1
    load_vector(here, near[...], far[...])
    load_vector(there, keep(linked, next_near), keep(linked, next_far))
    ham = real_product(own_e[0], mate_e[0], here) + real_product(own_t[0], mate_t[0], there)
    out[...] = near[...] - half_step * rotate(ham)


def level_kernel(spacing, near, far, own, mate, *refs):
    beneath, above, store = refs[-3:]

    @pl.when(lax.axis_index("slab") % (2 * spacing) == spacing)
    def _():
        load_vector(store, near[...], far[...])
        above[...] = complex_product(own[2:4], mate[2:4], store)
        beneath[...] = complex_product(own[0:2], mate[0:2], store)


def top_kernel(spacing, near, far, own, mate, *refs):
    beneath, store = refs[-2:]

    @pl.when(lax.axis_index("slab") % (2 * spacing) == spacing)
    def _():
        load_vector(store, near[...], far[...])
        beneath[...] = complex_product(own[0:2], mate[0:2], store)


def pivot_kernel(spacing, near, far, own, mate, before, out, store):
    active = lax.axis_index("slab") % (2 * spacing) == spacing

    @pl.when(active)
    def _():
        load_vector(store, near[...], far[...])
        out[...] = complex_product(own[4:6], mate[4:6], store)

    @pl.when(jnp.logical_not(active))
    def _():
        out[...] = before[...]


def root_kernel(count, *refs):
    near, far = refs[:2]
    shares = refs[2 : 2 + 2 * count]
    own, mate, before, out, store = refs[2 + 2 * count :]
    root = lax.axis_index("slab") == 0

    @pl.when(root)
    def _():
        whole = [near[...], far[...]]
        for n, share in enumerate(shares):
            whole[n % 2] = whole[n % 2] - share[...]
        load_vector(store, *whole)
        out[...] = complex_product(own[4:6], mate[4:6], store)

    @pl.when(jnp.logical_not(root))
    def _():
        out[...] = before[...]


def settle_kernel(spacing, part, near, far, own, mate, out, store):
    active = lax.axis_index("slab") % (2 * spacing) == spacing

    @pl.when(active)
    def _():
        load_vector(store, near[...], far[...])
        out[...] = part[...] - complex_product(own[6:8], mate[6:8], store)

    @pl.when(jnp.logical_not(active))
    def _():
        out[...] = part[...]


def both_kernel(slabs, spacing, part, other, low_near, low_far, up_near, up_far, own, mate, *refs):
    out, lower, upper = refs
    s = lax.axis_index("slab")
    active = s % (2 * spacing) == spacing
    linked = s + spacing < slabs

    @pl.when(active)
    def _():
        load_vector(lower, low_near[...], low_far[...])
        out[...] = part[...] - complex_product(own[6:8], mate[6:8], lower)

    @pl.when(active & linked)
    def _():
        load_vector(upper, up_near[...], up_far[...])
        out[...] -= complex_product(own[8:10], mate[8:10], upper)

    @pl.when(jnp.logical_not(active))
    def _():
        out[...] = other[...]


def copy_kernel(values, *refs):
    refs[-1][...] = values[...]


def call(
    kernel,
    *operands,
    outs=1,
    scratch=(),
    unused=(),
    shape=jax.ShapeDtypeStruct((Q, LANES), wide),
    flops=10**9,
):
    vmem = pl.BlockSpec(memory_space=pltpu.VMEM)
    return pl.pallas_call(
        kernel,
        out_shape=shape if outs == 1 else (shape,) * outs,
        in_specs=[vmem] * len(operands) + [pl.BlockSpec(memory_space=pl.ANY)] * len(unused),
        out_specs=vmem if outs == 1 else (vmem,) * outs,
        scratch_shapes=list(scratch),
        cost_estimate=pl.CostEstimate(flops=flops, bytes_accessed=1, transcendentals=0),
        compiler_params=pltpu.CompilerParams(vmem_limit_bytes=16 * 2**20),
    )(*operands, *unused)


def completed(route, count, cols):
    target = dict(route)
    taken = set(target.values())
    for a in [a for a in range(count) if a not in target and a not in taken]:
        target[a] = a ^ 1
        taken.add(a ^ 1)
    for a in range(count):
        if a not in target:
            target[a] = next(b for b in range(count) if b not in taken and b % cols == a % cols)
            taken.add(target[a])
    if sorted(target.values()) != list(range(count)):
        raise ValueError("no permutation")
    return sorted(target.items())


def per_device(slabs, cols, waves, energy, tunnel, pivots, below, above, back_lower, back_upper):
    everyone = range(cols)
    width = energy.shape[2]
    store = pltpu.VMEM((width, LANES), short)
    levels = slabs.bit_length() - 1
    every = range(slabs)
    s = lax.axis_index("slab")

    def send(values, moves, flip=0, whole=True):
        route = []
        for c in everyone:
            for a, b, *h in moves:
                route.append((a * cols + c, b * cols + (c ^ flip)))
                for h in h:
                    route.append((b * cols + (c ^ flip), h * cols + c))
                    route.append((h * cols + c, a * cols + c))
        if whole:
            route = completed(route, slabs * cols, cols)
        return lax.ppermute(values, ("slab", "col"), route)

    def both(values, near_moves, far_moves):
        return send(values, near_moves), send(values, far_moves, 2)

    def swap(values):
        return send(values, [(a, a) for a in every], 1)

    def exchange(values, chosen=every):
        return send(values, [(a, a) for a in chosen], 2)

    def kernel(body, *arguments):
        return functools.partial(body, *arguments)

    def stack(*arrays, after):
        depth = sum(v.shape[0] for v in arrays)
        shape = jax.ShapeDtypeStruct((depth, Q, width), wide)
        return call(stack_kernel, *arrays, unused=(after,), shape=shape, flops=1)

    mate_waves = swap(waves)
    t_pair = tunnel, swap(tunnel)
    e_pair = energy, swap(energy)
    side = call(side_kernel, shape=jax.ShapeDtypeStruct((8, LANES), jnp.int32))
    psi, up_near, up_far = call(
        open_kernel, waves, mate_waves, side, *t_pair, outs=3, scratch=[pltpu.VMEM((64, width), wide)]
    )
    up = up_near + exchange(up_far)
    prev = send(up, [(a, a + 1) for a in every[:-1]], whole=False)
    down = [(a + 1, a) for a in every[:-1]]
    next_near = send(psi, down, whole=False)
    next_far = send(psi, down, 2, whole=False)
    rest = call(
        kernel(ham_kernel, slabs),
        psi,
        exchange(psi),
        next_near,
        next_far,
        *e_pair,
        *t_pair,
        scratch=[store, store],
        unused=(up,),
    )
    base = near = rest - prev
    front = stack(below[0], above[0], pivots[0], back_lower[0], back_upper[0], after=near)
    front = front, swap(front)
    back = front

    pivot = base
    far = exchange(near, [a for a in every if a % 2 == 1])
    for level in range(levels):
        d = 2**level
        if level == levels - 1:
            beneath = call(kernel(top_kernel, d), near, far, *front, scratch=[store])
            shares = both(beneath, [(d, 0, d + 1)], [(d, 0, d + 3)])
            if level > 1:
                shares = shares + late
            pivot = call(kernel(pivot_kernel, d), near, far, *back, pivot, scratch=[store])
            pivot = call(
                kernel(root_kernel, len(shares) // 2),
                base,
                base_far,
                *shares,
                *back,
                pivot,
                scratch=[store],
            )
            break
        urgent = [b for b in every if b % (4 * d) == 2 * d]
        patient = [b for b in every if b % (4 * d) == 0]
        beneath, over = call(
            kernel(level_kernel, d),
            near,
            far,
            *front,
            outs=2,
            scratch=[store],
            unused=() if level == 0 else (base,),
        )
        if level == 0:
            more = send(over, [(b - 1, b, b - 2) for b in urgent])
            less = send(beneath, [(b + 1, b, b - 2) for b in urgent])
            pivot = call(kernel(pivot_kernel, d), near, far, *back, pivot, scratch=[store])
            held = call(copy_kernel, beneath, unused=(pivot,))
            late = [send(held, [(b + 1, b, b + 3) for b in patient])]
            if len(patient) > 1:
                held = call(copy_kernel, over, unused=(pivot,))
                late.append(send(held, [(b - 1, b, b + 1) for b in patient if b > 0]))
            near = base - more - less
            far = exchange(near, urgent)
            base = call(kernel(reduce_kernel, d, len(late)), base, *late)
            base_far = exchange(base, patient)
            continue
        more = both(over, [(b - d, b, b - 1) for b in urgent], [(b - d, b, b - 3) for b in urgent])
        less = both(
            beneath, [(b + d, b, b + 1) for b in urgent], [(b + d, b, b + 3) for b in urgent]
        )
        pivot = call(kernel(pivot_kernel, d), near, far, *back, pivot, scratch=[store])
        if level > 1:
            is_late = s % (2 * d) == 0
            for n, share in enumerate(late):
                share = jnp.where(is_late & ((s > 0) | (n < 2)), share, 0.0)
                if n % 2 == 0:
                    base = base - share
                else:
                    base_far = base_far - share
        near = base - more[0] - less[0]
        far = base_far - more[1] - less[1]
        held = call(copy_kernel, beneath, unused=(base_far,))
        late = both(
            held, [(b + d, b, b + d + 1) for b in patient], [(b + d, b, b + d + 3) for b in patient]
        )
        if len(patient) > 1:
            held = call(copy_kernel, over, unused=(base_far,))
            late = late + both(
                held,
                [(b - d, b, b - d + 1) for b in patient if b > 0],
                [(b - d, b, b - d + 3) for b in patient if b > 0],
            )

    solved = pivot
    for level in reversed(range(levels)):
        d = 2**level
        sources = [a for a in every if a % (2 * d) == 0]
        upper = [a for a in sources if a > 0]
        if d > 1:
            if upper:
                up_near = send(solved, [(a, a - d, a - 1) for a in upper])
            low_near = send(solved, [(a, a + d, a + 3) for a in sources])
            if upper:
                up_far = send(solved, [(a, a - d, a + 3) for a in upper], 2)
            low_far = send(solved, [(a, a + d, a + 1) for a in sources], 2)
        else:
            low_near = send(solved, [(a, a ^ 1) for a in every])
            ways = [(a, a - 1) for a in upper] + [(a - 1, a) for a in upper]
            up_near = send(solved, ways)
            up_far = send(solved, ways, 2)
            low_far = exchange(low_near, [a + 1 for a in sources])
        if not upper:
            solved = call(
                kernel(settle_kernel, d),
                pivot,
                low_near,
                low_far,
                *back,
                scratch=[store],
            )
        else:
            solved = call(
                kernel(both_kernel, slabs, d),
                pivot,
                solved,
                low_near,
                low_far,
                up_near,
                up_far,
                *back,
                scratch=[store, store],
            )
    out = call(regroup_kernel, solved, swap(solved))
    return out[None]


def solution(mesh):
    slabs, cols = mesh.shape["slab"], mesh.shape["col"]
    vector = P("slab", "col", None)
    block = P("slab", None, "col", None)
    return jax.shard_map(
        functools.partial(per_device, slabs, cols),
        mesh=mesh,
        in_specs=(vector,) * 3 + (block,) * 5,
        out_specs=vector,
        check_vma=False,
    )
```

```python
import functools

import jax
import jax.numpy as jnp
from jax import lax
from jax.experimental import pallas as pl
from jax.experimental.pallas import tpu as pltpu
from jax.sharding import PartitionSpec as P


half_step = 0.5
wide = jnp.float32
short = jnp.bfloat16
Q = 128
LANES = 128


def lanes(values):
    return lax.broadcasted_iota(jnp.int32, values.shape, 1)


def swap_halves(values):
    return pltpu.roll(values, 64, 1)


def join(left, right):
    return jnp.where(lanes(left) < 64, left, right)


def rotate(values):
    even = lanes(values) % 2 == 0
    return jnp.where(even, -pltpu.roll(values, LANES - 1, 1), pltpu.roll(values, 1, 1))


def split(values):
    high = values.astype(short)
    return high, (values - high.astype(wide)).astype(short)


def quarter(number):
    return pl.ds(pl.multiple_of(number * Q, Q), Q)


def spread(store, packed, first):
    high = packed.astype(short).astype(wide)
    low = packed - high
    store[quarter(first), :] = join(high, swap_halves(low)).astype(short)
    store[quarter(first ^ 1), :] = join(swap_halves(high), low).astype(short)


def load_vector(store, near, far):
    c = lax.axis_index("col")
    spread(store, near, c)
    spread(store, far, c ^ 2)


def keep(wanted, values):
    return jnp.where(wanted, values[...], 0.0)


def rows_product(block, store):
    high, low = split(block)
    vector = store[...]
    return jnp.dot(high, vector, preferred_element_type=wide) + jnp.dot(
        low, vector, preferred_element_type=wide
    )


def fold(values):
    return values + swap_halves(values)


def real_product(own, mate, store):
    return join(fold(rows_product(own, store)), fold(rows_product(mate, store)))


def complex_half(block, store):
    both = rows_product(block.reshape(2 * Q, block.shape[-1]), store)
    return fold(both[:Q] + rotate(both[Q:]))


def complex_product(own, mate, store):
    return join(complex_half(own, store), complex_half(mate, store))


def this_core(left, right):
    first = lax.axis_index("col") % 2 == 0
    return jnp.where(first, join(left, swap_halves(right)), join(swap_halves(left), right))


def side_kernel(side):
    side[...] = jnp.zeros_like(side) + lax.axis_index("col")


def regroup_kernel(mine, other, out):
    rows = join(mine[...], other[...])
    out[...] = jnp.where(lax.axis_index("col") % 2 == 0, rows, swap_halves(rows))


def stack_kernel(*refs):
    *sources, _, out = refs
    place = 0
    for source in sources:
        depth = source.shape[0]
        out[place : place + depth] = source[...]
        place += depth


def reduce_kernel(spacing, count, base, *refs):
    out = refs[-1]
    less, *more = refs[:count]
    s = lax.axis_index("slab")
    kept = s % (4 * spacing) == 0
    values = base[...] - keep(kept, less)
    for late in more:
        values = values - keep(kept & (s > 0), late)
    out[...] = values


def open_kernel(mine, other, side, own, mate, psi, near, far, store):
    c = lax.axis_index("col")
    packed = this_core(mine[0], other[0])
    psi[...] = packed
    turned = packed.T
    total = None
    for rows, block in ((turned[:64], own[0]), (turned[64:], mate[0])):
        high, low = split(rows)
        pair = jnp.concatenate([high, low], axis=0)
        block_high, block_low = split(block)
        part = jnp.dot(pair, block_high, preferred_element_type=wide) + jnp.dot(
            pair, block_low, preferred_element_type=wide
        )
        part = part[:64] + part[64:]
        total = part if total is None else total + part
    store[...] = total
    for out, first in ((far, c ^ 2), (near, c)):
        pair = jnp.concatenate(
            [store[:, quarter(first)], store[:, quarter(first ^ 1)]], axis=0
        )
        out[...] = half_step * rotate(pair.T)


def ham_kernel(slabs, near, far, next_near, next_far, own_e, mate_e, own_t, mate_t, *refs):
    out, here, there = refs[-3:]
    linked = lax.axis_index("slab") < slabs - 1
    load_vector(here, near[...], far[...])
    load_vector(there, keep(linked, next_near), keep(linked, next_far))
    ham = real_product(own_e[0], mate_e[0], here) + real_product(own_t[0], mate_t[0], there)
    out[...] = near[...] - half_step * rotate(ham)


def level_kernel(spacing, near, far, own, mate, *refs):
    beneath, above, store = refs[-3:]

    @pl.when(lax.axis_index("slab") % (2 * spacing) == spacing)
    def _():
        load_vector(store, near[...], far[...])
        above[...] = complex_product(own[2:4], mate[2:4], store)
        beneath[...] = complex_product(own[0:2], mate[0:2], store)


def top_kernel(spacing, near, far, own, mate, *refs):
    beneath, store = refs[-2:]

    @pl.when(lax.axis_index("slab") % (2 * spacing) == spacing)
    def _():
        load_vector(store, near[...], far[...])
        beneath[...] = complex_product(own[0:2], mate[0:2], store)


def pivot_kernel(spacing, near, far, own, mate, before, out, store):
    active = lax.axis_index("slab") % (2 * spacing) == spacing

    @pl.when(active)
    def _():
        load_vector(store, near[...], far[...])
        out[...] = complex_product(own[4:6], mate[4:6], store)

    @pl.when(jnp.logical_not(active))
    def _():
        out[...] = before[...]


def root_kernel(count, *refs):
    near, far = refs[:2]
    shares = refs[2 : 2 + 2 * count]
    own, mate, before, out, store = refs[2 + 2 * count :]
    root = lax.axis_index("slab") == 0

    @pl.when(root)
    def _():
        whole = [near[...], far[...]]
        for n, share in enumerate(shares):
            whole[n % 2] = whole[n % 2] - share[...]
        load_vector(store, *whole)
        out[...] = complex_product(own[4:6], mate[4:6], store)

    @pl.when(jnp.logical_not(root))
    def _():
        out[...] = before[...]


def settle_kernel(spacing, part, near, far, own, mate, out, store):
    active = lax.axis_index("slab") % (2 * spacing) == spacing

    @pl.when(active)
    def _():
        load_vector(store, near[...], far[...])
        out[...] = part[...] - complex_product(own[6:8], mate[6:8], store)

    @pl.when(jnp.logical_not(active))
    def _():
        out[...] = part[...]


def both_kernel(slabs, spacing, count, part, other, *refs):
    vectors = refs[:4]
    early = refs[4:count]
    own, mate, out, lower, upper = refs[count:]
    s = lax.axis_index("slab")
    active = s % (2 * spacing) == spacing
    first = s % (4 * spacing) == spacing
    linked = s + spacing < slabs

    def pick(n, wanted):
        values = vectors[n][...]
        return jnp.where(wanted, early[n][...], values) if n < len(early) else values

    @pl.when(active)
    def _():
        load_vector(lower, pick(0, first), pick(1, first))
        out[...] = part[...] - complex_product(own[6:8], mate[6:8], lower)

    @pl.when(active & linked)
    def _():
        second = jnp.logical_not(first)
        load_vector(upper, pick(2, second), pick(3, second))
        out[...] -= complex_product(own[8:10], mate[8:10], upper)

    @pl.when(jnp.logical_not(active))
    def _():
        out[...] = other[...]


def copy_kernel(values, *refs):
    refs[-1][...] = values[...]


def call(
    kernel,
    *operands,
    outs=1,
    scratch=(),
    unused=(),
    shape=jax.ShapeDtypeStruct((Q, LANES), wide),
    flops=10**9,
):
    vmem = pl.BlockSpec(memory_space=pltpu.VMEM)
    return pl.pallas_call(
        kernel,
        out_shape=shape if outs == 1 else (shape,) * outs,
        in_specs=[vmem] * len(operands) + [pl.BlockSpec(memory_space=pl.ANY)] * len(unused),
        out_specs=vmem if outs == 1 else (vmem,) * outs,
        scratch_shapes=list(scratch),
        cost_estimate=pl.CostEstimate(flops=flops, bytes_accessed=1, transcendentals=0),
        compiler_params=pltpu.CompilerParams(vmem_limit_bytes=16 * 2**20),
    )(*operands, *unused)


def completed(route, count, cols):
    target = dict(route)
    taken = set(target.values())
    for a in [a for a in range(count) if a not in target and a not in taken]:
        target[a] = a
        taken.add(a)
    for a in range(count):
        if a not in target:
            target[a] = next(b for b in range(count) if b not in taken and b % cols == a % cols)
            taken.add(target[a])
    if sorted(target.values()) != list(range(count)):
        raise ValueError("no permutation")
    return sorted(target.items())


def per_device(slabs, cols, waves, energy, tunnel, pivots, below, above, back_lower, back_upper):
    everyone = range(cols)
    width = energy.shape[2]
    store = pltpu.VMEM((width, LANES), short)
    levels = slabs.bit_length() - 1
    every = range(slabs)
    s = lax.axis_index("slab")

    def send(values, moves, flip=0):
        route = []
        for c in everyone:
            for a, b, *h in moves:
                route.append((a * cols + c, b * cols + (c ^ flip)))
                for h in h:
                    route.append((b * cols + (c ^ flip), h * cols + c))
                    route.append((h * cols + c, a * cols + c))
        return lax.ppermute(values, ("slab", "col"), completed(route, slabs * cols, cols))

    def both(values, near_moves, far_moves):
        return send(values, near_moves), send(values, far_moves, 2)

    def swap(values):
        return send(values, [(a, a) for a in every], 1)

    def exchange(values, chosen=every):
        return send(values, [(a, a) for a in chosen], 2)

    def kernel(body, *arguments):
        return functools.partial(body, *arguments)

    def stack(*arrays, after):
        depth = sum(v.shape[0] for v in arrays)
        shape = jax.ShapeDtypeStruct((depth, Q, width), wide)
        return call(stack_kernel, *arrays, unused=(after,), shape=shape, flops=1)

    mate_waves = swap(waves)
    t_pair = tunnel, swap(tunnel)
    e_pair = energy, swap(energy)
    side = call(side_kernel, shape=jax.ShapeDtypeStruct((8, LANES), jnp.int32))
    psi, up_near, up_far = call(
        open_kernel, waves, mate_waves, side, *t_pair, outs=3, scratch=[pltpu.VMEM((64, width), wide)]
    )
    up = up_near + exchange(up_far)
    prev = send(up, [(a, a + 1) for a in every[:-1]])
    down = [(a + 1, a) for a in every[:-1]]
    next_near = send(psi, down)
    next_far = send(psi, down, 2)
    rest = call(
        kernel(ham_kernel, slabs),
        psi,
        exchange(psi),
        next_near,
        next_far,
        *e_pair,
        *t_pair,
        scratch=[store, store],
        unused=(up,),
    )
    base = near = rest - jnp.where(s > 0, prev, 0.0)
    front = stack(below[0], above[0], pivots[0], back_lower[0], back_upper[0], after=near)
    front = front, swap(front)
    back = front

    pivot = base
    far = exchange(near, [a for a in every if a % 2 == 1])
    for level in range(levels):
        d = 2**level
        if level == levels - 1:
            beneath = call(kernel(top_kernel, d), near, far, *front, scratch=[store])
            shares = both(beneath, [(d, 0, d - 1)], [(d, 0, d - 3)])
            if level > 1:
                shares = shares + late
            pivot = call(kernel(pivot_kernel, d), near, far, *back, pivot, scratch=[store])
            pivot = call(
                kernel(root_kernel, len(shares) // 2),
                base,
                base_far,
                *shares,
                *back,
                pivot,
                scratch=[store],
            )
            break
        urgent = [b for b in every if b % (4 * d) == 2 * d]
        patient = [b for b in every if b % (4 * d) == 0]
        beneath, over = call(
            kernel(level_kernel, d),
            near,
            far,
            *front,
            outs=2,
            scratch=[store],
            unused=() if level == 0 else (base,),
        )
        if level == 0:
            more = send(over, [(b - 1, b, b - 2) for b in urgent])
            less = send(beneath, [(b + 1, b, b - 2) for b in urgent])
            pivot = call(kernel(pivot_kernel, d), near, far, *back, pivot, scratch=[store])
            held = call(copy_kernel, beneath, unused=(pivot,))
            late = [send(held, [(b + 1, b, b + 3) for b in patient])]
            if len(patient) > 1:
                held = call(copy_kernel, over, unused=(pivot,))
                late.append(send(held, [(b - 1, b, b + 1) for b in patient if b > 0]))
            near = base - more - less
            far = exchange(near, urgent)
            base = call(kernel(reduce_kernel, d, len(late)), base, *late)
            base_far = exchange(base, patient)
            continue
        more = both(over, [(b - d, b, b - 1) for b in urgent], [(b - d, b, b - 3) for b in urgent])
        less = both(
            beneath, [(b + d, b, b + 1) for b in urgent], [(b + d, b, b + 3) for b in urgent]
        )
        pivot = call(kernel(pivot_kernel, d), near, far, *back, pivot, scratch=[store])
        if level > 1:
            is_late = s % (2 * d) == 0
            for n, share in enumerate(late):
                share = jnp.where(is_late & ((s > 0) | (n < 2)), share, 0.0)
                if n % 2 == 0:
                    base = base - share
                else:
                    base_far = base_far - share
        near = base - more[0] - less[0]
        far = base_far - more[1] - less[1]
        held = call(copy_kernel, beneath, unused=(base_far,))
        late = both(
            held, [(b + d, b, b + d + 1) for b in patient], [(b + d, b, b + d + 3) for b in patient]
        )
        if len(patient) > 1:
            held = call(copy_kernel, over, unused=(base_far,))
            late = late + both(
                held,
                [(b - d, b, b - d + 1) for b in patient if b > 0],
                [(b - d, b, b - d + 3) for b in patient if b > 0],
            )

    solved = pivot
    for level in reversed(range(levels)):
        d = 2**level
        sources = [a for a in every if a % (2 * d) == 0]
        upper = [a for a in sources if a > 0]
        if d == 1:
            low_near = send(solved, [(a, a ^ 1) for a in every])
            ways = [(a, a - 1) for a in upper] + [(a - 1, a) for a in upper]
            up_near = send(solved, ways)
            up_far = send(solved, ways, 2)
            low_far = exchange(low_near, [a + 1 for a in sources])
            vectors = low_near, low_far, up_near, up_far
        elif level == levels - 1:
            vectors = both(solved, [(0, d, 1)], [(0, d, 3)])
        else:
            sources = [a for a in every if a % (4 * d) == 2 * d]
            up_near = send(solved, [(a, a - d, a + 1) for a in sources])
            low_near = send(solved, [(a, a + d, a - 1) for a in sources])
            up_far = send(solved, [(a, a - d, a + 3) for a in sources], 2)
            low_far = send(solved, [(a, a + d, a - 3) for a in sources], 2)
            vectors = (low_near, low_far, up_near, up_far) + early
        if level > 1:
            half = d // 2
            sources = [a for a in every if a % (2 * d) == 0]
            early = both(
                solved,
                [(a, a + half, a + 2 * half + 1) for a in sources],
                [(a, a + half, a + 2 * half + 3) for a in sources],
            )
            if len(sources) > 1:
                early += both(
                    solved,
                    [(a, a - half, a - 2 * half + 1) for a in sources if a > 0],
                    [(a, a - half, a - 2 * half + 3) for a in sources if a > 0],
                )
        if level == levels - 1 and levels > 1:
            solved = call(kernel(settle_kernel, d), pivot, *vectors, *back, scratch=[store])
        else:
            solved = call(
                kernel(both_kernel, slabs, d, len(vectors)),
                pivot,
                solved,
                *vectors,
                *back,
                scratch=[store, store],
            )
    out = call(regroup_kernel, solved, swap(solved))
    return out[None]


def solution(mesh):
    slabs, cols = mesh.shape["slab"], mesh.shape["col"]
    vector = P("slab", "col", None)
    block = P("slab", None, "col", None)
    return jax.shard_map(
        functools.partial(per_device, slabs, cols),
        mesh=mesh,
        in_specs=(vector,) * 3 + (block,) * 5,
        out_specs=vector,
        check_vma=False,
    )
```

```python
import functools

import jax
import jax.numpy as jnp
from jax import lax
from jax.experimental import pallas as pl
from jax.experimental.pallas import tpu as pltpu
from jax.sharding import PartitionSpec as P


half_step = 0.5
wide = jnp.float32
short = jnp.bfloat16
Q = 128
LANES = 128


def lanes(values):
    return lax.broadcasted_iota(jnp.int32, values.shape, 1)


def swap_halves(values):
    return pltpu.roll(values, 64, 1)


def join(left, right):
    return jnp.where(lanes(left) < 64, left, right)


def rotate(values):
    even = lanes(values) % 2 == 0
    return jnp.where(even, -pltpu.roll(values, LANES - 1, 1), pltpu.roll(values, 1, 1))


def split(values):
    high = values.astype(short)
    return high, (values - high.astype(wide)).astype(short)


def quarter(number):
    return pl.ds(pl.multiple_of(number * Q, Q), Q)


def spread(store, packed, first):
    high = packed.astype(short).astype(wide)
    low = packed - high
    store[quarter(first), :] = join(high, swap_halves(low)).astype(short)
    store[quarter(first ^ 1), :] = join(swap_halves(high), low).astype(short)


def load_vector(store, near, far):
    c = lax.axis_index("col")
    spread(store, near, c)
    spread(store, far, c ^ 2)


def keep(wanted, values):
    return jnp.where(wanted, values[...], 0.0)


def rows_product(block, store):
    high, low = split(block)
    vector = store[...]
    return jnp.dot(high, vector, preferred_element_type=wide) + jnp.dot(
        low, vector, preferred_element_type=wide
    )


def fold(values):
    return values + swap_halves(values)


def real_product(own, mate, store):
    return join(fold(rows_product(own, store)), fold(rows_product(mate, store)))


def complex_half(block, store):
    both = rows_product(block.reshape(2 * Q, block.shape[-1]), store)
    return fold(both[:Q] + rotate(both[Q:]))


def complex_product(own, mate, store):
    return join(complex_half(own, store), complex_half(mate, store))


def this_core(left, right):
    first = lax.axis_index("col") % 2 == 0
    return jnp.where(first, join(left, swap_halves(right)), join(swap_halves(left), right))


def side_kernel(side):
    side[...] = jnp.zeros_like(side) + lax.axis_index("col")


def regroup_kernel(mine, other, out):
    rows = join(mine[...], other[...])
    out[...] = jnp.where(lax.axis_index("col") % 2 == 0, rows, swap_halves(rows))


def stack_kernel(*refs):
    *sources, _, out = refs
    place = 0
    for source in sources:
        depth = source.shape[0]
        out[place : place + depth] = source[...]
        place += depth


def reduce_kernel(spacing, count, base, *refs):
    out = refs[-1]
    less, *more = refs[:count]
    s = lax.axis_index("slab")
    kept = s % (4 * spacing) == 0
    values = base[...] - keep(kept, less)
    for late in more:
        values = values - keep(kept & (s > 0), late)
    out[...] = values


def open_kernel(mine, other, side, own, mate, psi, near, far, store):
    c = lax.axis_index("col")
    packed = this_core(mine[0], other[0])
    psi[...] = packed
    turned = packed.T
    total = None
    for rows, block in ((turned[:64], own[0]), (turned[64:], mate[0])):
        high, low = split(rows)
        pair = jnp.concatenate([high, low], axis=0)
        block_high, block_low = split(block)
        part = jnp.dot(pair, block_high, preferred_element_type=wide) + jnp.dot(
            pair, block_low, preferred_element_type=wide
        )
        part = part[:64] + part[64:]
        total = part if total is None else total + part
    store[...] = total
    for out, first in ((far, c ^ 2), (near, c)):
        pair = jnp.concatenate(
            [store[:, quarter(first)], store[:, quarter(first ^ 1)]], axis=0
        )
        out[...] = half_step * rotate(pair.T)


def ham_kernel(slabs, near, far, next_near, next_far, own_e, mate_e, own_t, mate_t, *refs):
    out, here, there = refs[-3:]
    linked = lax.axis_index("slab") < slabs - 1
    load_vector(here, near[...], far[...])
    load_vector(there, keep(linked, next_near), keep(linked, next_far))
    ham = real_product(own_e[0], mate_e[0], here) + real_product(own_t[0], mate_t[0], there)
    out[...] = near[...] - half_step * rotate(ham)


def level_kernel(spacing, near, far, own, mate, tail, *refs):
    beneath, above, store = refs[-3:]

    @pl.when(lax.axis_index("slab") % (2 * spacing) == spacing)
    def _():
        load_vector(store, near[...], far[...])
        above[...] = complex_product(own[2:4], mate[2:4], store) + tail[...]
        beneath[...] = complex_product(own[0:2], mate[0:2], store)


def top_kernel(spacing, near, far, own, mate, *refs):
    beneath, store = refs[-2:]

    @pl.when(lax.axis_index("slab") % (2 * spacing) == spacing)
    def _():
        load_vector(store, near[...], far[...])
        beneath[...] = complex_product(own[0:2], mate[0:2], store)


def pivot_kernel(spacing, near, far, own, mate, before, out, store):
    active = lax.axis_index("slab") % (2 * spacing) == spacing

    @pl.when(active)
    def _():
        load_vector(store, near[...], far[...])
        out[...] = complex_product(own[4:6], mate[4:6], store)

    @pl.when(jnp.logical_not(active))
    def _():
        out[...] = before[...]


def root_kernel(count, *refs):
    near, far = refs[:2]
    shares = refs[2 : 2 + 2 * count]
    own, mate, before, out, store = refs[2 + 2 * count :]
    root = lax.axis_index("slab") == 0

    @pl.when(root)
    def _():
        whole = [near[...], far[...]]
        for n, share in enumerate(shares):
            whole[n % 2] = whole[n % 2] - share[...]
        load_vector(store, *whole)
        out[...] = complex_product(own[4:6], mate[4:6], store)

    @pl.when(jnp.logical_not(root))
    def _():
        out[...] = before[...]


def settle_kernel(spacing, part, near, far, own, mate, out, store):
    active = lax.axis_index("slab") % (2 * spacing) == spacing

    @pl.when(active)
    def _():
        load_vector(store, near[...], far[...])
        out[...] = part[...] - complex_product(own[6:8], mate[6:8], store)

    @pl.when(jnp.logical_not(active))
    def _():
        out[...] = part[...]


def both_kernel(slabs, spacing, count, part, other, *refs):
    vectors = refs[:4]
    early = refs[4:count]
    own, mate, out, lower, upper = refs[count:]
    s = lax.axis_index("slab")
    active = s % (2 * spacing) == spacing
    first = s % (4 * spacing) == spacing
    linked = s + spacing < slabs

    def pick(n, wanted):
        values = vectors[n][...]
        return jnp.where(wanted, early[n][...], values) if n < len(early) else values

    @pl.when(active)
    def _():
        load_vector(lower, pick(0, first), pick(1, first))
        out[...] = part[...] - complex_product(own[6:8], mate[6:8], lower)

    @pl.when(active & linked)
    def _():
        second = jnp.logical_not(first)
        load_vector(upper, pick(2, second), pick(3, second))
        out[...] -= complex_product(own[8:10], mate[8:10], upper)

    @pl.when(jnp.logical_not(active))
    def _():
        out[...] = other[...]


def copy_kernel(values, *refs):
    refs[-1][...] = values[...]


def call(
    kernel,
    *operands,
    outs=1,
    scratch=(),
    unused=(),
    shape=jax.ShapeDtypeStruct((Q, LANES), wide),
    flops=10**9,
):
    vmem = pl.BlockSpec(memory_space=pltpu.VMEM)
    return pl.pallas_call(
        kernel,
        out_shape=shape if outs == 1 else (shape,) * outs,
        in_specs=[vmem] * len(operands) + [pl.BlockSpec(memory_space=pl.ANY)] * len(unused),
        out_specs=vmem if outs == 1 else (vmem,) * outs,
        scratch_shapes=list(scratch),
        cost_estimate=pl.CostEstimate(flops=flops, bytes_accessed=1, transcendentals=0),
        compiler_params=pltpu.CompilerParams(vmem_limit_bytes=16 * 2**20),
    )(*operands, *unused)


def completed(route, count, cols):
    target = dict(route)
    taken = set(target.values())
    for a in [a for a in range(count) if a not in target and a not in taken]:
        target[a] = a ^ 1
        taken.add(a ^ 1)
    for a in range(count):
        if a not in target:
            target[a] = next(b for b in range(count) if b not in taken and b % cols == a % cols)
            taken.add(target[a])
    if sorted(target.values()) != list(range(count)):
        raise ValueError("no permutation")
    return sorted(target.items())


def per_device(slabs, cols, waves, energy, tunnel, pivots, below, above, back_lower, back_upper):
    everyone = range(cols)
    width = energy.shape[2]
    store = pltpu.VMEM((width, LANES), short)
    levels = slabs.bit_length() - 1
    every = range(slabs)
    s = lax.axis_index("slab")

    def send(values, moves, flip=0):
        route = []
        for c in everyone:
            for a, b, *h in moves:
                route.append((a * cols + c, b * cols + (c ^ flip)))
                for h in h:
                    route.append((b * cols + (c ^ flip), h * cols + c))
                    route.append((h * cols + c, a * cols + c))
        return lax.ppermute(values, ("slab", "col"), completed(route, slabs * cols, cols))

    def both(values, near_moves, far_moves):
        return send(values, near_moves), send(values, far_moves, 2)

    def swap(values):
        return send(values, [(a, a) for a in every], 1)

    def exchange(values, chosen=every):
        return send(values, [(a, a) for a in chosen], 2)

    def kernel(body, *arguments):
        return functools.partial(body, *arguments)

    def stack(*arrays, after):
        depth = sum(v.shape[0] for v in arrays)
        shape = jax.ShapeDtypeStruct((depth, Q, width), wide)
        return call(stack_kernel, *arrays, unused=(after,), shape=shape, flops=1)

    mate_waves = swap(waves)
    t_pair = tunnel, swap(tunnel)
    e_pair = energy, swap(energy)
    side = call(side_kernel, shape=jax.ShapeDtypeStruct((8, LANES), jnp.int32))
    psi, up_near, up_far = call(
        open_kernel, waves, mate_waves, side, *t_pair, outs=3, scratch=[pltpu.VMEM((64, width), wide)]
    )
    up = up_near + exchange(up_far)
    prev_odd = send(up, [(a, a ^ 1) for a in every])
    down = [(a + 1, a) for a in every[:-1]]
    next_near = send(psi, down)
    next_far = send(psi, down, 2)
    rest = call(
        kernel(ham_kernel, slabs),
        psi,
        exchange(psi),
        next_near,
        next_far,
        *e_pair,
        *t_pair,
        scratch=[store, store],
        unused=(up,),
    )
    near = rest - prev_odd
    far = exchange(near)
    blocks = (below[0], above[0], pivots[0], back_lower[0], back_upper[0])
    front = stack(*blocks, after=near)
    front = front, swap(front)
    back = front
    base = rest

    pivot = near
    for level in range(levels):
        d = 2**level
        if level == levels - 1:
            beneath = call(kernel(top_kernel, d), near, far, *front, scratch=[store])
            shares = both(beneath, [(d, 0, d - 1)], [(d, 0, d - 3)])
            if level > 1:
                shares = shares + late
            pivot = call(kernel(pivot_kernel, d), near, far, *back, pivot, scratch=[store])
            pivot = call(
                kernel(root_kernel, len(shares) // 2),
                base,
                base_far,
                *shares,
                *back,
                pivot,
                scratch=[store],
            )
            break
        urgent = [b for b in every if b % (4 * d) == 2 * d]
        patient = [b for b in every if b % (4 * d) == 0]
        beneath, over = call(
            kernel(level_kernel, d),
            near,
            far,
            *front,
            up if level == 0 else jnp.zeros_like(up),
            outs=2,
            scratch=[store],
            unused=() if level == 0 else (base,),
        )
        if level == 0:
            more = send(over, [(b - 1, b, b - 2) for b in urgent])
            less = send(beneath, [(b + 1, b, b - 2) for b in urgent])
            pivot = call(kernel(pivot_kernel, d), near, far, *back, pivot, scratch=[store])
            held = call(copy_kernel, beneath, unused=(pivot,))
            late = [send(held, [(b + 1, b, b + 3) for b in patient])]
            if len(patient) > 1:
                held = call(copy_kernel, over, unused=(pivot,))
                late.append(send(held, [(b - 1, b, b + 1) for b in patient if b > 0]))
            near = base - more - less
            far = exchange(near, urgent)
            base = call(kernel(reduce_kernel, d, len(late)), base, *late)
            base_far = exchange(base, patient)
            continue
        more = both(over, [(b - d, b, b - 1) for b in urgent], [(b - d, b, b - 3) for b in urgent])
        less = both(
            beneath, [(b + d, b, b + 1) for b in urgent], [(b + d, b, b + 3) for b in urgent]
        )
        pivot = call(kernel(pivot_kernel, d), near, far, *back, pivot, scratch=[store])
        if level > 1:
            is_late = s % (2 * d) == 0
            for n, share in enumerate(late):
                share = jnp.where(is_late & ((s > 0) | (n < 2)), share, 0.0)
                if n % 2 == 0:
                    base = base - share
                else:
                    base_far = base_far - share
        near = base - more[0] - less[0]
        far = base_far - more[1] - less[1]
        held = call(copy_kernel, beneath, unused=(base_far,))
        late = both(
            held, [(b + d, b, b + d + 1) for b in patient], [(b + d, b, b + d + 3) for b in patient]
        )
        if len(patient) > 1:
            held = call(copy_kernel, over, unused=(base_far,))
            late = late + both(
                held,
                [(b - d, b, b - d + 1) for b in patient if b > 0],
                [(b - d, b, b - d + 3) for b in patient if b > 0],
            )

    solved = pivot
    for level in reversed(range(levels)):
        d = 2**level
        sources = [a for a in every if a % (2 * d) == 0]
        upper = [a for a in sources if a > 0]
        if d == 1:
            low_near = send(solved, [(a, a ^ 1) for a in every])
            ways = [(a, a - 1) for a in upper] + [(a - 1, a) for a in upper]
            up_near = send(solved, ways)
            up_far = send(solved, ways, 2)
            low_far = exchange(low_near, [a + 1 for a in sources])
            vectors = low_near, low_far, up_near, up_far
        elif level == levels - 1:
            vectors = both(solved, [(0, d, 1)], [(0, d, 3)])
        else:
            sources = [a for a in every if a % (4 * d) == 2 * d]
            up_near = send(solved, [(a, a - d, a + 1) for a in sources])
            low_near = send(solved, [(a, a + d, a - 1) for a in sources])
            up_far = send(solved, [(a, a - d, a + 3) for a in sources], 2)
            low_far = send(solved, [(a, a + d, a - 3) for a in sources], 2)
            vectors = (low_near, low_far, up_near, up_far) + early
        if level > 1:
            half = d // 2
            sources = [a for a in every if a % (2 * d) == 0]
            early = both(
                solved,
                [(a, a + half, a + 2 * half + 1) for a in sources],
                [(a, a + half, a + 2 * half + 3) for a in sources],
            )
            if len(sources) > 1:
                early += both(
                    solved,
                    [(a, a - half, a - 2 * half + 1) for a in sources if a > 0],
                    [(a, a - half, a - 2 * half + 3) for a in sources if a > 0],
                )
        if level == levels - 1 and levels > 1:
            solved = call(kernel(settle_kernel, d), pivot, *vectors, *back, scratch=[store])
        else:
            solved = call(
                kernel(both_kernel, slabs, d, len(vectors)),
                pivot,
                solved,
                *vectors,
                *back,
                scratch=[store, store],
            )
    out = call(regroup_kernel, solved, swap(solved))
    return out[None]


def solution(mesh):
    slabs, cols = mesh.shape["slab"], mesh.shape["col"]
    vector = P("slab", "col", None)
    block = P("slab", None, "col", None)
    return jax.shard_map(
        functools.partial(per_device, slabs, cols),
        mesh=mesh,
        in_specs=(vector,) * 3 + (block,) * 5,
        out_specs=vector,
        check_vma=False,
    )
```

```python
import functools

import jax
import jax.numpy as jnp
from jax import lax
from jax.experimental import pallas as pl
from jax.experimental.pallas import tpu as pltpu
from jax.sharding import PartitionSpec as P


half_step = 0.5
wide = jnp.float32
short = jnp.bfloat16
Q = 128
LANES = 128


def lanes(values):
    return lax.broadcasted_iota(jnp.int32, values.shape, 1)


def swap_halves(values):
    return pltpu.roll(values, 64, 1)


def join(left, right):
    return jnp.where(lanes(left) < 64, left, right)


def rotate(values):
    even = lanes(values) % 2 == 0
    return jnp.where(even, -pltpu.roll(values, LANES - 1, 1), pltpu.roll(values, 1, 1))


def split(values):
    high = values.astype(short)
    return high, (values - high.astype(wide)).astype(short)


def quarter(number):
    return pl.ds(pl.multiple_of(number * Q, Q), Q)


def spread(store, packed, first):
    high = packed.astype(short).astype(wide)
    low = packed - high
    store[quarter(first), :] = join(high, swap_halves(low)).astype(short)
    store[quarter(first ^ 1), :] = join(swap_halves(high), low).astype(short)


def load_vector(store, near, far):
    c = lax.axis_index("col")
    spread(store, near, c)
    spread(store, far, c ^ 2)


def keep(wanted, values):
    return jnp.where(wanted, values[...], 0.0)


def rows_product(block, store):
    high, low = split(block)
    vector = store[...]
    return jnp.dot(high, vector, preferred_element_type=wide) + jnp.dot(
        low, vector, preferred_element_type=wide
    )


def fold(values):
    return values + swap_halves(values)


def real_product(own, mate, store):
    return join(fold(rows_product(own, store)), fold(rows_product(mate, store)))


def complex_half(block, store):
    both = rows_product(block.reshape(2 * Q, block.shape[-1]), store)
    return fold(both[:Q] + rotate(both[Q:]))


def complex_product(own, mate, store):
    return join(complex_half(own, store), complex_half(mate, store))


def this_core(left, right):
    first = lax.axis_index("col") % 2 == 0
    return jnp.where(first, join(left, swap_halves(right)), join(swap_halves(left), right))


def side_kernel(side):
    side[...] = jnp.zeros_like(side) + lax.axis_index("col")


def regroup_kernel(mine, other, out):
    rows = join(mine[...], other[...])
    out[...] = jnp.where(lax.axis_index("col") % 2 == 0, rows, swap_halves(rows))


def stack_kernel(*refs):
    *sources, _, out = refs
    place = 0
    for source in sources:
        depth = source.shape[0]
        out[place : place + depth] = source[...]
        place += depth


def reduce_kernel(spacing, count, base, *refs):
    out = refs[-1]
    less, *more = refs[:count]
    s = lax.axis_index("slab")
    kept = s % (4 * spacing) == 0
    values = base[...] - keep(kept, less)
    for late in more:
        values = values - keep(kept & (s > 0), late)
    out[...] = values


def open_kernel(mine, other, side, own, mate, psi, near, far, store):
    c = lax.axis_index("col")
    packed = this_core(mine[0], other[0])
    psi[...] = packed
    turned = packed.T
    total = None
    for rows, block in ((turned[:64], own[0]), (turned[64:], mate[0])):
        high, low = split(rows)
        pair = jnp.concatenate([high, low], axis=0)
        block_high, block_low = split(block)
        part = jnp.dot(pair, block_high, preferred_element_type=wide) + jnp.dot(
            pair, block_low, preferred_element_type=wide
        )
        part = part[:64] + part[64:]
        total = part if total is None else total + part
    store[...] = total
    for out, first in ((far, c ^ 2), (near, c)):
        pair = jnp.concatenate(
            [store[:, quarter(first)], store[:, quarter(first ^ 1)]], axis=0
        )
        out[...] = half_step * rotate(pair.T)


def ham_kernel(slabs, near, far, next_near, next_far, own_e, mate_e, own_t, mate_t, *refs):
    out, here, there = refs[-3:]
    s = lax.axis_index("slab")
    load_vector(here, near[...], far[...])
    out[...] = near[...] - half_step * rotate(real_product(own_e[0], mate_e[0], here))

    @pl.when((s % 2 == 1) & (s < slabs - 1))
    def _():
        load_vector(there, next_near[...], next_far[...])
        out[...] -= half_step * rotate(real_product(own_t[0], mate_t[0], there))


def even_kernel(rest, next_near, next_far, own, mate, out, store):
    @pl.when(lax.axis_index("slab") % 2 == 0)
    def _():
        load_vector(store, next_near[...], next_far[...])
        out[...] = rest[...] - half_step * rotate(real_product(own[0], mate[0], store))


def level_kernel(spacing, near, far, own, mate, tail, *refs):
    beneath, above, store = refs[-3:]

    @pl.when(lax.axis_index("slab") % (2 * spacing) == spacing)
    def _():
        load_vector(store, near[...], far[...])
        above[...] = complex_product(own[2:4], mate[2:4], store) + tail[...]
        beneath[...] = complex_product(own[0:2], mate[0:2], store)


def top_kernel(spacing, near, far, own, mate, *refs):
    beneath, store = refs[-2:]

    @pl.when(lax.axis_index("slab") % (2 * spacing) == spacing)
    def _():
        load_vector(store, near[...], far[...])
        beneath[...] = complex_product(own[0:2], mate[0:2], store)


def pivot_kernel(spacing, near, far, own, mate, before, out, store):
    active = lax.axis_index("slab") % (2 * spacing) == spacing

    @pl.when(active)
    def _():
        load_vector(store, near[...], far[...])
        out[...] = complex_product(own[4:6], mate[4:6], store)

    @pl.when(jnp.logical_not(active))
    def _():
        out[...] = before[...]


def root_kernel(count, *refs):
    near, far = refs[:2]
    shares = refs[2 : 2 + 2 * count]
    own, mate, before, out, store = refs[2 + 2 * count :]
    root = lax.axis_index("slab") == 0

    @pl.when(root)
    def _():
        whole = [near[...], far[...]]
        for n, share in enumerate(shares):
            whole[n % 2] = whole[n % 2] - share[...]
        load_vector(store, *whole)
        out[...] = complex_product(own[4:6], mate[4:6], store)

    @pl.when(jnp.logical_not(root))
    def _():
        out[...] = before[...]


def settle_kernel(spacing, part, near, far, own, mate, out, store):
    active = lax.axis_index("slab") % (2 * spacing) == spacing

    @pl.when(active)
    def _():
        load_vector(store, near[...], far[...])
        out[...] = part[...] - complex_product(own[6:8], mate[6:8], store)

    @pl.when(jnp.logical_not(active))
    def _():
        out[...] = part[...]


def both_kernel(slabs, spacing, count, part, other, *refs):
    vectors = refs[:4]
    early = refs[4:count]
    own, mate, out, lower, upper = refs[count:]
    s = lax.axis_index("slab")
    active = s % (2 * spacing) == spacing
    first = s % (4 * spacing) == spacing
    linked = s + spacing < slabs

    def pick(n, wanted):
        values = vectors[n][...]
        return jnp.where(wanted, early[n][...], values) if n < len(early) else values

    @pl.when(active)
    def _():
        load_vector(lower, pick(0, first), pick(1, first))
        out[...] = part[...] - complex_product(own[6:8], mate[6:8], lower)

    @pl.when(active & linked)
    def _():
        second = jnp.logical_not(first)
        load_vector(upper, pick(2, second), pick(3, second))
        out[...] -= complex_product(own[8:10], mate[8:10], upper)

    @pl.when(jnp.logical_not(active))
    def _():
        out[...] = other[...]


def copy_kernel(values, *refs):
    refs[-1][...] = values[...]


def call(
    kernel,
    *operands,
    outs=1,
    scratch=(),
    unused=(),
    shape=jax.ShapeDtypeStruct((Q, LANES), wide),
    flops=10**9,
):
    vmem = pl.BlockSpec(memory_space=pltpu.VMEM)
    return pl.pallas_call(
        kernel,
        out_shape=shape if outs == 1 else (shape,) * outs,
        in_specs=[vmem] * len(operands) + [pl.BlockSpec(memory_space=pl.ANY)] * len(unused),
        out_specs=vmem if outs == 1 else (vmem,) * outs,
        scratch_shapes=list(scratch),
        cost_estimate=pl.CostEstimate(flops=flops, bytes_accessed=1, transcendentals=0),
        compiler_params=pltpu.CompilerParams(vmem_limit_bytes=16 * 2**20),
    )(*operands, *unused)


def completed(route, count, cols):
    target = dict(route)
    taken = set(target.values())
    for a in [a for a in range(count) if a not in target and a not in taken]:
        target[a] = a ^ 1
        taken.add(a ^ 1)
    for a in range(count):
        if a not in target:
            target[a] = next(b for b in range(count) if b not in taken and b % cols == a % cols)
            taken.add(target[a])
    if sorted(target.values()) != list(range(count)):
        raise ValueError("no permutation")
    return sorted(target.items())


def per_device(slabs, cols, waves, energy, tunnel, pivots, below, above, back_lower, back_upper):
    everyone = range(cols)
    width = energy.shape[2]
    store = pltpu.VMEM((width, LANES), short)
    levels = slabs.bit_length() - 1
    every = range(slabs)
    s = lax.axis_index("slab")
    odd = s % 2 == 1

    def send(values, moves, flip=0):
        route = []
        for c in everyone:
            for a, b, *h in moves:
                route.append((a * cols + c, b * cols + (c ^ flip)))
                here = b * cols + (c ^ flip)
                for h in h:
                    route.append((here, h * cols + c))
                    here = h * cols + c
                if here != b * cols + (c ^ flip):
                    route.append((here, a * cols + c))
        return lax.ppermute(values, ("slab", "col"), completed(route, slabs * cols, cols))

    def both(values, near_moves, far_moves):
        return send(values, near_moves), send(values, far_moves, 2)

    def swap(values):
        return send(values, [(a, a) for a in every], 1)

    def exchange(values, chosen=every):
        return send(values, [(a, a) for a in chosen], 2)

    def kernel(body, *arguments):
        return functools.partial(body, *arguments)

    def stack(*arrays, after):
        depth = sum(v.shape[0] for v in arrays)
        shape = jax.ShapeDtypeStruct((depth, Q, width), wide)
        return call(stack_kernel, *arrays, unused=(after,), shape=shape, flops=1)

    mate_waves = swap(waves)
    t_pair = tunnel, swap(tunnel)
    e_pair = energy, swap(energy)
    side = call(side_kernel, shape=jax.ShapeDtypeStruct((8, LANES), jnp.int32))
    psi, up_near, up_far = call(
        open_kernel, waves, mate_waves, side, *t_pair, outs=3, scratch=[pltpu.VMEM((64, width), wide)]
    )
    up = up_near + exchange(up_far)
    psi_far = exchange(psi)
    between = [(a, b) for k in every[1:-1:2] for a, b in ((k, k + 1), (k + 1, k))]
    stepped = send(jnp.where(odd, psi, up), [(a, a ^ 1) for a in every])
    rest = call(
        kernel(ham_kernel, slabs),
        psi,
        psi_far,
        *both(psi, between, between),
        *e_pair,
        *t_pair,
        scratch=[store, store],
        unused=(up,),
    )
    near = rest - stepped
    far = exchange(jnp.where(odd, near, stepped))
    blocks = below[0], above[0], pivots[0], back_lower[0], back_upper[0]
    front = stack(*blocks, after=near)
    front = front, swap(front)
    back = front
    base = call(even_kernel, rest, stepped, far, *t_pair, scratch=[store])

    pivot = near
    for level in range(levels):
        d = 2**level
        if level == levels - 1:
            beneath = call(kernel(top_kernel, d), near, far, *front, scratch=[store])
            shares = both(beneath, [(d, 0, 1, d + 1)], [(d, 0, 1, d - 1)])
            if level > 1:
                shares = shares + late
            pivot = call(kernel(pivot_kernel, d), near, far, *back, pivot, scratch=[store])
            pivot = call(
                kernel(root_kernel, len(shares) // 2),
                base,
                base_far,
                *shares,
                *back,
                pivot,
                scratch=[store],
            )
            break
        urgent = [b for b in every if b % (4 * d) == 2 * d]
        patient = [b for b in every if b % (4 * d) == 0]
        beneath, over = call(
            kernel(level_kernel, d),
            near,
            far,
            *front,
            up if level == 0 else jnp.zeros_like(up),
            outs=2,
            scratch=[store],
        )
        if level == 0:
            more = send(over, [(b - 1, b, b - 2) for b in urgent])
            less = send(beneath, [(b + 1, b, b - 2) for b in urgent])
            pivot = call(kernel(pivot_kernel, d), near, far, *back, pivot, scratch=[store])
            held = call(copy_kernel, beneath, unused=(pivot,))
            late = [send(held, [(b + 1, b, b + 3) for b in patient])]
            if len(patient) > 1:
                held = call(copy_kernel, over, unused=(pivot,))
                late.append(send(held, [(b - 1, b, b + 1) for b in patient if b > 0]))
            near = base - more - less
            far = exchange(near, urgent)
            continue
        more = both(over, [(b - d, b, b - 1) for b in urgent], [(b - d, b, b - 3) for b in urgent])
        less = both(
            beneath, [(b + d, b, b + 1) for b in urgent], [(b + d, b, b + 3) for b in urgent]
        )
        pivot = call(kernel(pivot_kernel, d), near, far, *back, pivot, scratch=[store])
        if level == 1:
            base = call(kernel(reduce_kernel, 1, len(late)), base, *late, unused=(beneath,))
            base_far = exchange(base, [a for a in every if a % 4 == 0])
        else:
            is_late = s % (2 * d) == 0
            for n, share in enumerate(late):
                share = jnp.where(is_late & ((s > 0) | (n < 2)), share, 0.0)
                if n % 2 == 0:
                    base = base - share
                else:
                    base_far = base_far - share
        near = base - more[0] - less[0]
        far = base_far - more[1] - less[1]
        held = call(copy_kernel, beneath, unused=(base_far,))
        late = both(
            held, [(b + d, b, b + d + 1) for b in patient], [(b + d, b, b + d + 3) for b in patient]
        )
        if len(patient) > 1:
            held = call(copy_kernel, over, unused=(base_far,))
            late = late + both(
                held,
                [(b - d, b, b - d + 1) for b in patient if b > 0],
                [(b - d, b, b - d + 3) for b in patient if b > 0],
            )

    solved = pivot
    for level in reversed(range(levels)):
        d = 2**level
        sources = [a for a in every if a % (2 * d) == 0]
        upper = [a for a in sources if a > 0]
        if d == 1:
            low_near = send(solved, [(a, a ^ 1) for a in every])
            ways = [(a, a - 1) for a in upper] + [(a - 1, a) for a in upper]
            up_near = send(solved, ways)
            up_far = send(solved, ways, 2)
            low_far = exchange(low_near, [a + 1 for a in sources])
            vectors = low_near, low_far, up_near, up_far
        elif level == levels - 1:
            vectors = both(solved, [(0, d, d + 1, 1)], [(0, d, d + 1, 3)])
        else:
            sources = [a for a in every if a % (4 * d) == 2 * d]
            up_near = send(solved, [(a, a - d, a + 1) for a in sources])
            low_near = send(solved, [(a, a + d, a - 1) for a in sources])
            up_far = send(solved, [(a, a - d, a + 3) for a in sources], 2)
            low_far = send(solved, [(a, a + d, a - 3) for a in sources], 2)
            vectors = (low_near, low_far, up_near, up_far) + early
        if level > 1:
            half = d // 2
            sources = [a for a in every if a % (2 * d) == 0]
            early = both(
                solved,
                [(a, a + half, a + 2 * half + 1) for a in sources],
                [(a, a + half, a + 2 * half + 3) for a in sources],
            )
            if len(sources) > 1:
                early += both(
                    solved,
                    [(a, a - half, a - 2 * half + 1) for a in sources if a > 0],
                    [(a, a - half, a - 2 * half + 3) for a in sources if a > 0],
                )
        if level == levels - 1 and levels > 1:
            solved = call(kernel(settle_kernel, d), pivot, *vectors, *back, scratch=[store])
        else:
            solved = call(
                kernel(both_kernel, slabs, d, len(vectors)),
                pivot,
                solved,
                *vectors,
                *back,
                scratch=[store, store],
            )
    out = call(regroup_kernel, solved, swap(solved))
    return out[None]


def solution(mesh):
    slabs, cols = mesh.shape["slab"], mesh.shape["col"]
    vector = P("slab", "col", None)
    block = P("slab", None, "col", None)
    return jax.shard_map(
        functools.partial(per_device, slabs, cols),
        mesh=mesh,
        in_specs=(vector,) * 3 + (block,) * 5,
        out_specs=vector,
        check_vma=False,
    )
```

```python
import functools

import jax
import jax.numpy as jnp
from jax import lax
from jax.experimental import pallas as pl
from jax.experimental.pallas import tpu as pltpu
from jax.sharding import PartitionSpec as P


half_step = 0.5
wide = jnp.float32
short = jnp.bfloat16
Q = 128
LANES = 128


def lanes(values):
    return lax.broadcasted_iota(jnp.int32, values.shape, 1)


def swap_halves(values):
    return pltpu.roll(values, 64, 1)


def join(left, right):
    return jnp.where(lanes(left) < 64, left, right)


def rotate(values):
    even = lanes(values) % 2 == 0
    return jnp.where(even, -pltpu.roll(values, LANES - 1, 1), pltpu.roll(values, 1, 1))


def split(values):
    high = values.astype(short)
    return high, (values - high.astype(wide)).astype(short)


def quarter(number):
    return pl.ds(pl.multiple_of(number * Q, Q), Q)


def spread(store, packed, first):
    high = packed.astype(short).astype(wide)
    low = packed - high
    store[quarter(first), :] = join(high, swap_halves(low)).astype(short)
    store[quarter(first ^ 1), :] = join(swap_halves(high), low).astype(short)


def load_vector(store, near, far):
    c = lax.axis_index("col")
    spread(store, near, c)
    spread(store, far, c ^ 2)


def keep(wanted, values):
    return jnp.where(wanted, values[...], 0.0)


def rows_product(block, store):
    high, low = split(block)
    vector = store[...]
    return jnp.dot(high, vector, preferred_element_type=wide) + jnp.dot(
        low, vector, preferred_element_type=wide
    )


def fold(values):
    return values + swap_halves(values)


def real_product(own, mate, store):
    return join(fold(rows_product(own, store)), fold(rows_product(mate, store)))


def complex_half(block, store):
    both = rows_product(block.reshape(2 * Q, block.shape[-1]), store)
    return fold(both[:Q] + rotate(both[Q:]))


def complex_product(own, mate, store):
    return join(complex_half(own, store), complex_half(mate, store))


def this_core(left, right):
    first = lax.axis_index("col") % 2 == 0
    return jnp.where(first, join(left, swap_halves(right)), join(swap_halves(left), right))


def side_kernel(side):
    side[...] = jnp.zeros_like(side) + lax.axis_index("col")


def regroup_kernel(mine, other, out):
    rows = join(mine[...], other[...])
    out[...] = jnp.where(lax.axis_index("col") % 2 == 0, rows, swap_halves(rows))


def stack_kernel(*refs):
    *sources, _, out = refs
    place = 0
    for source in sources:
        depth = source.shape[0]
        out[place : place + depth] = source[...]
        place += depth


def open_kernel(mine, other, side, own, mate, psi, near, far, store):
    c = lax.axis_index("col")
    packed = this_core(mine[0], other[0])
    psi[...] = packed
    turned = packed.T
    total = None
    for rows, block in ((turned[:64], own[0]), (turned[64:], mate[0])):
        high, low = split(rows)
        pair = jnp.concatenate([high, low], axis=0)
        block_high, block_low = split(block)
        part = jnp.dot(pair, block_high, preferred_element_type=wide) + jnp.dot(
            pair, block_low, preferred_element_type=wide
        )
        part = part[:64] + part[64:]
        total = part if total is None else total + part
    store[...] = total
    for out, first in ((far, c ^ 2), (near, c)):
        pair = jnp.concatenate(
            [store[:, quarter(first)], store[:, quarter(first ^ 1)]], axis=0
        )
        out[...] = half_step * rotate(pair.T)


def cross_kernel(packed, near, other, up, crossing):
    whole = near[...] + other[...]
    up[...] = whole
    crossing[...] = jnp.where(lax.axis_index("slab") % 2 == 1, packed[...], whole)


def near_kernel(rest, stepped, near, crossing):
    whole = rest[...] - stepped[...]
    near[...] = whole
    crossing[...] = jnp.where(lax.axis_index("slab") % 2 == 1, whole, stepped[...])


def urgent_kernel(base, more, less, out):
    kept = lax.axis_index("slab") % 4 == 2
    out[...] = base[...] - keep(kept, more) - keep(kept, less)


def reduce_kernel(spacing, count, base, *refs):
    out = refs[-1]
    less, *more = refs[:count]
    s = lax.axis_index("slab")
    kept = s % (4 * spacing) == 0
    values = base[...] - keep(kept, less)
    for late in more:
        values = values - keep(kept & (s > 0), late)
    out[...] = values


def ham_kernel(slabs, near, far, next_near, next_far, own_e, mate_e, own_t, mate_t, *refs):
    out, here, there = refs[-3:]
    s = lax.axis_index("slab")
    load_vector(here, near[...], far[...])
    out[...] = near[...] - half_step * rotate(real_product(own_e[0], mate_e[0], here))

    @pl.when((s % 2 == 1) & (s < slabs - 1))
    def _():
        load_vector(there, next_near[...], next_far[...])
        out[...] -= half_step * rotate(real_product(own_t[0], mate_t[0], there))


def even_kernel(rest, next_near, next_far, own, mate, out, store):
    @pl.when(lax.axis_index("slab") % 2 == 0)
    def _():
        load_vector(store, next_near[...], next_far[...])
        out[...] = rest[...] - half_step * rotate(real_product(own[0], mate[0], store))


def level_kernel(spacing, near, far, own, mate, tail, *refs):
    beneath, above, store = refs[-3:]

    @pl.when(lax.axis_index("slab") % (2 * spacing) == spacing)
    def _():
        load_vector(store, near[...], far[...])
        above[...] = complex_product(own[2:4], mate[2:4], store) + tail[...]
        beneath[...] = complex_product(own[0:2], mate[0:2], store)


def top_kernel(spacing, near, far, own, mate, *refs):
    beneath, store = refs[-2:]

    @pl.when(lax.axis_index("slab") % (2 * spacing) == spacing)
    def _():
        load_vector(store, near[...], far[...])
        beneath[...] = complex_product(own[0:2], mate[0:2], store)


def pivot_kernel(spacing, near, far, own, mate, before, *refs):
    out, store = refs[-2:]
    active = lax.axis_index("slab") % (2 * spacing) == spacing

    @pl.when(active)
    def _():
        load_vector(store, near[...], far[...])
        out[...] = complex_product(own[4:6], mate[4:6], store)

    @pl.when(jnp.logical_not(active))
    def _():
        out[...] = before[...]


def root_kernel(count, *refs):
    near, far = refs[:2]
    shares = refs[2 : 2 + 2 * count]
    own, mate, before, out, store = refs[2 + 2 * count :]
    root = lax.axis_index("slab") == 0

    @pl.when(root)
    def _():
        whole = [near[...], far[...]]
        for n, share in enumerate(shares):
            whole[n % 2] = whole[n % 2] - share[...]
        load_vector(store, *whole)
        out[...] = complex_product(own[4:6], mate[4:6], store)

    @pl.when(jnp.logical_not(root))
    def _():
        out[...] = before[...]


def settle_kernel(spacing, part, near, far, own, mate, out, store):
    active = lax.axis_index("slab") % (2 * spacing) == spacing

    @pl.when(active)
    def _():
        load_vector(store, near[...], far[...])
        out[...] = part[...] - complex_product(own[6:8], mate[6:8], store)

    @pl.when(jnp.logical_not(active))
    def _():
        out[...] = part[...]


def both_kernel(slabs, spacing, count, part, other, *refs):
    vectors = refs[:4]
    early = refs[4:count]
    own, mate, out, lower, upper = refs[count:]
    s = lax.axis_index("slab")
    active = s % (2 * spacing) == spacing
    first = s % (4 * spacing) == spacing
    linked = s + spacing < slabs

    def pick(n, wanted):
        values = vectors[n][...]
        return jnp.where(wanted, early[n][...], values) if n < len(early) else values

    @pl.when(active)
    def _():
        load_vector(lower, pick(0, first), pick(1, first))
        out[...] = part[...] - complex_product(own[6:8], mate[6:8], lower)

    @pl.when(active & linked)
    def _():
        second = jnp.logical_not(first)
        load_vector(upper, pick(2, second), pick(3, second))
        out[...] -= complex_product(own[8:10], mate[8:10], upper)

    @pl.when(jnp.logical_not(active))
    def _():
        out[...] = other[...]


def copy_kernel(values, *refs):
    refs[-1][...] = values[...]


def call(
    kernel,
    *operands,
    outs=1,
    scratch=(),
    unused=(),
    shape=jax.ShapeDtypeStruct((Q, LANES), wide),
    flops=10**9,
):
    vmem = pl.BlockSpec(memory_space=pltpu.VMEM)
    return pl.pallas_call(
        kernel,
        out_shape=shape if outs == 1 else (shape,) * outs,
        in_specs=[vmem] * len(operands) + [pl.BlockSpec(memory_space=pl.ANY)] * len(unused),
        out_specs=vmem if outs == 1 else (vmem,) * outs,
        scratch_shapes=list(scratch),
        cost_estimate=pl.CostEstimate(flops=flops, bytes_accessed=1, transcendentals=0),
        compiler_params=pltpu.CompilerParams(vmem_limit_bytes=16 * 2**20),
    )(*operands, *unused)


def completed(route, count, cols):
    target = dict(route)
    taken = set(target.values())
    for a in [a for a in range(count) if a not in target and a not in taken]:
        target[a] = a ^ 1
        taken.add(a ^ 1)
    for a in range(count):
        if a not in target:
            target[a] = next(b for b in range(count) if b not in taken and b % cols == a % cols)
            taken.add(target[a])
    if sorted(target.values()) != list(range(count)):
        raise ValueError("no permutation")
    return sorted(target.items())


def per_device(slabs, cols, waves, energy, tunnel, pivots, below, above, back_lower, back_upper):
    everyone = range(cols)
    width = energy.shape[2]
    store = pltpu.VMEM((width, LANES), short)
    levels = slabs.bit_length() - 1
    every = range(slabs)

    def send(values, moves, flip=0):
        route = []
        for c in everyone:
            for a, b, *h in moves:
                route.append((a * cols + c, b * cols + (c ^ flip)))
                here = b * cols + (c ^ flip)
                for h in h:
                    route.append((here, h * cols + c))
                    here = h * cols + c
                if here != b * cols + (c ^ flip):
                    route.append((here, a * cols + c))
        return lax.ppermute(values, ("slab", "col"), completed(route, slabs * cols, cols))

    def both(values, near_moves, far_moves):
        return send(values, near_moves), send(values, far_moves, 2)

    def swap(values):
        return send(values, [(a, a) for a in every], 1)

    def exchange(values, chosen=every):
        return send(values, [(a, a) for a in chosen], 2)

    def kernel(body, *arguments):
        return functools.partial(body, *arguments)

    def stack(*arrays, after):
        depth = sum(v.shape[0] for v in arrays)
        shape = jax.ShapeDtypeStruct((depth, Q, width), wide)
        return call(stack_kernel, *arrays, unused=(after,), shape=shape, flops=1)

    mate_waves = swap(waves)
    t_pair = tunnel, swap(tunnel)
    e_pair = energy, swap(energy)
    side = call(side_kernel, shape=jax.ShapeDtypeStruct((8, LANES), jnp.int32))
    psi, up_near, up_far = call(
        open_kernel, waves, mate_waves, side, *t_pair, outs=3, scratch=[pltpu.VMEM((64, width), wide)]
    )
    up, crossing = call(cross_kernel, psi, up_near, exchange(up_far), outs=2)
    psi_far = exchange(psi)
    between = [(a, b) for k in every[1:-1:2] for a, b in ((k, k + 1), (k + 1, k))]
    stepped = send(crossing, [(a, a ^ 1) for a in every])
    rest = call(
        kernel(ham_kernel, slabs),
        psi,
        psi_far,
        *both(psi, between, between),
        *e_pair,
        *t_pair,
        scratch=[store, store],
        unused=(up,),
    )
    near, crossing = call(near_kernel, rest, stepped, outs=2)
    far = exchange(crossing)
    blocks = below[0], above[0], pivots[0], back_lower[0], back_upper[0]
    front = stack(*blocks, after=near)
    front = front, swap(front)
    back = front
    base = call(even_kernel, rest, stepped, far, *t_pair, scratch=[store])

    pivot = near
    for level in range(levels):
        d = 2**level
        if level == levels - 1:
            beneath = call(kernel(top_kernel, d), near, far, *front, scratch=[store])
            shares = both(beneath, [(d, 0, 1, d + 1)], [(d, 0, 1, d + 1)])
            if level > 1:
                shares = shares + late
            pivot = call(kernel(pivot_kernel, d), near, far, *back, pivot, scratch=[store])
            pivot = call(
                kernel(root_kernel, len(shares) // 2),
                base,
                base_far,
                *shares,
                *back,
                pivot,
                scratch=[store],
            )
            break
        urgent = [b for b in every if b % (4 * d) == 2 * d]
        patient = [b for b in every if b % (4 * d) == 0]
        beneath, over = call(
            kernel(level_kernel, d),
            near,
            far,
            *front,
            up if level == 0 else jnp.zeros_like(up),
            outs=2,
            scratch=[store],
            unused=(base,) if level == 1 else (),
        )
        if level == 0:
            more = send(over, [(b - 1, b, b - 2) for b in urgent])
            less = send(beneath, [(b + 1, b, b - 2) for b in urgent])
            pivot = call(
                kernel(pivot_kernel, d),
                near,
                far,
                *back,
                pivot,
                scratch=[store],
                unused=(over,),
                flops=1,
            )
            held = call(copy_kernel, beneath, unused=(pivot,), flops=1)
            late = [send(held, [(b + 1, b, b + 3) for b in patient])]
            if len(patient) > 1:
                held = call(copy_kernel, over, unused=(pivot,), flops=1)
                ways = [(b - 1, b, b + 1 if b + 4 < slabs else b + 3) for b in patient if b > 0]
                late.append(send(held, ways))
            near = call(urgent_kernel, base, more, less)
            far = exchange(near, urgent)
            base = call(kernel(reduce_kernel, d, len(late)), base, *late, unused=(near,))
            base_far = exchange(base, patient)
            continue
        more = both(over, [(b - d, b, b - 1) for b in urgent], [(b - d, b, b - 3) for b in urgent])
        less = both(
            beneath, [(b + d, b, b + 1) for b in urgent], [(b + d, b, b + 3) for b in urgent]
        )
        pivot = call(kernel(pivot_kernel, d), near, far, *back, pivot, scratch=[store])
        if level > 1:
            count = len(late) // 2
            base = call(kernel(reduce_kernel, d // 2, count), base, *late[::2], unused=(beneath,))
            base_far = call(
                kernel(reduce_kernel, d // 2, count), base_far, *late[1::2], unused=(beneath,)
            )
        near = base - more[0] - less[0]
        far = base_far - more[1] - less[1]
        held = call(copy_kernel, beneath, unused=(more[0],))
        late = both(
            held, [(b + d, b, b + d + 1) for b in patient], [(b + d, b, b + d + 3) for b in patient]
        )
        if len(patient) > 1:
            held = call(copy_kernel, over, unused=(more[0],))
            late = late + both(
                held,
                [(b - d, b, b - d + 1) for b in patient if b > 0],
                [(b - d, b, b - d + 3) for b in patient if b > 0],
            )

    solved = pivot
    for level in reversed(range(levels)):
        d = 2**level
        sources = [a for a in every if a % (2 * d) == 0]
        upper = [a for a in sources if a > 0]
        if d == 1:
            low_near = send(solved, [(a, a ^ 1) for a in every])
            ways = [(a, a - 1) for a in upper] + [(a - 1, a) for a in upper]
            up_near = send(solved, ways)
            up_far = send(solved, ways, 2)
            low_far = exchange(low_near, [a + 1 for a in sources])
            vectors = low_near, low_far, up_near, up_far
        elif level == levels - 1:
            vectors = both(solved, [(0, d, d + 1, 1)], [(0, d, d + 1, 1)])
        else:
            sources = [a for a in every if a % (4 * d) == 2 * d]
            ways = [(a, a - d, a - d + 1, a + 1) for a in sources]
            up_near, up_far = both(solved, ways, ways)
            ways = [(a, a + d, a + d + 1, a + 1) for a in sources]
            low_near, low_far = both(solved, ways, ways)
            vectors = (low_near, low_far, up_near, up_far) + early
        if level > 1:
            half = d // 2
            sources = [a for a in every if a % (2 * d) == 0]
            ways = [(a, a + half, a + half + 1, a + 1) for a in sources]
            early = both(solved, ways, ways)
            if len(sources) > 1:
                ways = [(a, a - half, a - half + 1, a + 1) for a in sources if a > 0]
                early += both(solved, ways, ways)
        if level == levels - 1 and levels > 1:
            solved = call(kernel(settle_kernel, d), pivot, *vectors, *back, scratch=[store])
        else:
            solved = call(
                kernel(both_kernel, slabs, d, len(vectors)),
                pivot,
                solved,
                *vectors,
                *back,
                scratch=[store, store],
            )
    out = call(regroup_kernel, solved, swap(solved))
    return out[None]


def solution(mesh):
    slabs, cols = mesh.shape["slab"], mesh.shape["col"]
    vector = P("slab", "col", None)
    block = P("slab", None, "col", None)
    return jax.shard_map(
        functools.partial(per_device, slabs, cols),
        mesh=mesh,
        in_specs=(vector,) * 3 + (block,) * 5,
        out_specs=vector,
        check_vma=False,
    )
```

```python
import functools

import jax
import jax.numpy as jnp
from jax import lax
from jax.experimental import pallas as pl
from jax.experimental.pallas import tpu as pltpu
from jax.sharding import PartitionSpec as P


half_step = 0.5
wide = jnp.float32
short = jnp.bfloat16
Q = 128
LANES = 128


def lanes(values):
    return lax.broadcasted_iota(jnp.int32, values.shape, 1)


def swap_halves(values):
    return pltpu.roll(values, 64, 1)


def join(left, right):
    return jnp.where(lanes(left) < 64, left, right)


def rotate(values):
    even = lanes(values) % 2 == 0
    return jnp.where(even, -pltpu.roll(values, LANES - 1, 1), pltpu.roll(values, 1, 1))


def split(values):
    high = values.astype(short)
    return high, (values - high.astype(wide)).astype(short)


def quarter(number):
    return pl.ds(pl.multiple_of(number * Q, Q), Q)


def spread(store, packed, first):
    high = packed.astype(short).astype(wide)
    low = packed - high
    store[quarter(first), :] = join(high, swap_halves(low)).astype(short)
    store[quarter(first ^ 1), :] = join(swap_halves(high), low).astype(short)


def load_vector(store, near, far):
    c = lax.axis_index("col")
    spread(store, near, c)
    spread(store, far, c ^ 2)


def keep(wanted, values):
    return jnp.where(wanted, values[...], 0.0)


def rows_product(block, store):
    high, low = split(block)
    vector = store[...]
    return jnp.dot(high, vector, preferred_element_type=wide) + jnp.dot(
        low, vector, preferred_element_type=wide
    )


def fold(values):
    return values + swap_halves(values)


def real_product(own, mate, store):
    return join(fold(rows_product(own, store)), fold(rows_product(mate, store)))


def complex_half(block, store):
    both = rows_product(block.reshape(2 * Q, block.shape[-1]), store)
    return fold(both[:Q] + rotate(both[Q:]))


def complex_product(own, mate, store):
    return join(complex_half(own, store), complex_half(mate, store))


def this_core(left, right):
    first = lax.axis_index("col") % 2 == 0
    return jnp.where(first, join(left, swap_halves(right)), join(swap_halves(left), right))


def side_kernel(side):
    side[...] = jnp.zeros_like(side) + lax.axis_index("col")


def regroup_kernel(mine, other, out):
    rows = join(mine[...], other[...])
    out[...] = jnp.where(lax.axis_index("col") % 2 == 0, rows, swap_halves(rows))


def stack_kernel(*refs):
    *sources, _, out = refs
    place = 0
    for source in sources:
        depth = source.shape[0]
        out[place : place + depth] = source[...]
        place += depth


def open_kernel(mine, other, side, own, mate, psi, near, far, store):
    c = lax.axis_index("col")
    packed = this_core(mine[0], other[0])
    psi[...] = packed
    turned = packed.T
    total = None
    for rows, block in ((turned[:64], own[0]), (turned[64:], mate[0])):
        high, low = split(rows)
        pair = jnp.concatenate([high, low], axis=0)
        block_high, block_low = split(block)
        part = jnp.dot(pair, block_high, preferred_element_type=wide) + jnp.dot(
            pair, block_low, preferred_element_type=wide
        )
        part = part[:64] + part[64:]
        total = part if total is None else total + part
    store[...] = total
    for out, first in ((far, c ^ 2), (near, c)):
        pair = jnp.concatenate(
            [store[:, quarter(first)], store[:, quarter(first ^ 1)]], axis=0
        )
        out[...] = half_step * rotate(pair.T)


def cross_kernel(packed, near, other, up, crossing):
    whole = near[...] + other[...]
    up[...] = whole
    crossing[...] = jnp.where(lax.axis_index("slab") % 2 == 1, packed[...], whole)


def near_kernel(rest, stepped, near, crossing):
    whole = rest[...] - stepped[...]
    near[...] = whole
    crossing[...] = jnp.where(lax.axis_index("slab") % 2 == 1, whole, stepped[...])


def urgent_kernel(base, more, less, out):
    kept = lax.axis_index("slab") % 4 == 2
    out[...] = base[...] - keep(kept, more) - keep(kept, less)


def reduce_kernel(spacing, count, base, *refs):
    out = refs[-1]
    less, *more = refs[:count]
    s = lax.axis_index("slab")
    kept = s % (4 * spacing) == 0
    values = base[...] - keep(kept, less)
    for late in more:
        values = values - keep(kept & (s > 0), late)
    out[...] = values


def ham_kernel(slabs, near, far, next_near, next_far, own_e, mate_e, own_t, mate_t, *refs):
    out, here, there = refs[-3:]
    s = lax.axis_index("slab")
    load_vector(here, near[...], far[...])
    out[...] = near[...] - half_step * rotate(real_product(own_e[0], mate_e[0], here))

    @pl.when((s % 2 == 1) & (s < slabs - 1))
    def _():
        load_vector(there, next_near[...], next_far[...])
        out[...] -= half_step * rotate(real_product(own_t[0], mate_t[0], there))


def even_kernel(rest, next_near, next_far, own, mate, out, store):
    @pl.when(lax.axis_index("slab") % 2 == 0)
    def _():
        load_vector(store, next_near[...], next_far[...])
        out[...] = rest[...] - half_step * rotate(real_product(own[0], mate[0], store))


def level_kernel(spacing, near, far, own, mate, tail, *refs):
    beneath, above, store = refs[-3:]

    @pl.when(lax.axis_index("slab") % (2 * spacing) == spacing)
    def _():
        load_vector(store, near[...], far[...])
        above[...] = complex_product(own[2:4], mate[2:4], store) + tail[...]
        beneath[...] = complex_product(own[0:2], mate[0:2], store)


def top_kernel(spacing, near, far, own, mate, *refs):
    beneath, store = refs[-2:]

    @pl.when(lax.axis_index("slab") % (2 * spacing) == spacing)
    def _():
        load_vector(store, near[...], far[...])
        beneath[...] = complex_product(own[0:2], mate[0:2], store)


def pivot_kernel(spacing, near, far, own, mate, before, *refs):
    out, store = refs[-2:]
    active = lax.axis_index("slab") % (2 * spacing) == spacing

    @pl.when(active)
    def _():
        load_vector(store, near[...], far[...])
        out[...] = complex_product(own[4:6], mate[4:6], store)

    @pl.when(jnp.logical_not(active))
    def _():
        out[...] = before[...]


def root_kernel(count, *refs):
    near, far = refs[:2]
    shares = refs[2 : 2 + 2 * count]
    own, mate, before, out, store = refs[2 + 2 * count :]
    root = lax.axis_index("slab") == 0

    @pl.when(root)
    def _():
        whole = [near[...], far[...]]
        for n, share in enumerate(shares):
            whole[n % 2] = whole[n % 2] - share[...]
        load_vector(store, *whole)
        out[...] = complex_product(own[4:6], mate[4:6], store)

    @pl.when(jnp.logical_not(root))
    def _():
        out[...] = before[...]


def settle_kernel(spacing, part, near, far, own, mate, out, store):
    active = lax.axis_index("slab") % (2 * spacing) == spacing

    @pl.when(active)
    def _():
        load_vector(store, near[...], far[...])
        out[...] = part[...] - complex_product(own[6:8], mate[6:8], store)

    @pl.when(jnp.logical_not(active))
    def _():
        out[...] = part[...]


def both_kernel(slabs, spacing, count, part, other, *refs):
    vectors = refs[:4]
    early = refs[4:count]
    own, mate, out, lower, upper = refs[count:]
    s = lax.axis_index("slab")
    active = s % (2 * spacing) == spacing
    first = s % (4 * spacing) == spacing
    linked = s + spacing < slabs

    def pick(n, wanted):
        values = vectors[n][...]
        return jnp.where(wanted, early[n][...], values) if n < len(early) else values

    @pl.when(active)
    def _():
        load_vector(lower, pick(0, first), pick(1, first))
        out[...] = part[...] - complex_product(own[6:8], mate[6:8], lower)

    @pl.when(active & linked)
    def _():
        second = jnp.logical_not(first)
        load_vector(upper, pick(2, second), pick(3, second))
        out[...] -= complex_product(own[8:10], mate[8:10], upper)

    @pl.when(jnp.logical_not(active))
    def _():
        out[...] = other[...]


def copy_kernel(values, *refs):
    refs[-1][...] = values[...]


def call(
    kernel,
    *operands,
    outs=1,
    scratch=(),
    unused=(),
    shape=jax.ShapeDtypeStruct((Q, LANES), wide),
    flops=10**9,
):
    vmem = pl.BlockSpec(memory_space=pltpu.VMEM)
    return pl.pallas_call(
        kernel,
        out_shape=shape if outs == 1 else (shape,) * outs,
        in_specs=[vmem] * len(operands) + [pl.BlockSpec(memory_space=pl.ANY)] * len(unused),
        out_specs=vmem if outs == 1 else (vmem,) * outs,
        scratch_shapes=list(scratch),
        cost_estimate=pl.CostEstimate(flops=flops, bytes_accessed=1, transcendentals=0),
        compiler_params=pltpu.CompilerParams(vmem_limit_bytes=16 * 2**20),
    )(*operands, *unused)


def completed(route, count, cols):
    target = dict(route)
    taken = set(target.values())
    for a in [a for a in range(count) if a not in target and a not in taken]:
        target[a] = a ^ 1
        taken.add(a ^ 1)
    for a in range(count):
        if a not in target:
            target[a] = next(b for b in range(count) if b not in taken and b % cols == a % cols)
            taken.add(target[a])
    if sorted(target.values()) != list(range(count)):
        raise ValueError("no permutation")
    return sorted(target.items())


def per_device(slabs, cols, waves, energy, tunnel, pivots, below, above, back_lower, back_upper):
    everyone = range(cols)
    width = energy.shape[2]
    store = pltpu.VMEM((width, LANES), short)
    levels = slabs.bit_length() - 1
    every = range(slabs)

    def send(values, moves, flip=0):
        route = []
        for c in everyone:
            for a, b, *h in moves:
                route.append((a * cols + c, b * cols + (c ^ flip)))
                here = b * cols + (c ^ flip)
                for h in h:
                    route.append((here, h * cols + c))
                    here = h * cols + c
                if here != b * cols + (c ^ flip):
                    route.append((here, a * cols + c))
        return lax.ppermute(values, ("slab", "col"), completed(route, slabs * cols, cols))

    def both(values, near_moves, far_moves):
        return send(values, near_moves), send(values, far_moves, 2)

    def swap(values):
        return send(values, [(a, a) for a in every], 1)

    def exchange(values, chosen=every):
        return send(values, [(a, a) for a in chosen], 2)

    def kernel(body, *arguments):
        return functools.partial(body, *arguments)

    def stack(*arrays, after):
        depth = sum(v.shape[0] for v in arrays)
        shape = jax.ShapeDtypeStruct((depth, Q, width), wide)
        return call(stack_kernel, *arrays, unused=(after,), shape=shape, flops=1)

    mate_waves = swap(waves)
    t_pair = tunnel, swap(tunnel)
    e_pair = energy, swap(energy)
    side = call(side_kernel, shape=jax.ShapeDtypeStruct((8, LANES), jnp.int32))
    psi, up_near, up_far = call(
        open_kernel, waves, mate_waves, side, *t_pair, outs=3, scratch=[pltpu.VMEM((64, width), wide)]
    )
    up, crossing = call(cross_kernel, psi, up_near, exchange(up_far), outs=2, flops=1)
    psi_far = exchange(psi)
    between = [(a, b) for k in every[1:-1:2] for a, b in ((k, k + 1), (k + 1, k))]
    stepped = send(crossing, [(a, a ^ 1) for a in every])
    rest = call(
        kernel(ham_kernel, slabs),
        psi,
        psi_far,
        *both(psi, between, between),
        *e_pair,
        *t_pair,
        scratch=[store, store],
        unused=(up,),
    )
    near, crossing = call(near_kernel, rest, stepped, outs=2, flops=1)
    far = exchange(crossing)
    blocks = below[0], above[0], pivots[0], back_lower[0], back_upper[0]
    front = stack(*blocks, after=near)
    front = front, swap(front)
    back = front
    base = call(even_kernel, rest, stepped, far, *t_pair, scratch=[store])

    pivot = near
    for level in range(levels):
        d = 2**level
        if level == levels - 1:
            beneath = call(kernel(top_kernel, d), near, far, *front, scratch=[store])
            shares = both(beneath, [(d, 0, 1, d - 1)], [(d, 0, 1, d + 3)])
            if level > 1:
                shares = shares + late
            pivot = call(kernel(pivot_kernel, d), near, far, *back, pivot, scratch=[store])
            pivot = call(
                kernel(root_kernel, len(shares) // 2),
                base,
                base_far,
                *shares,
                *back,
                pivot,
                scratch=[store],
            )
            break
        urgent = [b for b in every if b % (4 * d) == 2 * d]
        patient = [b for b in every if b % (4 * d) == 0]
        beneath, over = call(
            kernel(level_kernel, d),
            near,
            far,
            *front,
            up if level == 0 else jnp.zeros_like(up),
            outs=2,
            scratch=[store],
            unused=(base,) if level == 1 else (),
        )
        if level == 0:
            more = send(over, [(a, b) for k in urgent for a, b in ((k - 1, k), (k, k - 1))])
            less = send(beneath, [(b + 1, b, b - 2) for b in urgent])
            pivot = call(
                kernel(pivot_kernel, d),
                near,
                far,
                *back,
                pivot,
                scratch=[store],
                unused=(over,),
                flops=1,
            )
            held = call(copy_kernel, beneath, unused=(pivot,), flops=1)
            late = [send(held, [(b + 1, b, b + 3) for b in patient])]
            if len(patient) > 1:
                held = call(copy_kernel, over, unused=(pivot,), flops=1)
                ways = [(b - 1, b, b + 1 if b + 4 < slabs else b + 3) for b in patient if b > 0]
                late.append(send(held, ways))
            near = call(urgent_kernel, base, more, less)
            far = exchange(near, urgent)
            base = call(kernel(reduce_kernel, d, len(late)), base, *late, unused=(near,))
            base_far = exchange(base, patient)
            continue
        more = both(over, [(b - d, b, b - 1) for b in urgent], [(b - d, b, b - 3) for b in urgent])
        less = both(
            beneath, [(b + d, b, b + 1) for b in urgent], [(b + d, b, b + 3) for b in urgent]
        )
        pivot = call(kernel(pivot_kernel, d), near, far, *back, pivot, scratch=[store])
        if level > 1:
            count = len(late) // 2
            base = call(kernel(reduce_kernel, d // 2, count), base, *late[::2], unused=(beneath,))
            base_far = call(
                kernel(reduce_kernel, d // 2, count), base_far, *late[1::2], unused=(beneath,)
            )
        near = base - more[0] - less[0]
        far = base_far - more[1] - less[1]
        held = call(copy_kernel, beneath, unused=(more[0],))
        ways = [(b + d, b, b + 1, b + d + 1) for b in patient]
        late = both(held, ways, ways)
        if len(patient) > 1:
            held = call(copy_kernel, over, unused=(more[0],))
            late = late + both(
                held,
                [(b - d, b, b - d + 1) for b in patient if b > 0],
                [(b - d, b, b - d + 3) for b in patient if b > 0],
            )

    solved = pivot
    for level in reversed(range(levels)):
        d = 2**level
        sources = [a for a in every if a % (2 * d) == 0]
        upper = [a for a in sources if a > 0]
        if d == 1:
            low_near = send(solved, [(a, a ^ 1) for a in every])
            ways = [(a, a - 1) for a in upper] + [(a - 1, a) for a in upper]
            up_near = send(solved, ways)
            up_far = send(solved, ways, 2)
            low_far = exchange(low_near, [a + 1 for a in sources])
            vectors = low_near, low_far, up_near, up_far
        elif level == levels - 1:
            vectors = both(solved, [(0, d, d + 1, 1)], [(0, d, d + 1, 1)])
        else:
            sources = [a for a in every if a % (4 * d) == 2 * d]
            up_near = send(solved, [(a, a - d, a - d + 1, a + 1) for a in sources])
            last = -3 if d == 2 else 3
            up_far = send(solved, [(a, a - d, a - d + 1, a + last) for a in sources], 2)
            low_far = send(solved, [(a, a + d, a + d + 1, a - 1) for a in sources], 2)
            low_near = send(solved, [(a, a + d, a + d + 1) for a in sources])
            vectors = (low_near, low_far, up_near, up_far) + early
        if level > 1:
            half = d // 2
            sources = [a for a in every if a % (2 * d) == 0]
            ways = [(a, a + half, a + half + 1, a + 1) for a in sources]
            early = both(solved, ways, ways)
            if len(sources) > 1:
                ways = [(a, a - half, a - half + 1, a + 1) for a in sources if a > 0]
                early += both(solved, ways, ways)
        if level == levels - 1 and levels > 1:
            solved = call(kernel(settle_kernel, d), pivot, *vectors, *back, scratch=[store])
        else:
            solved = call(
                kernel(both_kernel, slabs, d, len(vectors)),
                pivot,
                solved,
                *vectors,
                *back,
                scratch=[store, store],
            )
    out = call(regroup_kernel, solved, swap(solved))
    return out[None]


def solution(mesh):
    slabs, cols = mesh.shape["slab"], mesh.shape["col"]
    vector = P("slab", "col", None)
    block = P("slab", None, "col", None)
    return jax.shard_map(
        functools.partial(per_device, slabs, cols),
        mesh=mesh,
        in_specs=(vector,) * 3 + (block,) * 5,
        out_specs=vector,
        check_vma=False,
    )
```

```python
import functools

import jax
import jax.numpy as jnp
from jax import lax
from jax.experimental import pallas as pl
from jax.experimental.pallas import tpu as pltpu
from jax.sharding import PartitionSpec as P


half_step = 0.5
wide = jnp.float32
short = jnp.bfloat16
Q = 128
LANES = 128


def lanes(values):
    return lax.broadcasted_iota(jnp.int32, values.shape, 1)


def swap_halves(values):
    return pltpu.roll(values, 64, 1)


def join(left, right):
    return jnp.where(lanes(left) < 64, left, right)


def rotate(values):
    even = lanes(values) % 2 == 0
    return jnp.where(even, -pltpu.roll(values, LANES - 1, 1), pltpu.roll(values, 1, 1))


def split(values):
    high = values.astype(short)
    return high, (values - high.astype(wide)).astype(short)


def quarter(number):
    return pl.ds(pl.multiple_of(number * Q, Q), Q)


def spread(store, packed, first):
    high = packed.astype(short).astype(wide)
    low = packed - high
    store[quarter(first), :] = join(high, swap_halves(low)).astype(short)
    store[quarter(first ^ 1), :] = join(swap_halves(high), low).astype(short)


def load_vector(store, near, far):
    c = lax.axis_index("col")
    spread(store, near, c)
    spread(store, far, c ^ 2)


def keep(wanted, values):
    return jnp.where(wanted, values[...], 0.0)


def rows_product(block, store):
    high, low = split(block)
    vector = store[...]
    return jnp.dot(high, vector, preferred_element_type=wide) + jnp.dot(
        low, vector, preferred_element_type=wide
    )


def fold(values):
    return values + swap_halves(values)


def real_product(own, mate, store):
    return join(fold(rows_product(own, store)), fold(rows_product(mate, store)))


def complex_half(block, store):
    both = rows_product(block.reshape(2 * Q, block.shape[-1]), store)
    return fold(both[:Q] + rotate(both[Q:]))


def complex_product(own, mate, store):
    return join(complex_half(own, store), complex_half(mate, store))


def this_core(left, right):
    first = lax.axis_index("col") % 2 == 0
    return jnp.where(first, join(left, swap_halves(right)), join(swap_halves(left), right))


def side_kernel(side):
    side[...] = jnp.zeros_like(side) + lax.axis_index("col")


def regroup_kernel(mine, other, out):
    rows = join(mine[...], other[...])
    out[...] = jnp.where(lax.axis_index("col") % 2 == 0, rows, swap_halves(rows))


def stack_kernel(*refs):
    *sources, _, out = refs
    place = 0
    for source in sources:
        depth = source.shape[0]
        out[place : place + depth] = source[...]
        place += depth


def open_kernel(mine, other, side, own, mate, psi, near, far, store):
    c = lax.axis_index("col")
    packed = this_core(mine[0], other[0])
    psi[...] = packed
    turned = packed.T
    total = None
    for rows, block in ((turned[:64], own[0]), (turned[64:], mate[0])):
        high, low = split(rows)
        pair = jnp.concatenate([high, low], axis=0)
        block_high, block_low = split(block)
        part = jnp.dot(pair, block_high, preferred_element_type=wide) + jnp.dot(
            pair, block_low, preferred_element_type=wide
        )
        part = part[:64] + part[64:]
        total = part if total is None else total + part
    store[...] = total
    for out, first in ((far, c ^ 2), (near, c)):
        pair = jnp.concatenate(
            [store[:, quarter(first)], store[:, quarter(first ^ 1)]], axis=0
        )
        out[...] = half_step * rotate(pair.T)


def cross_kernel(packed, near, other, up, crossing):
    whole = near[...] + other[...]
    up[...] = whole
    crossing[...] = jnp.where(lax.axis_index("slab") % 2 == 1, packed[...], whole)


def near_kernel(rest, stepped, near, crossing):
    whole = rest[...] - stepped[...]
    near[...] = whole
    crossing[...] = jnp.where(lax.axis_index("slab") % 2 == 1, whole, stepped[...])


def even_slabs_kernel(base, more, less, out):
    s = lax.axis_index("slab")
    even = s % 2 == 0
    out[...] = base[...] - keep(even & (s > 0), more) - keep(even, less)


def reduce_kernel(spacing, count, base, *refs):
    out = refs[-1]
    less, *more = refs[:count]
    s = lax.axis_index("slab")
    kept = s % (4 * spacing) == 0
    values = base[...] - keep(kept, less)
    for late in more:
        values = values - keep(kept & (s > 0), late)
    out[...] = values


def ham_kernel(slabs, near, far, next_near, next_far, own_e, mate_e, own_t, mate_t, *refs):
    out, here, there = refs[-3:]
    s = lax.axis_index("slab")
    load_vector(here, near[...], far[...])
    out[...] = near[...] - half_step * rotate(real_product(own_e[0], mate_e[0], here))

    @pl.when((s % 2 == 1) & (s < slabs - 1))
    def _():
        load_vector(there, next_near[...], next_far[...])
        out[...] -= half_step * rotate(real_product(own_t[0], mate_t[0], there))


def even_kernel(rest, next_near, next_far, own, mate, out, store):
    @pl.when(lax.axis_index("slab") % 2 == 0)
    def _():
        load_vector(store, next_near[...], next_far[...])
        out[...] = rest[...] - half_step * rotate(real_product(own[0], mate[0], store))


def level_kernel(spacing, near, far, own, mate, tail, *refs):
    beneath, above, store = refs[-3:]

    @pl.when(lax.axis_index("slab") % (2 * spacing) == spacing)
    def _():
        load_vector(store, near[...], far[...])
        above[...] = complex_product(own[2:4], mate[2:4], store) + tail[...]
        beneath[...] = complex_product(own[0:2], mate[0:2], store)


def top_kernel(spacing, near, far, own, mate, *refs):
    beneath, store = refs[-2:]

    @pl.when(lax.axis_index("slab") % (2 * spacing) == spacing)
    def _():
        load_vector(store, near[...], far[...])
        beneath[...] = complex_product(own[0:2], mate[0:2], store)


def pivot_kernel(spacing, near, far, own, mate, before, *refs):
    out, store = refs[-2:]
    active = lax.axis_index("slab") % (2 * spacing) == spacing

    @pl.when(active)
    def _():
        load_vector(store, near[...], far[...])
        out[...] = complex_product(own[4:6], mate[4:6], store)

    @pl.when(jnp.logical_not(active))
    def _():
        out[...] = before[...]


def root_kernel(count, *refs):
    near, far = refs[:2]
    shares = refs[2 : 2 + 2 * count]
    own, mate, before, out, store = refs[2 + 2 * count :]
    root = lax.axis_index("slab") == 0

    @pl.when(root)
    def _():
        whole = [near[...], far[...]]
        for n, share in enumerate(shares):
            whole[n % 2] = whole[n % 2] - share[...]
        load_vector(store, *whole)
        out[...] = complex_product(own[4:6], mate[4:6], store)

    @pl.when(jnp.logical_not(root))
    def _():
        out[...] = before[...]


def settle_kernel(spacing, part, near, far, own, mate, out, store):
    active = lax.axis_index("slab") % (2 * spacing) == spacing

    @pl.when(active)
    def _():
        load_vector(store, near[...], far[...])
        out[...] = part[...] - complex_product(own[6:8], mate[6:8], store)

    @pl.when(jnp.logical_not(active))
    def _():
        out[...] = part[...]


def both_kernel(slabs, spacing, count, part, other, *refs):
    vectors = refs[:4]
    early = refs[4:count]
    own, mate, out, lower, upper = refs[count:]
    s = lax.axis_index("slab")
    active = s % (2 * spacing) == spacing
    first = s % (4 * spacing) == spacing
    linked = s + spacing < slabs

    def pick(n, wanted):
        values = vectors[n][...]
        return jnp.where(wanted, early[n][...], values) if n < len(early) else values

    @pl.when(active)
    def _():
        load_vector(lower, pick(0, first), pick(1, first))
        out[...] = part[...] - complex_product(own[6:8], mate[6:8], lower)

    @pl.when(active & linked)
    def _():
        second = jnp.logical_not(first)
        load_vector(upper, pick(2, second), pick(3, second))
        out[...] -= complex_product(own[8:10], mate[8:10], upper)

    @pl.when(jnp.logical_not(active))
    def _():
        out[...] = other[...]


def copy_kernel(values, *refs):
    refs[-1][...] = values[...]


def call(
    kernel,
    *operands,
    outs=1,
    scratch=(),
    unused=(),
    shape=jax.ShapeDtypeStruct((Q, LANES), wide),
    flops=10**9,
):
    vmem = pl.BlockSpec(memory_space=pltpu.VMEM)
    return pl.pallas_call(
        kernel,
        out_shape=shape if outs == 1 else (shape,) * outs,
        in_specs=[vmem] * len(operands) + [pl.BlockSpec(memory_space=pl.ANY)] * len(unused),
        out_specs=vmem if outs == 1 else (vmem,) * outs,
        scratch_shapes=list(scratch),
        cost_estimate=pl.CostEstimate(flops=flops, bytes_accessed=1, transcendentals=0),
        compiler_params=pltpu.CompilerParams(vmem_limit_bytes=16 * 2**20),
    )(*operands, *unused)


def completed(route, count, cols):
    target = dict(route)
    taken = set(target.values())
    for a in [a for a in range(count) if a not in target and a not in taken]:
        target[a] = a ^ 1
        taken.add(a ^ 1)
    for a in range(count):
        if a not in target:
            target[a] = next(b for b in range(count) if b not in taken and b % cols == a % cols)
            taken.add(target[a])
    if sorted(target.values()) != list(range(count)):
        raise ValueError("no permutation")
    return sorted(target.items())


def per_device(slabs, cols, waves, energy, tunnel, pivots, below, above, back_lower, back_upper):
    everyone = range(cols)
    width = energy.shape[2]
    store = pltpu.VMEM((width, LANES), short)
    levels = slabs.bit_length() - 1
    every = range(slabs)

    def send(values, moves, flip=0):
        route = []
        for c in everyone:
            for a, b, *h in moves:
                route.append((a * cols + c, b * cols + (c ^ flip)))
                here = b * cols + (c ^ flip)
                for h in h:
                    route.append((here, h * cols + c))
                    here = h * cols + c
                if here != b * cols + (c ^ flip):
                    route.append((here, a * cols + c))
        return lax.ppermute(values, ("slab", "col"), completed(route, slabs * cols, cols))

    def both(values, near_moves, far_moves):
        return send(values, near_moves), send(values, far_moves, 2)

    def swap(values):
        return send(values, [(a, a) for a in every], 1)

    def exchange(values, chosen=every):
        return send(values, [(a, a) for a in chosen], 2)

    def kernel(body, *arguments):
        return functools.partial(body, *arguments)

    def stack(*arrays, after):
        depth = sum(v.shape[0] for v in arrays)
        shape = jax.ShapeDtypeStruct((depth, Q, width), wide)
        return call(stack_kernel, *arrays, unused=(after,), shape=shape, flops=1)

    mate_waves = swap(waves)
    t_pair = tunnel, swap(tunnel)
    e_pair = energy, swap(energy)
    side = call(side_kernel, shape=jax.ShapeDtypeStruct((8, LANES), jnp.int32))
    psi, up_near, up_far = call(
        open_kernel, waves, mate_waves, side, *t_pair, outs=3, scratch=[pltpu.VMEM((64, width), wide)]
    )
    up, crossing = call(cross_kernel, psi, up_near, exchange(up_far), outs=2, flops=1)
    psi_far = exchange(psi)
    between = [(a, b) for k in every[1:-1:2] for a, b in ((k, k + 1), (k + 1, k))]
    stepped = send(crossing, [(a, a ^ 1) for a in every])
    rest = call(
        kernel(ham_kernel, slabs),
        psi,
        psi_far,
        *both(psi, between, between),
        *e_pair,
        *t_pair,
        scratch=[store, store],
        unused=(up,),
    )
    near, crossing = call(near_kernel, rest, stepped, outs=2, flops=1)
    far = exchange(crossing)
    blocks = below[0], above[0], pivots[0], back_lower[0], back_upper[0]
    front = stack(*blocks, after=near)
    front = front, swap(front)
    back = front
    base = call(even_kernel, rest, stepped, far, *t_pair, scratch=[store])

    pivot = near
    for level in range(levels):
        d = 2**level
        if level == levels - 1:
            beneath = call(kernel(top_kernel, d), near, far, *front, scratch=[store])
            shares = both(beneath, [(d, 0, 1, d + 1)], [(d, 0, 1, d - 1)])
            if level > 1:
                shares = shares + late
            pivot = call(kernel(pivot_kernel, d), near, far, *back, pivot, scratch=[store])
            pivot = call(
                kernel(root_kernel, len(shares) // 2),
                base,
                base_far,
                *shares,
                *back,
                pivot,
                scratch=[store],
            )
            break
        urgent = [b for b in every if b % (4 * d) == 2 * d]
        patient = [b for b in every if b % (4 * d) == 0]
        beneath, over = call(
            kernel(level_kernel, d),
            near,
            far,
            *front,
            up if level == 0 else jnp.zeros_like(up),
            outs=2,
            scratch=[store],
        )
        if level == 0:
            more = send(over, between)
            less = send(beneath, [(a, a ^ 1) for a in every])
            pivot = call(
                kernel(pivot_kernel, d),
                near,
                far,
                *back,
                pivot,
                scratch=[store],
                unused=(over,),
                flops=1,
            )
            base = near = call(even_slabs_kernel, base, more, less)
            base_far = far = exchange(near, every[::2])
            late = ()
            continue
        more = both(over, [(b - d, b, b - 1) for b in urgent], [(b - d, b, b - 3) for b in urgent])
        less = both(
            beneath, [(b + d, b, b + 1) for b in urgent], [(b + d, b, b + 3) for b in urgent]
        )
        pivot = call(kernel(pivot_kernel, d), near, far, *back, pivot, scratch=[store])
        if late:
            count = len(late) // 2
            base = call(kernel(reduce_kernel, d // 2, count), base, *late[::2], unused=(beneath,))
            base_far = call(
                kernel(reduce_kernel, d // 2, count), base_far, *late[1::2], unused=(beneath,)
            )
        near = base - more[0] - less[0]
        far = base_far - more[1] - less[1]
        held = call(copy_kernel, beneath, unused=(more[0],))
        ways = [(b + d, b, b + 1) for b in patient]
        late = both(held, ways, ways)
        if len(patient) > 1:
            held = call(copy_kernel, over, unused=(more[0],))
            late = late + both(
                held,
                [(b - d, b, b - d + 1) for b in patient if b > 0],
                [(b - d, b, b - d + 3) for b in patient if b > 0],
            )

    solved = pivot
    for level in reversed(range(levels)):
        d = 2**level
        sources = [a for a in every if a % (2 * d) == 0]
        upper = [a for a in sources if a > 0]
        if d == 1:
            low_near = send(solved, [(a, a ^ 1) for a in every])
            ways = [(a, a - 1) for a in upper] + [(a - 1, a) for a in upper]
            up_near = send(solved, ways)
            up_far = send(solved, ways, 2)
            low_far = exchange(low_near, [a + 1 for a in sources])
            vectors = low_near, low_far, up_near, up_far
        elif level == levels - 1:
            vectors = both(solved, [(0, d, d + 1, 1)], [(0, d, d + 1, 1)])
        else:
            sources = [a for a in every if a % (4 * d) == 2 * d]
            up_near = send(solved, [(a, a - d, a - d + 1, a + 1) for a in sources])
            up_far = send(solved, [(a, a - d, a - d + 1, a + 1) for a in sources], 2)
            low_far = send(solved, [(a, a + d, a + d + 1, a - 1) for a in sources], 2)
            low_near = send(solved, [(a, a + d, a + d + 1) for a in sources])
            vectors = (low_near, low_far, up_near, up_far) + early
        if level > 1:
            half = d // 2
            sources = [a for a in every if a % (2 * d) == 0]
            ways = [(a, a + half, a + half + 1, a + 1) for a in sources]
            early = both(solved, ways, ways)
            if len(sources) > 1:
                ways = [(a, a - half, a - half + 1, a + 1) for a in sources if a > 0]
                early += both(solved, ways, ways)
        if level == levels - 1 and levels > 1:
            solved = call(kernel(settle_kernel, d), pivot, *vectors, *back, scratch=[store])
        else:
            solved = call(
                kernel(both_kernel, slabs, d, len(vectors)),
                pivot,
                solved,
                *vectors,
                *back,
                scratch=[store, store],
            )
    out = call(regroup_kernel, solved, swap(solved))
    return out[None]


def solution(mesh):
    slabs, cols = mesh.shape["slab"], mesh.shape["col"]
    vector = P("slab", "col", None)
    block = P("slab", None, "col", None)
    return jax.shard_map(
        functools.partial(per_device, slabs, cols),
        mesh=mesh,
        in_specs=(vector,) * 3 + (block,) * 5,
        out_specs=vector,
        check_vma=False,
    )
```

```python
import functools

import jax
import jax.numpy as jnp
from jax import lax
from jax.experimental import pallas as pl
from jax.experimental.pallas import tpu as pltpu
from jax.sharding import PartitionSpec as P


half_step = 0.5
wide = jnp.float32
short = jnp.bfloat16
Q = 128
LANES = 128


def lanes(values):
    return lax.broadcasted_iota(jnp.int32, values.shape, 1)


def swap_halves(values):
    return pltpu.roll(values, 64, 1)


def join(left, right):
    return jnp.where(lanes(left) < 64, left, right)


def rotate(values):
    even = lanes(values) % 2 == 0
    return jnp.where(even, -pltpu.roll(values, LANES - 1, 1), pltpu.roll(values, 1, 1))


def split(values):
    high = values.astype(short)
    return high, (values - high.astype(wide)).astype(short)


def quarter(number):
    return pl.ds(pl.multiple_of(number * Q, Q), Q)


def spread(store, packed, first):
    high = packed.astype(short).astype(wide)
    low = packed - high
    store[quarter(first), :] = join(high, swap_halves(low)).astype(short)
    store[quarter(first ^ 1), :] = join(swap_halves(high), low).astype(short)


def load_vector(store, near, far):
    c = lax.axis_index("col")
    spread(store, near, c)
    spread(store, far, c ^ 2)


def keep(wanted, values):
    return jnp.where(wanted, values[...], 0.0)


def rows_product(block, store):
    high, low = split(block)
    vector = store[...]
    return jnp.dot(high, vector, preferred_element_type=wide) + jnp.dot(
        low, vector, preferred_element_type=wide
    )


def fold(values):
    return values + swap_halves(values)


def real_product(own, mate, store):
    return join(fold(rows_product(own, store)), fold(rows_product(mate, store)))


def complex_half(block, store):
    both = rows_product(block.reshape(2 * Q, block.shape[-1]), store)
    return fold(both[:Q] + rotate(both[Q:]))


def complex_product(own, mate, store):
    return join(complex_half(own, store), complex_half(mate, store))


def this_core(left, right):
    first = lax.axis_index("col") % 2 == 0
    return jnp.where(first, join(left, swap_halves(right)), join(swap_halves(left), right))


def side_kernel(side):
    side[...] = jnp.zeros_like(side) + lax.axis_index("col")


def regroup_kernel(mine, other, out):
    rows = join(mine[...], other[...])
    out[...] = jnp.where(lax.axis_index("col") % 2 == 0, rows, swap_halves(rows))


def stack_kernel(*refs):
    *sources, _, out = refs
    place = 0
    for source in sources:
        depth = source.shape[0]
        out[place : place + depth] = source[...]
        place += depth


def open_kernel(mine, other, side, own, mate, psi, near, far, store):
    c = lax.axis_index("col")
    packed = this_core(mine[0], other[0])
    psi[...] = packed
    turned = packed.T
    total = None
    for rows, block in ((turned[:64], own[0]), (turned[64:], mate[0])):
        high, low = split(rows)
        pair = jnp.concatenate([high, low], axis=0)
        block_high, block_low = split(block)
        part = jnp.dot(pair, block_high, preferred_element_type=wide) + jnp.dot(
            pair, block_low, preferred_element_type=wide
        )
        part = part[:64] + part[64:]
        total = part if total is None else total + part
    store[...] = total
    for out, first in ((far, c ^ 2), (near, c)):
        pair = jnp.concatenate(
            [store[:, quarter(first)], store[:, quarter(first ^ 1)]], axis=0
        )
        out[...] = half_step * rotate(pair.T)


def cross_kernel(packed, near, other, up, crossing):
    whole = near[...] + other[...]
    up[...] = whole
    crossing[...] = jnp.where(lax.axis_index("slab") % 2 == 1, packed[...], whole)


def near_kernel(rest, stepped, near, crossing):
    whole = rest[...] - stepped[...]
    near[...] = whole
    crossing[...] = jnp.where(lax.axis_index("slab") % 2 == 1, whole, stepped[...])


def even_slabs_kernel(base, more, less, out):
    s = lax.axis_index("slab")
    even = s % 2 == 0
    out[...] = base[...] - keep(even & (s > 0), more) - keep(even, less)


def reduce_kernel(spacing, count, base, *refs):
    out = refs[-1]
    less, *more = refs[:count]
    s = lax.axis_index("slab")
    kept = s % (4 * spacing) == 0
    values = base[...] - keep(kept, less)
    for late in more:
        values = values - keep(kept & (s > 0), late)
    out[...] = values


def ham_kernel(slabs, near, far, next_near, next_far, own_e, mate_e, own_t, mate_t, *refs):
    out, here, there = refs[-3:]
    s = lax.axis_index("slab")
    load_vector(here, near[...], far[...])
    out[...] = near[...] - half_step * rotate(real_product(own_e[0], mate_e[0], here))

    @pl.when((s % 2 == 1) & (s < slabs - 1))
    def _():
        load_vector(there, next_near[...], next_far[...])
        out[...] -= half_step * rotate(real_product(own_t[0], mate_t[0], there))


def even_kernel(rest, next_near, next_far, own, mate, out, store):
    @pl.when(lax.axis_index("slab") % 2 == 0)
    def _():
        load_vector(store, next_near[...], next_far[...])
        out[...] = rest[...] - half_step * rotate(real_product(own[0], mate[0], store))


def level_kernel(spacing, near, far, own, mate, *refs):
    beneath, above, store = refs[-3:]

    @pl.when(lax.axis_index("slab") % (2 * spacing) == spacing)
    def _():
        load_vector(store, near[...], far[...])
        above[...] = complex_product(own[2:4], mate[2:4], store)
        beneath[...] = complex_product(own[0:2], mate[0:2], store)


def over_kernel(spacing, near, far, own, mate, *refs):
    tail, _, out, store = refs

    @pl.when(lax.axis_index("slab") % (2 * spacing) == spacing)
    def _():
        load_vector(store, near[...], far[...])
        out[...] = complex_product(own[2:4], mate[2:4], store) + tail[...]


def top_kernel(spacing, near, far, own, mate, *refs):
    beneath, store = refs[-2:]

    @pl.when(lax.axis_index("slab") % (2 * spacing) == spacing)
    def _():
        load_vector(store, near[...], far[...])
        beneath[...] = complex_product(own[0:2], mate[0:2], store)


def pivot_kernel(spacing, near, far, own, mate, before, *refs):
    out, store = refs[-2:]
    active = lax.axis_index("slab") % (2 * spacing) == spacing

    @pl.when(active)
    def _():
        load_vector(store, near[...], far[...])
        out[...] = complex_product(own[4:6], mate[4:6], store)

    @pl.when(jnp.logical_not(active))
    def _():
        out[...] = before[...]


def root_kernel(count, *refs):
    near, far = refs[:2]
    shares = refs[2 : 2 + 2 * count]
    own, mate, before, out, store = refs[2 + 2 * count :]
    root = lax.axis_index("slab") == 0

    @pl.when(root)
    def _():
        whole = [near[...], far[...]]
        for n, share in enumerate(shares):
            whole[n % 2] = whole[n % 2] - share[...]
        load_vector(store, *whole)
        out[...] = complex_product(own[4:6], mate[4:6], store)

    @pl.when(jnp.logical_not(root))
    def _():
        out[...] = before[...]


def settle_kernel(spacing, part, near, far, own, mate, out, store):
    active = lax.axis_index("slab") % (2 * spacing) == spacing

    @pl.when(active)
    def _():
        load_vector(store, near[...], far[...])
        out[...] = part[...] - complex_product(own[6:8], mate[6:8], store)

    @pl.when(jnp.logical_not(active))
    def _():
        out[...] = part[...]


def both_kernel(slabs, spacing, count, part, other, *refs):
    vectors = refs[:4]
    early = refs[4:count]
    own, mate, out, lower, upper = refs[count:]
    s = lax.axis_index("slab")
    active = s % (2 * spacing) == spacing
    first = s % (4 * spacing) == spacing
    linked = s + spacing < slabs

    def pick(n, wanted):
        values = vectors[n][...]
        return jnp.where(wanted, early[n][...], values) if n < len(early) else values

    @pl.when(active)
    def _():
        load_vector(lower, pick(0, first), pick(1, first))
        out[...] = part[...] - complex_product(own[6:8], mate[6:8], lower)

    @pl.when(active & linked)
    def _():
        second = jnp.logical_not(first)
        load_vector(upper, pick(2, second), pick(3, second))
        out[...] -= complex_product(own[8:10], mate[8:10], upper)

    @pl.when(jnp.logical_not(active))
    def _():
        out[...] = other[...]


def copy_kernel(values, *refs):
    refs[-1][...] = values[...]


def call(
    kernel,
    *operands,
    outs=1,
    scratch=(),
    unused=(),
    shape=jax.ShapeDtypeStruct((Q, LANES), wide),
    flops=10**9,
):
    vmem = pl.BlockSpec(memory_space=pltpu.VMEM)
    return pl.pallas_call(
        kernel,
        out_shape=shape if outs == 1 else (shape,) * outs,
        in_specs=[vmem] * len(operands) + [pl.BlockSpec(memory_space=pl.ANY)] * len(unused),
        out_specs=vmem if outs == 1 else (vmem,) * outs,
        scratch_shapes=list(scratch),
        cost_estimate=pl.CostEstimate(flops=flops, bytes_accessed=1, transcendentals=0),
        compiler_params=pltpu.CompilerParams(vmem_limit_bytes=16 * 2**20),
    )(*operands, *unused)


def completed(route, count, cols):
    target = dict(route)
    taken = set(target.values())
    for a in [a for a in range(count) if a not in target and a not in taken]:
        target[a] = a ^ 1
        taken.add(a ^ 1)
    for a in range(count):
        if a not in target:
            target[a] = next(b for b in range(count) if b not in taken and b % cols == a % cols)
            taken.add(target[a])
    if sorted(target.values()) != list(range(count)):
        raise ValueError("no permutation")
    return sorted(target.items())


def per_device(slabs, cols, waves, energy, tunnel, pivots, below, above, back_lower, back_upper):
    everyone = range(cols)
    width = energy.shape[2]
    store = pltpu.VMEM((width, LANES), short)
    levels = slabs.bit_length() - 1
    every = range(slabs)

    def send(values, moves, flip=0):
        route = []
        for c in everyone:
            for a, b, *h in moves:
                route.append((a * cols + c, b * cols + (c ^ flip)))
                here = b * cols + (c ^ flip)
                for h in h:
                    route.append((here, h * cols + c))
                    here = h * cols + c
                if here != b * cols + (c ^ flip):
                    route.append((here, a * cols + c))
        return lax.ppermute(values, ("slab", "col"), completed(route, slabs * cols, cols))

    def both(values, near_moves, far_moves):
        return send(values, near_moves), send(values, far_moves, 2)

    def swap(values):
        return send(values, [(a, a) for a in every], 1)

    def exchange(values, chosen=every):
        return send(values, [(a, a) for a in chosen], 2)

    def kernel(body, *arguments):
        return functools.partial(body, *arguments)

    def stack(*arrays, after):
        depth = sum(v.shape[0] for v in arrays)
        shape = jax.ShapeDtypeStruct((depth, Q, width), wide)
        return call(stack_kernel, *arrays, unused=(after,), shape=shape, flops=1)

    mate_waves = swap(waves)
    t_pair = tunnel, swap(tunnel)
    e_pair = energy, swap(energy)
    side = call(side_kernel, shape=jax.ShapeDtypeStruct((8, LANES), jnp.int32))
    psi, up_near, up_far = call(
        open_kernel, waves, mate_waves, side, *t_pair, outs=3, scratch=[pltpu.VMEM((64, width), wide)]
    )
    up, crossing = call(cross_kernel, psi, up_near, exchange(up_far), outs=2, flops=1)
    psi_far = exchange(psi)
    between = [(a, b) for k in every[1:-1:2] for a, b in ((k, k + 1), (k + 1, k))]
    stepped = send(crossing, [(a, a ^ 1) for a in every])
    rest = call(
        kernel(ham_kernel, slabs),
        psi,
        psi_far,
        *both(psi, between, between),
        *e_pair,
        *t_pair,
        scratch=[store, store],
        unused=(up,),
    )
    near, crossing = call(near_kernel, rest, stepped, outs=2, flops=1)
    far = exchange(crossing)
    blocks = below[0], above[0], pivots[0], back_lower[0], back_upper[0]
    front = stack(*blocks, after=near)
    front = front, swap(front)
    back = front
    base = call(even_kernel, rest, stepped, far, *t_pair, scratch=[store])

    pivot = near
    waiting = None

    def late_shares(after):
        if waiting is None:
            return ()
        beneath, over, d = waiting
        patient = [b for b in every if b % (4 * d) == 0]
        held = call(copy_kernel, beneath, unused=(after,))
        ways = [(b + d, b, b + 1) for b in patient]
        shares = both(held, ways, ways)
        if len(patient) > 1:
            held = call(copy_kernel, over, unused=(after,))
            shares += both(
                held,
                [(b - d, b, b - d + 1) for b in patient if b > 0],
                [(b - d, b, b - d + 3) for b in patient if b > 0],
            )
        return shares

    for level in range(levels):
        d = 2**level
        if level == levels - 1:
            beneath = call(kernel(top_kernel, d), near, far, *front, scratch=[store])
            shares = late_shares(beneath)
            shares += both(beneath, [(d, 0, 1, d + 1)], [(d, 0, 1, d - 1)])
            pivot = call(kernel(pivot_kernel, d), near, far, *back, pivot, scratch=[store])
            pivot = call(
                kernel(root_kernel, len(shares) // 2),
                base,
                base_far,
                *shares,
                *back,
                pivot,
                scratch=[store],
            )
            break
        if level > 0:
            beneath, over = call(
                kernel(level_kernel, d), near, far, *front, outs=2, scratch=[store]
            )
        else:
            beneath = call(kernel(top_kernel, d), near, far, *front, scratch=[store])
            over = call(
                kernel(over_kernel, d), near, far, *front, up, scratch=[store], unused=(beneath,)
            )
        if level == 0:
            more = send(over, between)
            less = send(beneath, [(a, a ^ 1) for a in every])
            pivot = call(
                kernel(pivot_kernel, d),
                near,
                far,
                *back,
                pivot,
                scratch=[store],
                unused=(over,),
                flops=1,
            )
            base = near = call(even_slabs_kernel, base, more, less)
            base_far = far = exchange(near, every[::2])
            continue
        urgent = [b for b in every if b % (4 * d) == 2 * d]
        more = both(over, [(b - d, b, b - 1) for b in urgent], [(b - d, b, b - 3) for b in urgent])
        less = both(
            beneath, [(b + d, b, b + 1) for b in urgent], [(b + d, b, b + 3) for b in urgent]
        )
        pivot = call(kernel(pivot_kernel, d), near, far, *back, pivot, scratch=[store])
        late = late_shares(beneath)
        if late:
            count = len(late) // 2
            base = call(kernel(reduce_kernel, d // 2, count), base, *late[::2])
            base_far = call(kernel(reduce_kernel, d // 2, count), base_far, *late[1::2])
        near = base - more[0] - less[0]
        far = base_far - more[1] - less[1]
        waiting = beneath, over, d

    solved = pivot
    for level in reversed(range(levels)):
        d = 2**level
        sources = [a for a in every if a % (2 * d) == 0]
        upper = [a for a in sources if a > 0]
        if d == 1:
            low_near = send(solved, [(a, a ^ 1) for a in every])
            ways = [(a, a - 1) for a in upper] + [(a - 1, a) for a in upper]
            up_near = send(solved, ways)
            up_far = send(solved, ways, 2)
            low_far = exchange(low_near, [a + 1 for a in sources])
            vectors = low_near, low_far, up_near, up_far
        elif level == levels - 1:
            vectors = both(solved, [(0, d, d + 1, 1)], [(0, d, d + 1, 1)])
        else:
            sources = [a for a in every if a % (4 * d) == 2 * d]
            up_near = send(solved, [(a, a - d, a - d + 1, a + 1) for a in sources])
            up_far = send(solved, [(a, a - d, a - d + 1, a + 1) for a in sources], 2)
            low_far = send(solved, [(a, a + d, a + d + 1, a + 1) for a in sources], 2)
            low_near = send(solved, [(a, a + d, a + d + 1, a + 1) for a in sources])
            vectors = (low_near, low_far, up_near, up_far) + early
        if level > 1:
            half = d // 2
            sources = [a for a in every if a % (2 * d) == 0]
            ways = [(a, a + half, a + half + 1, a + 1) for a in sources]
            early = both(solved, ways, ways)
            if len(sources) > 1:
                ways = [(a, a - half, a - half + 1, a + 1) for a in sources if a > 0]
                early += both(solved, ways, ways)
        if level == levels - 1 and levels > 1:
            solved = call(kernel(settle_kernel, d), pivot, *vectors, *back, scratch=[store])
        else:
            solved = call(
                kernel(both_kernel, slabs, d, len(vectors)),
                pivot,
                solved,
                *vectors,
                *back,
                scratch=[store, store],
            )
    out = call(regroup_kernel, solved, swap(solved))
    return out[None]


def solution(mesh):
    slabs, cols = mesh.shape["slab"], mesh.shape["col"]
    vector = P("slab", "col", None)
    block = P("slab", None, "col", None)
    return jax.shard_map(
        functools.partial(per_device, slabs, cols),
        mesh=mesh,
        in_specs=(vector,) * 3 + (block,) * 5,
        out_specs=vector,
        check_vma=False,
    )
```

```python
import functools

import jax
import jax.numpy as jnp
from jax import lax
from jax.experimental import pallas as pl
from jax.experimental.pallas import tpu as pltpu
from jax.sharding import PartitionSpec as P


half_step = 0.5
wide = jnp.float32
short = jnp.bfloat16
Q = 128
LANES = 128


def lanes(values):
    return lax.broadcasted_iota(jnp.int32, values.shape, 1)


def swap_halves(values):
    return pltpu.roll(values, 64, 1)


def join(left, right):
    return jnp.where(lanes(left) < 64, left, right)


def rotate(values):
    even = lanes(values) % 2 == 0
    return jnp.where(even, -pltpu.roll(values, LANES - 1, 1), pltpu.roll(values, 1, 1))


def split(values):
    high = values.astype(short)
    return high, (values - high.astype(wide)).astype(short)


def quarter(number):
    return pl.ds(pl.multiple_of(number * Q, Q), Q)


def spread(store, packed, first):
    high = packed.astype(short).astype(wide)
    low = packed - high
    store[quarter(first), :] = join(high, swap_halves(low)).astype(short)
    store[quarter(first ^ 1), :] = join(swap_halves(high), low).astype(short)


def load_vector(store, near, far):
    c = lax.axis_index("col")
    spread(store, near, c)
    spread(store, far, c ^ 2)


def keep(wanted, values):
    return jnp.where(wanted, values[...], 0.0)


def rows_product(block, store):
    high, low = split(block)
    vector = store[...]
    return jnp.dot(high, vector, preferred_element_type=wide) + jnp.dot(
        low, vector, preferred_element_type=wide
    )


def fold(values):
    return values + swap_halves(values)


def real_product(own, mate, store):
    return join(fold(rows_product(own, store)), fold(rows_product(mate, store)))


def complex_half(block, store):
    both = rows_product(block.reshape(2 * Q, block.shape[-1]), store)
    return fold(both[:Q] + rotate(both[Q:]))


def complex_product(own, mate, store):
    return join(complex_half(own, store), complex_half(mate, store))


def this_core(left, right):
    first = lax.axis_index("col") % 2 == 0
    return jnp.where(first, join(left, swap_halves(right)), join(swap_halves(left), right))


def side_kernel(side):
    side[...] = jnp.zeros_like(side) + lax.axis_index("col")


def regroup_kernel(mine, other, out):
    rows = join(mine[...], other[...])
    out[...] = jnp.where(lax.axis_index("col") % 2 == 0, rows, swap_halves(rows))


def stack_kernel(*refs):
    *sources, _, out = refs
    place = 0
    for source in sources:
        depth = source.shape[0]
        out[place : place + depth] = source[...]
        place += depth


def open_kernel(mine, other, side, own, mate, psi, near, far, store):
    c = lax.axis_index("col")
    packed = this_core(mine[0], other[0])
    psi[...] = packed
    turned = packed.T
    total = None
    for rows, block in ((turned[:64], own[0]), (turned[64:], mate[0])):
        high, low = split(rows)
        pair = jnp.concatenate([high, low], axis=0)
        block_high, block_low = split(block)
        part = jnp.dot(pair, block_high, preferred_element_type=wide) + jnp.dot(
            pair, block_low, preferred_element_type=wide
        )
        part = part[:64] + part[64:]
        total = part if total is None else total + part
    store[...] = total
    for out, first in ((far, c ^ 2), (near, c)):
        pair = jnp.concatenate(
            [store[:, quarter(first)], store[:, quarter(first ^ 1)]], axis=0
        )
        out[...] = half_step * rotate(pair.T)


def cross_kernel(packed, near, other, up, crossing):
    whole = near[...] + other[...]
    up[...] = whole
    crossing[...] = jnp.where(lax.axis_index("slab") % 2 == 1, packed[...], whole)


def near_kernel(rest, stepped, near, crossing):
    whole = rest[...] - stepped[...]
    near[...] = whole
    crossing[...] = jnp.where(lax.axis_index("slab") % 2 == 1, whole, stepped[...])


def even_slabs_kernel(base, more, less, out):
    s = lax.axis_index("slab")
    even = s % 2 == 0
    out[...] = base[...] - keep(even & (s > 0), more) - keep(even, less)


def reduce_kernel(spacing, count, base, *refs):
    out = refs[-1]
    less, *more = refs[:count]
    s = lax.axis_index("slab")
    kept = s % (4 * spacing) == 0
    values = base[...] - keep(kept, less)
    for late in more:
        values = values - keep(kept & (s > 0), late)
    out[...] = values


def ham_kernel(slabs, near, far, next_near, next_far, own_e, mate_e, own_t, mate_t, *refs):
    out, here, there = refs[-3:]
    s = lax.axis_index("slab")
    load_vector(here, near[...], far[...])
    out[...] = near[...] - half_step * rotate(real_product(own_e[0], mate_e[0], here))

    @pl.when((s % 2 == 1) & (s < slabs - 1))
    def _():
        load_vector(there, next_near[...], next_far[...])
        out[...] -= half_step * rotate(real_product(own_t[0], mate_t[0], there))


def even_kernel(rest, next_near, next_far, own, mate, out, store):
    @pl.when(lax.axis_index("slab") % 2 == 0)
    def _():
        load_vector(store, next_near[...], next_far[...])
        out[...] = rest[...] - half_step * rotate(real_product(own[0], mate[0], store))


def level_kernel(spacing, near, far, own, mate, *refs):
    beneath, above, store = refs[-3:]

    @pl.when(lax.axis_index("slab") % (2 * spacing) == spacing)
    def _():
        load_vector(store, near[...], far[...])
        above[...] = complex_product(own[2:4], mate[2:4], store)
        beneath[...] = complex_product(own[0:2], mate[0:2], store)


def over_kernel(spacing, near, far, own, mate, *refs):
    tail, _, out, store = refs

    @pl.when(lax.axis_index("slab") % (2 * spacing) == spacing)
    def _():
        load_vector(store, near[...], far[...])
        out[...] = complex_product(own[2:4], mate[2:4], store) + tail[...]


def top_kernel(spacing, near, far, own, mate, *refs):
    beneath, store = refs[-2:]

    @pl.when(lax.axis_index("slab") % (2 * spacing) == spacing)
    def _():
        load_vector(store, near[...], far[...])
        beneath[...] = complex_product(own[0:2], mate[0:2], store)


def pivot_kernel(spacing, near, far, own, mate, before, *refs):
    out, store = refs[-2:]
    active = lax.axis_index("slab") % (2 * spacing) == spacing

    @pl.when(active)
    def _():
        load_vector(store, near[...], far[...])
        out[...] = complex_product(own[4:6], mate[4:6], store)

    @pl.when(jnp.logical_not(active))
    def _():
        out[...] = before[...]


def root_kernel(count, *refs):
    near, far = refs[:2]
    shares = refs[2 : 2 + 2 * count]
    own, mate, before, out, store = refs[2 + 2 * count :]
    root = lax.axis_index("slab") == 0

    @pl.when(root)
    def _():
        whole = [near[...], far[...]]
        for n, share in enumerate(shares):
            whole[n % 2] = whole[n % 2] - share[...]
        load_vector(store, *whole)
        out[...] = complex_product(own[4:6], mate[4:6], store)

    @pl.when(jnp.logical_not(root))
    def _():
        out[...] = before[...]


def settle_kernel(spacing, part, near, far, own, mate, out, store):
    active = lax.axis_index("slab") % (2 * spacing) == spacing

    @pl.when(active)
    def _():
        load_vector(store, near[...], far[...])
        out[...] = part[...] - complex_product(own[6:8], mate[6:8], store)

    @pl.when(jnp.logical_not(active))
    def _():
        out[...] = part[...]


def both_kernel(slabs, spacing, count, part, other, *refs):
    vectors = refs[:4]
    early = refs[4:count]
    own, mate, out, lower, upper = refs[count:]
    s = lax.axis_index("slab")
    active = s % (2 * spacing) == spacing
    first = s % (4 * spacing) == spacing
    linked = s + spacing < slabs

    def pick(n, wanted):
        values = vectors[n][...]
        return jnp.where(wanted, early[n][...], values) if n < len(early) else values

    @pl.when(active)
    def _():
        load_vector(lower, pick(0, first), pick(1, first))
        out[...] = part[...] - complex_product(own[6:8], mate[6:8], lower)

    @pl.when(active & linked)
    def _():
        second = jnp.logical_not(first)
        load_vector(upper, pick(2, second), pick(3, second))
        out[...] -= complex_product(own[8:10], mate[8:10], upper)

    @pl.when(jnp.logical_not(active))
    def _():
        out[...] = other[...]


def copy_kernel(values, *refs):
    refs[-1][...] = values[...]


def call(
    kernel,
    *operands,
    outs=1,
    scratch=(),
    unused=(),
    shape=jax.ShapeDtypeStruct((Q, LANES), wide),
    flops=10**9,
):
    vmem = pl.BlockSpec(memory_space=pltpu.VMEM)
    return pl.pallas_call(
        kernel,
        out_shape=shape if outs == 1 else (shape,) * outs,
        in_specs=[vmem] * len(operands) + [pl.BlockSpec(memory_space=pl.ANY)] * len(unused),
        out_specs=vmem if outs == 1 else (vmem,) * outs,
        scratch_shapes=list(scratch),
        cost_estimate=pl.CostEstimate(flops=flops, bytes_accessed=1, transcendentals=0),
        compiler_params=pltpu.CompilerParams(vmem_limit_bytes=16 * 2**20),
    )(*operands, *unused)


def completed(route, count, cols):
    target = dict(route)
    taken = set(target.values())
    for a in [a for a in range(count) if a not in target and a not in taken]:
        target[a] = a ^ 1
        taken.add(a ^ 1)
    for a in range(count):
        if a not in target:
            target[a] = next(b for b in range(count) if b not in taken and b % cols == a % cols)
            taken.add(target[a])
    if sorted(target.values()) != list(range(count)):
        raise ValueError("no permutation")
    return sorted(target.items())


def per_device(slabs, cols, waves, energy, tunnel, pivots, below, above, back_lower, back_upper):
    everyone = range(cols)
    width = energy.shape[2]
    store = pltpu.VMEM((width, LANES), short)
    levels = slabs.bit_length() - 1
    every = range(slabs)

    def send(values, moves, flip=0):
        route = []
        for c in everyone:
            for a, b, *h in moves:
                route.append((a * cols + c, b * cols + (c ^ flip)))
                here = b * cols + (c ^ flip)
                for h in h:
                    route.append((here, h * cols + c))
                    here = h * cols + c
                if here != b * cols + (c ^ flip):
                    route.append((here, a * cols + c))
        return lax.ppermute(values, ("slab", "col"), completed(route, slabs * cols, cols))

    def both(values, near_moves, far_moves):
        return send(values, near_moves), send(values, far_moves, 2)

    def swap(values):
        return send(values, [(a, a) for a in every], 1)

    def exchange(values, chosen=every):
        return send(values, [(a, a) for a in chosen], 2)

    def kernel(body, *arguments):
        return functools.partial(body, *arguments)

    def stack(*arrays, after):
        depth = sum(v.shape[0] for v in arrays)
        shape = jax.ShapeDtypeStruct((depth, Q, width), wide)
        return call(stack_kernel, *arrays, unused=(after,), shape=shape, flops=1)

    mate_waves = swap(waves)
    t_pair = tunnel, swap(tunnel)
    e_pair = energy, swap(energy)
    side = call(side_kernel, shape=jax.ShapeDtypeStruct((8, LANES), jnp.int32))
    psi, up_near, up_far = call(
        open_kernel, waves, mate_waves, side, *t_pair, outs=3, scratch=[pltpu.VMEM((64, width), wide)]
    )
    up, crossing = call(cross_kernel, psi, up_near, exchange(up_far), outs=2, flops=1)
    psi_far = exchange(psi)
    between = [(a, b) for k in every[1:-1:2] for a, b in ((k, k + 1), (k + 1, k))]
    stepped = send(crossing, [(a, a ^ 1) for a in every])
    rest = call(
        kernel(ham_kernel, slabs),
        psi,
        psi_far,
        *both(psi, between, between),
        *e_pair,
        *t_pair,
        scratch=[store, store],
        unused=(up,),
    )
    near, crossing = call(near_kernel, rest, stepped, outs=2, flops=1)
    far = exchange(crossing)
    blocks = below[0], above[0], pivots[0], back_lower[0], back_upper[0]
    front = stack(*blocks, after=near)
    front = front, swap(front)
    back = front
    base = call(even_kernel, rest, stepped, far, *t_pair, scratch=[store])

    pivot = near
    waiting = None

    def late_shares(after):
        if waiting is None:
            return ()
        beneath, over, d = waiting
        patient = [b for b in every if b % (4 * d) == 0]
        held = call(copy_kernel, beneath, unused=(after,))
        ways = [(b + d, b, b + 1) for b in patient]
        shares = both(held, ways, ways)
        if len(patient) > 1:
            held = call(copy_kernel, over, unused=(after,))
            shares += both(
                held,
                [(b - d, b, b - d + 1) for b in patient if b > 0],
                [(b - d, b, b - d + 3) for b in patient if b > 0],
            )
        return shares

    for level in range(levels):
        d = 2**level
        if level == levels - 1:
            beneath = call(kernel(top_kernel, d), near, far, *front, scratch=[store])
            shares = late_shares(beneath)
            shares += both(beneath, [(d, 0, 1, d + 1)], [(d, 0, 1, d - 1)])
            pivot = call(kernel(pivot_kernel, d), near, far, *back, pivot, scratch=[store])
            pivot = call(
                kernel(root_kernel, len(shares) // 2),
                base,
                base_far,
                *shares,
                *back,
                pivot,
                scratch=[store],
            )
            break
        if level > 0:
            beneath, over = call(
                kernel(level_kernel, d), near, far, *front, outs=2, scratch=[store]
            )
        else:
            beneath = call(kernel(top_kernel, d), near, far, *front, scratch=[store])
            over = call(
                kernel(over_kernel, d), near, far, *front, up, scratch=[store], unused=(beneath,)
            )
        if level == 0:
            more = send(over, between)
            less = send(beneath, [(a, a ^ 1) for a in every])
            pivot = call(
                kernel(pivot_kernel, d),
                near,
                far,
                *back,
                pivot,
                scratch=[store],
                unused=(over,),
                flops=1,
            )
            base = near = call(even_slabs_kernel, base, more, less)
            base_far = far = exchange(near, every[::2])
            continue
        urgent = [b for b in every if b % (4 * d) == 2 * d]
        more = both(
            over, [(b - d, b, b - 1) for b in urgent], [(b - d, b, b - 2 * d) for b in urgent]
        )
        less = both(
            beneath, [(b + d, b, b + 1) for b in urgent], [(b + d, b, b + 3) for b in urgent]
        )
        pivot = call(kernel(pivot_kernel, d), near, far, *back, pivot, scratch=[store])
        late = late_shares(beneath)
        if late:
            count = len(late) // 2
            base = call(kernel(reduce_kernel, d // 2, count), base, *late[::2])
            base_far = call(kernel(reduce_kernel, d // 2, count), base_far, *late[1::2])
        near = base - more[0] - less[0]
        far = base_far - more[1] - less[1]
        waiting = beneath, over, d

    solved = pivot
    for level in reversed(range(levels)):
        d = 2**level
        sources = [a for a in every if a % (2 * d) == 0]
        upper = [a for a in sources if a > 0]
        if d == 1:
            low_near = send(solved, [(a, a ^ 1) for a in every])
            ways = [(a, a - 1) for a in upper] + [(a - 1, a) for a in upper]
            up_near = send(solved, ways)
            up_far = send(solved, ways, 2)
            low_far = exchange(low_near, [a + 1 for a in sources])
            vectors = low_near, low_far, up_near, up_far
        elif level == levels - 1:
            vectors = both(solved, [(0, d, d + 1, 1)], [(0, d, d + 1, 1)])
        else:
            sources = [a for a in every if a % (4 * d) == 2 * d]
            up_near = send(solved, [(a, a - d, a - d + 1, a + 1) for a in sources])
            up_far = send(solved, [(a, a - d, a - d + 1, a + 1) for a in sources], 2)
            low_far = send(solved, [(a, a + d, a + d + 1, a + 1) for a in sources], 2)
            low_near = send(solved, [(a, a + d, a + d + 1, a + 1) for a in sources])
            vectors = (low_near, low_far, up_near, up_far) + early
        if level > 1:
            half = d // 2
            sources = [a for a in every if a % (2 * d) == 0]
            held = call(copy_kernel, solved, unused=(vectors[0],))
            ways = [(a, a + half, a + half + 1, a + 1) for a in sources]
            early = both(held, ways, ways)
            if len(sources) > 1:
                ways = [(a, a - half, a - half + 1, a + 1) for a in sources if a > 0]
                early += both(held, ways, ways)
        if level == levels - 1 and levels > 1:
            solved = call(kernel(settle_kernel, d), pivot, *vectors, *back, scratch=[store])
        else:
            solved = call(
                kernel(both_kernel, slabs, d, len(vectors)),
                pivot,
                solved,
                *vectors,
                *back,
                scratch=[store, store],
            )
    out = call(regroup_kernel, solved, swap(solved))
    return out[None]


def solution(mesh):
    slabs, cols = mesh.shape["slab"], mesh.shape["col"]
    vector = P("slab", "col", None)
    block = P("slab", None, "col", None)
    return jax.shard_map(
        functools.partial(per_device, slabs, cols),
        mesh=mesh,
        in_specs=(vector,) * 3 + (block,) * 5,
        out_specs=vector,
        check_vma=False,
    )
```

```python
import functools

import jax
import jax.numpy as jnp
from jax import lax
from jax.experimental import pallas as pl
from jax.experimental.pallas import tpu as pltpu
from jax.sharding import PartitionSpec as P


half_step = 0.5
wide = jnp.float32
short = jnp.bfloat16
Q = 128
LANES = 128


def lanes(values):
    return lax.broadcasted_iota(jnp.int32, values.shape, 1)


def swap_halves(values):
    return pltpu.roll(values, 64, 1)


def join(left, right):
    return jnp.where(lanes(left) < 64, left, right)


def rotate(values):
    even = lanes(values) % 2 == 0
    return jnp.where(even, -pltpu.roll(values, LANES - 1, 1), pltpu.roll(values, 1, 1))


def split(values):
    high = values.astype(short)
    return high, (values - high.astype(wide)).astype(short)


def quarter(number):
    return pl.ds(pl.multiple_of(number * Q, Q), Q)


def spread(store, packed, first):
    high = packed.astype(short).astype(wide)
    low = packed - high
    store[quarter(first), :] = join(high, swap_halves(low)).astype(short)
    store[quarter(first ^ 1), :] = join(swap_halves(high), low).astype(short)


def load_vector(store, near, far):
    c = lax.axis_index("col")
    spread(store, near, c)
    spread(store, far, c ^ 2)


def keep(wanted, values):
    return jnp.where(wanted, values[...], 0.0)


def rows_product(block, store):
    high, low = split(block)
    vector = store[...]
    return jnp.dot(high, vector, preferred_element_type=wide) + jnp.dot(
        low, vector, preferred_element_type=wide
    )


def fold(values):
    return values + swap_halves(values)


def real_product(own, mate, store):
    return join(fold(rows_product(own, store)), fold(rows_product(mate, store)))


def complex_half(block, store):
    both = rows_product(block.reshape(2 * Q, block.shape[-1]), store)
    return fold(both[:Q] + rotate(both[Q:]))


def complex_product(own, mate, store):
    return join(complex_half(own, store), complex_half(mate, store))


def this_core(left, right):
    first = lax.axis_index("col") % 2 == 0
    return jnp.where(first, join(left, swap_halves(right)), join(swap_halves(left), right))


def side_kernel(side):
    side[...] = jnp.zeros_like(side) + lax.axis_index("col")


def regroup_kernel(mine, other, out):
    rows = join(mine[...], other[...])
    out[...] = jnp.where(lax.axis_index("col") % 2 == 0, rows, swap_halves(rows))


def stack_kernel(*refs):
    *sources, _, out = refs
    place = 0
    for source in sources:
        depth = source.shape[0]
        out[place : place + depth] = source[...]
        place += depth


def open_kernel(mine, other, side, own, mate, psi, near, far, store):
    c = lax.axis_index("col")
    packed = this_core(mine[0], other[0])
    psi[...] = packed
    turned = packed.T
    total = None
    for rows, block in ((turned[:64], own[0]), (turned[64:], mate[0])):
        high, low = split(rows)
        pair = jnp.concatenate([high, low], axis=0)
        block_high, block_low = split(block)
        part = jnp.dot(pair, block_high, preferred_element_type=wide) + jnp.dot(
            pair, block_low, preferred_element_type=wide
        )
        part = part[:64] + part[64:]
        total = part if total is None else total + part
    store[...] = total
    for out, first in ((far, c ^ 2), (near, c)):
        pair = jnp.concatenate(
            [store[:, quarter(first)], store[:, quarter(first ^ 1)]], axis=0
        )
        out[...] = half_step * rotate(pair.T)


def cross_kernel(packed, near, other, up, crossing):
    whole = near[...] + other[...]
    up[...] = whole
    crossing[...] = jnp.where(lax.axis_index("slab") % 2 == 1, packed[...], whole)


def near_kernel(rest, stepped, near, crossing):
    whole = rest[...] - stepped[...]
    near[...] = whole
    crossing[...] = jnp.where(lax.axis_index("slab") % 2 == 1, whole, stepped[...])


def join_kernel(spacing, base, more, less, out):
    s = lax.axis_index("slab")
    left = s % (2 * spacing) == 0
    out[...] = base[...] - keep(left & (s > 0), more) - keep(left, less)


def ham_kernel(slabs, near, far, next_near, next_far, own_e, mate_e, own_t, mate_t, *refs):
    out, here, there = refs[-3:]
    s = lax.axis_index("slab")
    load_vector(here, near[...], far[...])
    out[...] = near[...] - half_step * rotate(real_product(own_e[0], mate_e[0], here))

    @pl.when((s % 2 == 1) & (s < slabs - 1))
    def _():
        load_vector(there, next_near[...], next_far[...])
        out[...] -= half_step * rotate(real_product(own_t[0], mate_t[0], there))


def even_kernel(rest, next_near, next_far, own, mate, out, store):
    @pl.when(lax.axis_index("slab") % 2 == 0)
    def _():
        load_vector(store, next_near[...], next_far[...])
        out[...] = rest[...] - half_step * rotate(real_product(own[0], mate[0], store))


def level_kernel(spacing, near, far, own, mate, *refs):
    beneath, above, store = refs[-3:]

    @pl.when(lax.axis_index("slab") % (2 * spacing) == spacing)
    def _():
        load_vector(store, near[...], far[...])
        above[...] = complex_product(own[2:4], mate[2:4], store)
        beneath[...] = complex_product(own[0:2], mate[0:2], store)


def over_kernel(spacing, near, far, own, mate, *refs):
    tail, _, out, store = refs

    @pl.when(lax.axis_index("slab") % (2 * spacing) == spacing)
    def _():
        load_vector(store, near[...], far[...])
        out[...] = complex_product(own[2:4], mate[2:4], store) + tail[...]


def top_kernel(spacing, near, far, own, mate, *refs):
    beneath, store = refs[-2:]

    @pl.when(lax.axis_index("slab") % (2 * spacing) == spacing)
    def _():
        load_vector(store, near[...], far[...])
        beneath[...] = complex_product(own[0:2], mate[0:2], store)


def pivot_kernel(spacing, near, far, own, mate, before, *refs):
    out, store = refs[-2:]
    active = lax.axis_index("slab") % (2 * spacing) == spacing

    @pl.when(active)
    def _():
        load_vector(store, near[...], far[...])
        out[...] = complex_product(own[4:6], mate[4:6], store)

    @pl.when(jnp.logical_not(active))
    def _():
        out[...] = before[...]


def root_kernel(count, *refs):
    near, far = refs[:2]
    shares = refs[2 : 2 + 2 * count]
    own, mate, before, out, store = refs[2 + 2 * count :]
    root = lax.axis_index("slab") == 0

    @pl.when(root)
    def _():
        whole = [near[...], far[...]]
        for n, share in enumerate(shares):
            whole[n % 2] = whole[n % 2] - share[...]
        load_vector(store, *whole)
        out[...] = complex_product(own[4:6], mate[4:6], store)

    @pl.when(jnp.logical_not(root))
    def _():
        out[...] = before[...]


def settle_kernel(spacing, part, near, far, own, mate, out, store):
    active = lax.axis_index("slab") % (2 * spacing) == spacing

    @pl.when(active)
    def _():
        load_vector(store, near[...], far[...])
        out[...] = part[...] - complex_product(own[6:8], mate[6:8], store)

    @pl.when(jnp.logical_not(active))
    def _():
        out[...] = part[...]


def both_kernel(slabs, spacing, count, part, other, *refs):
    vectors = refs[:4]
    early = refs[4:count]
    own, mate, out, lower, upper = refs[count:]
    s = lax.axis_index("slab")
    active = s % (2 * spacing) == spacing
    first = s % (4 * spacing) == spacing
    linked = s + spacing < slabs

    def pick(n, wanted):
        values = vectors[n][...]
        return jnp.where(wanted, early[n][...], values) if n < len(early) else values

    @pl.when(active)
    def _():
        load_vector(lower, pick(0, first), pick(1, first))
        out[...] = part[...] - complex_product(own[6:8], mate[6:8], lower)

    @pl.when(active & linked)
    def _():
        second = jnp.logical_not(first)
        load_vector(upper, pick(2, second), pick(3, second))
        out[...] -= complex_product(own[8:10], mate[8:10], upper)

    @pl.when(jnp.logical_not(active))
    def _():
        out[...] = other[...]


def call(
    kernel,
    *operands,
    outs=1,
    scratch=(),
    unused=(),
    shape=jax.ShapeDtypeStruct((Q, LANES), wide),
    flops=10**9,
):
    vmem = pl.BlockSpec(memory_space=pltpu.VMEM)
    return pl.pallas_call(
        kernel,
        out_shape=shape if outs == 1 else (shape,) * outs,
        in_specs=[vmem] * len(operands) + [pl.BlockSpec(memory_space=pl.ANY)] * len(unused),
        out_specs=vmem if outs == 1 else (vmem,) * outs,
        scratch_shapes=list(scratch),
        cost_estimate=pl.CostEstimate(flops=flops, bytes_accessed=1, transcendentals=0),
        compiler_params=pltpu.CompilerParams(vmem_limit_bytes=16 * 2**20),
    )(*operands, *unused)


def completed(route, count, cols):
    target = dict(route)
    taken = set(target.values())
    for a in [a for a in range(count) if a not in target and a not in taken]:
        target[a] = a ^ 1
        taken.add(a ^ 1)
    for a in range(count):
        if a not in target:
            target[a] = next(b for b in range(count) if b not in taken and b % cols == a % cols)
            taken.add(target[a])
    if sorted(target.values()) != list(range(count)):
        raise ValueError("no permutation")
    return sorted(target.items())


def per_device(slabs, cols, waves, energy, tunnel, pivots, below, above, back_lower, back_upper):
    everyone = range(cols)
    width = energy.shape[2]
    store = pltpu.VMEM((width, LANES), short)
    levels = slabs.bit_length() - 1
    every = range(slabs)

    def send(values, moves, flip=0):
        route = []
        for c in everyone:
            for a, b, *h in moves:
                route.append((a * cols + c, b * cols + (c ^ flip)))
                here = b * cols + (c ^ flip)
                for h in h:
                    route.append((here, h * cols + c))
                    here = h * cols + c
                if here != b * cols + (c ^ flip):
                    route.append((here, a * cols + c))
        return lax.ppermute(values, ("slab", "col"), completed(route, slabs * cols, cols))

    def both(values, near_moves, far_moves):
        return send(values, near_moves), send(values, far_moves, 2)

    def swap(values):
        return send(values, [(a, a) for a in every], 1)

    def exchange(values, chosen=every):
        return send(values, [(a, a) for a in chosen], 2)

    def kernel(body, *arguments):
        return functools.partial(body, *arguments)

    def stack(*arrays, after):
        depth = sum(v.shape[0] for v in arrays)
        shape = jax.ShapeDtypeStruct((depth, Q, width), wide)
        return call(stack_kernel, *arrays, unused=(after,), shape=shape, flops=1)

    mate_waves = swap(waves)
    t_pair = tunnel, swap(tunnel)
    e_pair = energy, swap(energy)
    side = call(side_kernel, shape=jax.ShapeDtypeStruct((8, LANES), jnp.int32))
    psi, up_near, up_far = call(
        open_kernel, waves, mate_waves, side, *t_pair, outs=3, scratch=[pltpu.VMEM((64, width), wide)]
    )
    up, crossing = call(cross_kernel, psi, up_near, exchange(up_far), outs=2, flops=1)
    psi_far = exchange(psi)
    between = [(a, b) for k in every[1:-1:2] for a, b in ((k, k + 1), (k + 1, k))]
    stepped = send(crossing, [(a, a ^ 1) for a in every])
    rest = call(
        kernel(ham_kernel, slabs),
        psi,
        psi_far,
        *both(psi, between, between),
        *e_pair,
        *t_pair,
        scratch=[store, store],
        unused=(up,),
    )
    near, crossing = call(near_kernel, rest, stepped, outs=2, flops=1)
    far = exchange(crossing)
    blocks = below[0], above[0], pivots[0], back_lower[0], back_upper[0]
    front = stack(*blocks, after=near)
    front = front, swap(front)
    back = front
    base = call(even_kernel, rest, stepped, far, *t_pair, scratch=[store])

    pivot = near
    for level in range(levels):
        d = 2**level
        if level == levels - 1:
            beneath = call(kernel(top_kernel, d), near, far, *front, scratch=[store])
            shares = both(beneath, [(d, 0, 1, d + 1)], [(d, 0, 1, d - 1)])
            pivot = call(kernel(pivot_kernel, d), near, far, *back, pivot, scratch=[store])
            pivot = call(
                kernel(root_kernel, len(shares) // 2),
                base,
                base_far,
                *shares,
                *back,
                pivot,
                scratch=[store],
            )
            break
        if level > 0:
            beneath, over = call(
                kernel(level_kernel, d), near, far, *front, outs=2, scratch=[store]
            )
        else:
            beneath = call(kernel(top_kernel, d), near, far, *front, scratch=[store])
            over = call(
                kernel(over_kernel, d), near, far, *front, up, scratch=[store], unused=(beneath,)
            )
        if level == 0:
            more = send(over, between)
            less = send(beneath, [(a, a ^ 1) for a in every])
            pivot = call(
                kernel(pivot_kernel, d),
                near,
                far,
                *back,
                pivot,
                scratch=[store],
                unused=(over,),
                flops=1,
            )
            base = near = call(kernel(join_kernel, d), base, more, less)
            base_far = far = exchange(near, every[::2])
            continue
        active = [a for a in every if a % (2 * d) == d]
        rising = [a for a in active if a + d < slabs]
        more = both(
            over, [(a, a + d, a + 1) for a in rising], [(a, a + d, a - 1) for a in rising]
        )
        less = both(
            beneath, [(a, a - d, a - 1) for a in active], [(a, a - d, a + 1) for a in active]
        )
        pivot = call(kernel(pivot_kernel, d), near, far, *back, pivot, scratch=[store])
        near = base = call(kernel(join_kernel, d), base, more[0], less[0])
        far = base_far = call(kernel(join_kernel, d), base_far, more[1], less[1])

    solved = pivot
    for level in reversed(range(levels)):
        d = 2**level
        sources = [a for a in every if a % (2 * d) == 0]
        upper = [a for a in sources if a > 0]
        if d == 1:
            low_near = send(solved, [(a, a ^ 1) for a in every])
            ways = [(a, a - 1) for a in upper] + [(a - 1, a) for a in upper]
            up_near = send(solved, ways)
            up_far = send(solved, ways, 2)
            low_far = exchange(low_near, [a + 1 for a in sources])
            vectors = low_near, low_far, up_near, up_far
        elif level == levels - 1:
            vectors = both(solved, [(0, d, d + 1, 1)], [(0, d, d + 1, 1)])
        else:
            sources = [a for a in every if a % (4 * d) == 2 * d]
            up_near = send(solved, [(a, a - d, a - d + 1, a + 1) for a in sources])
            up_far = send(solved, [(a, a - d, a - d + 1, a + 1) for a in sources], 2)
            low_far = send(solved, [(a, a + d, a + d + 1, a + 1) for a in sources], 2)
            low_near = send(solved, [(a, a + d, a + d + 1, a + 1) for a in sources])
            vectors = (low_near, low_far, up_near, up_far) + early
        if level > 1:
            half = d // 2
            sources = [a for a in every if a % (2 * d) == 0]
            ways = [(a, a + half, a + half + 1, a + 1) for a in sources]
            early = both(solved, ways, ways)
            if len(sources) > 1:
                ways = [(a, a - half, a - half + 1, a + 1) for a in sources if a > 0]
                early += both(solved, ways, ways)
        if level == levels - 1 and levels > 1:
            solved = call(kernel(settle_kernel, d), pivot, *vectors, *back, scratch=[store])
        else:
            solved = call(
                kernel(both_kernel, slabs, d, len(vectors)),
                pivot,
                solved,
                *vectors,
                *back,
                scratch=[store, store],
            )
    out = call(regroup_kernel, solved, swap(solved))
    return out[None]


def solution(mesh):
    slabs, cols = mesh.shape["slab"], mesh.shape["col"]
    vector = P("slab", "col", None)
    block = P("slab", None, "col", None)
    return jax.shard_map(
        functools.partial(per_device, slabs, cols),
        mesh=mesh,
        in_specs=(vector,) * 3 + (block,) * 5,
        out_specs=vector,
        check_vma=False,
    )
```

```python
import functools

import jax
import jax.numpy as jnp
from jax import lax
from jax.experimental import pallas as pl
from jax.experimental.pallas import tpu as pltpu
from jax.sharding import PartitionSpec as P


half_step = 0.5
wide = jnp.float32
short = jnp.bfloat16
Q = 128
LANES = 128


def lanes(values):
    return lax.broadcasted_iota(jnp.int32, values.shape, 1)


def swap_halves(values):
    return pltpu.roll(values, 64, 1)


def join(left, right):
    return jnp.where(lanes(left) < 64, left, right)


def rotate(values):
    even = lanes(values) % 2 == 0
    return jnp.where(even, -pltpu.roll(values, LANES - 1, 1), pltpu.roll(values, 1, 1))


def split(values):
    high = values.astype(short)
    return high, (values - high.astype(wide)).astype(short)


def quarter(number):
    return pl.ds(pl.multiple_of(number * Q, Q), Q)


def spread(store, packed, first):
    high = packed.astype(short).astype(wide)
    low = packed - high
    store[quarter(first), :] = join(high, swap_halves(low)).astype(short)
    store[quarter(first ^ 1), :] = join(swap_halves(high), low).astype(short)


def load_vector(store, near, far):
    c = lax.axis_index("col")
    spread(store, near, c)
    spread(store, far, c ^ 2)


def keep(wanted, values):
    return jnp.where(wanted, values[...], 0.0)


def rows_product(block, store):
    high, low = split(block)
    vector = store[...]
    return jnp.dot(high, vector, preferred_element_type=wide) + jnp.dot(
        low, vector, preferred_element_type=wide
    )


def fold(values):
    return values + swap_halves(values)


def real_product(own, mate, store):
    return join(fold(rows_product(own, store)), fold(rows_product(mate, store)))


def complex_half(block, store):
    both = rows_product(block.reshape(2 * Q, block.shape[-1]), store)
    return fold(both[:Q] + rotate(both[Q:]))


def complex_product(own, mate, store):
    return join(complex_half(own, store), complex_half(mate, store))


def this_core(left, right):
    first = lax.axis_index("col") % 2 == 0
    return jnp.where(first, join(left, swap_halves(right)), join(swap_halves(left), right))


def side_kernel(side):
    side[...] = jnp.zeros_like(side) + lax.axis_index("col")


def regroup_kernel(mine, other, out):
    rows = join(mine[...], other[...])
    out[...] = jnp.where(lax.axis_index("col") % 2 == 0, rows, swap_halves(rows))


def stack_kernel(*refs):
    *sources, _, out = refs
    place = 0
    for source in sources:
        depth = source.shape[0]
        out[place : place + depth] = source[...]
        place += depth


def open_kernel(mine, other, side, own, mate, psi, near, far, store):
    c = lax.axis_index("col")
    packed = this_core(mine[0], other[0])
    psi[...] = packed
    turned = packed.T
    total = None
    for rows, block in ((turned[:64], own[0]), (turned[64:], mate[0])):
        high, low = split(rows)
        pair = jnp.concatenate([high, low], axis=0)
        block_high, block_low = split(block)
        part = jnp.dot(pair, block_high, preferred_element_type=wide) + jnp.dot(
            pair, block_low, preferred_element_type=wide
        )
        part = part[:64] + part[64:]
        total = part if total is None else total + part
    store[...] = total
    for out, first in ((far, c ^ 2), (near, c)):
        pair = jnp.concatenate(
            [store[:, quarter(first)], store[:, quarter(first ^ 1)]], axis=0
        )
        out[...] = half_step * rotate(pair.T)


def cross_kernel(packed, near, other, up, crossing):
    whole = near[...] + other[...]
    up[...] = whole
    crossing[...] = jnp.where(lax.axis_index("slab") % 2 == 1, packed[...], whole)


def near_kernel(rest, stepped, near, crossing):
    whole = rest[...] - stepped[...]
    near[...] = whole
    crossing[...] = jnp.where(lax.axis_index("slab") % 2 == 1, whole, stepped[...])


def join_kernel(spacing, base, more, less, out):
    s = lax.axis_index("slab")
    left = s % (2 * spacing) == 0
    out[...] = base[...] - keep(left & (s > 0), more) - keep(left, less)


def ham_kernel(slabs, near, far, next_near, next_far, own_e, mate_e, own_t, mate_t, *refs):
    out, here, there = refs[-3:]
    s = lax.axis_index("slab")
    load_vector(here, near[...], far[...])
    out[...] = near[...] - half_step * rotate(real_product(own_e[0], mate_e[0], here))

    @pl.when((s % 2 == 1) & (s < slabs - 1))
    def _():
        load_vector(there, next_near[...], next_far[...])
        out[...] -= half_step * rotate(real_product(own_t[0], mate_t[0], there))


def even_kernel(rest, next_near, next_far, own, mate, out, store):
    @pl.when(lax.axis_index("slab") % 2 == 0)
    def _():
        load_vector(store, next_near[...], next_far[...])
        out[...] = rest[...] - half_step * rotate(real_product(own[0], mate[0], store))


def level_kernel(spacing, near, far, own, mate, *refs):
    beneath, above, store = refs[-3:]

    @pl.when(lax.axis_index("slab") % (2 * spacing) == spacing)
    def _():
        load_vector(store, near[...], far[...])
        above[...] = complex_product(own[2:4], mate[2:4], store)
        beneath[...] = complex_product(own[0:2], mate[0:2], store)


def over_kernel(spacing, near, far, own, mate, *refs):
    tail, _, out, store = refs

    @pl.when(lax.axis_index("slab") % (2 * spacing) == spacing)
    def _():
        load_vector(store, near[...], far[...])
        out[...] = complex_product(own[2:4], mate[2:4], store) + tail[...]


def top_kernel(spacing, near, far, own, mate, *refs):
    beneath, store = refs[-2:]

    @pl.when(lax.axis_index("slab") % (2 * spacing) == spacing)
    def _():
        load_vector(store, near[...], far[...])
        beneath[...] = complex_product(own[0:2], mate[0:2], store)


def pivot_kernel(spacing, near, far, own, mate, before, *refs):
    out, store = refs[-2:]
    active = lax.axis_index("slab") % (2 * spacing) == spacing

    @pl.when(active)
    def _():
        load_vector(store, near[...], far[...])
        out[...] = complex_product(own[4:6], mate[4:6], store)

    @pl.when(jnp.logical_not(active))
    def _():
        out[...] = before[...]


def root_kernel(count, *refs):
    near, far = refs[:2]
    shares = refs[2 : 2 + 2 * count]
    own, mate, before, out, store = refs[2 + 2 * count :]
    root = lax.axis_index("slab") == 0

    @pl.when(root)
    def _():
        whole = [near[...], far[...]]
        for n, share in enumerate(shares):
            whole[n % 2] = whole[n % 2] - share[...]
        load_vector(store, *whole)
        out[...] = complex_product(own[4:6], mate[4:6], store)

    @pl.when(jnp.logical_not(root))
    def _():
        out[...] = before[...]


def settle_kernel(spacing, part, near, far, own, mate, out, store):
    active = lax.axis_index("slab") % (2 * spacing) == spacing

    @pl.when(active)
    def _():
        load_vector(store, near[...], far[...])
        out[...] = part[...] - complex_product(own[6:8], mate[6:8], store)

    @pl.when(jnp.logical_not(active))
    def _():
        out[...] = part[...]


def both_kernel(slabs, spacing, count, part, other, *refs):
    vectors = refs[:4]
    early = refs[4:count]
    own, mate, out, lower, upper = refs[count:]
    s = lax.axis_index("slab")
    active = s % (2 * spacing) == spacing
    first = s % (4 * spacing) == spacing
    linked = s + spacing < slabs

    def pick(n, wanted):
        values = vectors[n][...]
        return jnp.where(wanted, early[n][...], values) if n < len(early) else values

    @pl.when(active)
    def _():
        load_vector(lower, pick(0, first), pick(1, first))
        out[...] = part[...] - complex_product(own[6:8], mate[6:8], lower)

    @pl.when(active & linked)
    def _():
        second = jnp.logical_not(first)
        load_vector(upper, pick(2, second), pick(3, second))
        out[...] -= complex_product(own[8:10], mate[8:10], upper)

    @pl.when(jnp.logical_not(active))
    def _():
        out[...] = other[...]


def call(
    kernel,
    *operands,
    outs=1,
    scratch=(),
    unused=(),
    shape=jax.ShapeDtypeStruct((Q, LANES), wide),
    flops=10**9,
):
    vmem = pl.BlockSpec(memory_space=pltpu.VMEM)
    return pl.pallas_call(
        kernel,
        out_shape=shape if outs == 1 else (shape,) * outs,
        in_specs=[vmem] * len(operands) + [pl.BlockSpec(memory_space=pl.ANY)] * len(unused),
        out_specs=vmem if outs == 1 else (vmem,) * outs,
        scratch_shapes=list(scratch),
        cost_estimate=pl.CostEstimate(flops=flops, bytes_accessed=1, transcendentals=0),
        compiler_params=pltpu.CompilerParams(vmem_limit_bytes=16 * 2**20),
    )(*operands, *unused)


def completed(route, count, cols):
    target = dict(route)
    taken = set(target.values())
    for a in [a for a in range(count) if a not in target and a not in taken]:
        target[a] = a ^ 1
        taken.add(a ^ 1)
    for a in range(count):
        if a not in target:
            target[a] = next(b for b in range(count) if b not in taken and b % cols == a % cols)
            taken.add(target[a])
    if sorted(target.values()) != list(range(count)):
        raise ValueError("no permutation")
    return sorted(target.items())


def per_device(slabs, cols, waves, energy, tunnel, pivots, below, above, back_lower, back_upper):
    everyone = range(cols)
    width = energy.shape[2]
    store = pltpu.VMEM((width, LANES), short)
    levels = slabs.bit_length() - 1
    every = range(slabs)

    def send(values, moves, flip=0):
        route = []
        for c in everyone:
            for a, b, *h in moves:
                route.append((a * cols + c, b * cols + (c ^ flip)))
                here = b * cols + (c ^ flip)
                for h in h:
                    route.append((here, h * cols + c))
                    here = h * cols + c
                if here != b * cols + (c ^ flip):
                    route.append((here, a * cols + c))
        return lax.ppermute(values, ("slab", "col"), completed(route, slabs * cols, cols))

    def both(values, near_moves, far_moves):
        return send(values, near_moves), send(values, far_moves, 2)

    def swap(values):
        return send(values, [(a, a) for a in every], 1)

    def exchange(values, chosen=every):
        return send(values, [(a, a) for a in chosen], 2)

    def kernel(body, *arguments):
        return functools.partial(body, *arguments)

    def stack(*arrays, after):
        depth = sum(v.shape[0] for v in arrays)
        shape = jax.ShapeDtypeStruct((depth, Q, width), wide)
        return call(stack_kernel, *arrays, unused=(after,), shape=shape, flops=1)

    mate_waves = swap(waves)
    t_pair = tunnel, swap(tunnel)
    e_pair = energy, swap(energy)
    side = call(side_kernel, shape=jax.ShapeDtypeStruct((8, LANES), jnp.int32))
    psi, up_near, up_far = call(
        open_kernel, waves, mate_waves, side, *t_pair, outs=3, scratch=[pltpu.VMEM((64, width), wide)]
    )
    up, crossing = call(cross_kernel, psi, up_near, exchange(up_far), outs=2, flops=1)
    psi_far = exchange(psi)
    between = [(a, b) for k in every[1:-1:2] for a, b in ((k, k + 1), (k + 1, k))]
    stepped = send(crossing, [(a, a ^ 1) for a in every])
    rest = call(
        kernel(ham_kernel, slabs),
        psi,
        psi_far,
        *both(psi, between, between),
        *e_pair,
        *t_pair,
        scratch=[store, store],
        unused=(up,),
    )
    near, crossing = call(near_kernel, rest, stepped, outs=2, flops=1)
    far = exchange(crossing)
    blocks = below[0], above[0], pivots[0], back_lower[0], back_upper[0]
    front = stack(*blocks, after=near)
    front = front, swap(front)
    back = front
    base = call(even_kernel, rest, stepped, far, *t_pair, scratch=[store])

    pivot = near
    for level in range(levels):
        d = 2**level
        if level == levels - 1:
            beneath = call(kernel(top_kernel, d), near, far, *front, scratch=[store])
            shares = both(beneath, [(d, 0, 1, d + 1)], [(d, 0, 1, d - 1)])
            pivot = call(kernel(pivot_kernel, d), near, far, *back, pivot, scratch=[store])
            pivot = call(
                kernel(root_kernel, len(shares) // 2),
                base,
                base_far,
                *shares,
                *back,
                pivot,
                scratch=[store],
            )
            break
        if level > 0:
            beneath, over = call(
                kernel(level_kernel, d), near, far, *front, outs=2, scratch=[store]
            )
        else:
            beneath = call(kernel(top_kernel, d), near, far, *front, scratch=[store])
            over = call(
                kernel(over_kernel, d), near, far, *front, up, scratch=[store], unused=(beneath,)
            )
        if level == 0:
            more = send(over, between)
            less = send(beneath, [(a, a ^ 1) for a in every])
            pivot = call(
                kernel(pivot_kernel, d),
                near,
                far,
                *back,
                pivot,
                scratch=[store],
                unused=(over,),
                flops=1,
            )
            base = near = call(kernel(join_kernel, d), base, more, less)
            base_far = far = exchange(near, every[::2])
            continue
        active = [a for a in every if a % (2 * d) == d]

        def ways(step, helper):
            moves = []
            for a in active:
                b = a + step
                if b % (4 * d) == 2 * d:
                    moves.append((a, b, a + helper))
                elif b < slabs:
                    moves += [(a, b), (b, a)]
            return moves

        more = both(over, ways(d, 1), ways(d, -1))
        less = both(beneath, ways(-d, -1), ways(-d, 1))
        pivot = call(kernel(pivot_kernel, d), near, far, *back, pivot, scratch=[store])
        near = base = call(kernel(join_kernel, d), base, more[0], less[0])
        far = base_far = call(kernel(join_kernel, d), base_far, more[1], less[1])

    solved = pivot
    for level in reversed(range(levels)):
        d = 2**level
        sources = [a for a in every if a % (2 * d) == 0]
        upper = [a for a in sources if a > 0]
        if d == 1:
            low_near = send(solved, [(a, a ^ 1) for a in every])
            ways = [(a, a - 1) for a in upper] + [(a - 1, a) for a in upper]
            up_near = send(solved, ways)
            up_far = send(solved, ways, 2)
            low_far = exchange(low_near, [a + 1 for a in sources])
            vectors = low_near, low_far, up_near, up_far
        elif level == levels - 1:
            vectors = both(solved, [(0, d, d + 1, 1)], [(0, d, d + 1, 1)])
        else:
            sources = [a for a in every if a % (4 * d) == 2 * d]
            up_near = send(solved, [(a, a - d, a - d + 1, a + 1) for a in sources])
            up_far = send(solved, [(a, a - d, a - d + 1, a + 1) for a in sources], 2)
            low_far = send(solved, [(a, a + d, a + d + 1, a + 1) for a in sources], 2)
            low_near = send(solved, [(a, a + d, a + d + 1, a + 1) for a in sources])
            vectors = (low_near, low_far, up_near, up_far) + early
        if level > 1:
            half = d // 2
            sources = [a for a in every if a % (2 * d) == 0]
            ways = [(a, a + half, a + half + 1, a + 1) for a in sources]
            early = both(solved, ways, ways)
            if len(sources) > 1:
                ways = [(a, a - half, a - half + 1, a + 1) for a in sources if a > 0]
                early += both(solved, ways, ways)
        if level == levels - 1 and levels > 1:
            solved = call(kernel(settle_kernel, d), pivot, *vectors, *back, scratch=[store])
        else:
            solved = call(
                kernel(both_kernel, slabs, d, len(vectors)),
                pivot,
                solved,
                *vectors,
                *back,
                scratch=[store, store],
            )
    out = call(regroup_kernel, solved, swap(solved))
    return out[None]


def solution(mesh):
    slabs, cols = mesh.shape["slab"], mesh.shape["col"]
    vector = P("slab", "col", None)
    block = P("slab", None, "col", None)
    return jax.shard_map(
        functools.partial(per_device, slabs, cols),
        mesh=mesh,
        in_specs=(vector,) * 3 + (block,) * 5,
        out_specs=vector,
        check_vma=False,
    )
```

```python
import functools

import jax
import jax.numpy as jnp
from jax import lax
from jax.experimental import pallas as pl
from jax.experimental.pallas import tpu as pltpu
from jax.sharding import PartitionSpec as P


half_step = 0.5
wide = jnp.float32
short = jnp.bfloat16
Q = 128
LANES = 128


def lanes(values):
    return lax.broadcasted_iota(jnp.int32, values.shape, 1)


def swap_halves(values):
    return pltpu.roll(values, 64, 1)


def join(left, right):
    return jnp.where(lanes(left) < 64, left, right)


def rotate(values):
    even = lanes(values) % 2 == 0
    return jnp.where(even, -pltpu.roll(values, LANES - 1, 1), pltpu.roll(values, 1, 1))


def split(values):
    high = values.astype(short)
    return high, (values - high.astype(wide)).astype(short)


def quarter(number):
    return pl.ds(pl.multiple_of(number * Q, Q), Q)


def spread(store, packed, first):
    high = packed.astype(short).astype(wide)
    low = packed - high
    store[quarter(first), :] = join(high, swap_halves(low)).astype(short)
    store[quarter(first ^ 1), :] = join(swap_halves(high), low).astype(short)


def load_vector(store, near, far):
    c = lax.axis_index("col")
    spread(store, near, c)
    spread(store, far, c ^ 2)


def keep(wanted, values):
    return jnp.where(wanted, values[...], 0.0)


def rows_product(block, store):
    high, low = split(block)
    vector = store[...]
    return jnp.dot(high, vector, preferred_element_type=wide) + jnp.dot(
        low, vector, preferred_element_type=wide
    )


def fold(values):
    return values + swap_halves(values)


def real_product(own, mate, store):
    return join(fold(rows_product(own, store)), fold(rows_product(mate, store)))


def complex_half(block, store):
    both = rows_product(block.reshape(2 * Q, block.shape[-1]), store)
    return fold(both[:Q] + rotate(both[Q:]))


def complex_product(own, mate, store):
    return join(complex_half(own, store), complex_half(mate, store))


def this_core(left, right):
    first = lax.axis_index("col") % 2 == 0
    return jnp.where(first, join(left, swap_halves(right)), join(swap_halves(left), right))


def side_kernel(side):
    side[...] = jnp.zeros_like(side) + lax.axis_index("col")


def regroup_kernel(mine, other, out):
    rows = join(mine[...], other[...])
    out[...] = jnp.where(lax.axis_index("col") % 2 == 0, rows, swap_halves(rows))


def stack_kernel(*refs):
    *sources, _, out = refs
    place = 0
    for source in sources:
        depth = source.shape[0]
        out[place : place + depth] = source[...]
        place += depth


def open_kernel(mine, other, side, own, mate, psi, near, far, store):
    c = lax.axis_index("col")
    packed = this_core(mine[0], other[0])
    psi[...] = packed
    turned = packed.T
    total = None
    for rows, block in ((turned[:64], own[0]), (turned[64:], mate[0])):
        high, low = split(rows)
        pair = jnp.concatenate([high, low], axis=0)
        block_high, block_low = split(block)
        part = jnp.dot(pair, block_high, preferred_element_type=wide) + jnp.dot(
            pair, block_low, preferred_element_type=wide
        )
        part = part[:64] + part[64:]
        total = part if total is None else total + part
    store[...] = total
    for out, first in ((far, c ^ 2), (near, c)):
        pair = jnp.concatenate(
            [store[:, quarter(first)], store[:, quarter(first ^ 1)]], axis=0
        )
        out[...] = half_step * rotate(pair.T)


def cross_kernel(packed, near, other, up, crossing):
    whole = near[...] + other[...]
    up[...] = whole
    crossing[...] = jnp.where(lax.axis_index("slab") % 2 == 1, packed[...], whole)


def near_kernel(rest, stepped, near, crossing):
    whole = rest[...] - stepped[...]
    near[...] = whole
    crossing[...] = jnp.where(lax.axis_index("slab") % 2 == 1, whole, stepped[...])


def join_kernel(spacing, base, more, less, out):
    s = lax.axis_index("slab")
    left = s % (2 * spacing) == 0
    out[...] = base[...] - keep(left & (s > 0), more) - keep(left, less)


def ham_kernel(slabs, near, far, next_near, next_far, own_e, mate_e, own_t, mate_t, *refs):
    out, here, there = refs[-3:]
    s = lax.axis_index("slab")
    load_vector(here, near[...], far[...])
    out[...] = near[...] - half_step * rotate(real_product(own_e[0], mate_e[0], here))

    @pl.when((s % 2 == 1) & (s < slabs - 1))
    def _():
        load_vector(there, next_near[...], next_far[...])
        out[...] -= half_step * rotate(real_product(own_t[0], mate_t[0], there))


def even_kernel(rest, next_near, next_far, own, mate, out, store):
    @pl.when(lax.axis_index("slab") % 2 == 0)
    def _():
        load_vector(store, next_near[...], next_far[...])
        out[...] = rest[...] - half_step * rotate(real_product(own[0], mate[0], store))


def level_kernel(spacing, near, far, own, mate, *refs):
    beneath, above, store = refs[-3:]

    @pl.when(lax.axis_index("slab") % (2 * spacing) == spacing)
    def _():
        load_vector(store, near[...], far[...])
        above[...] = complex_product(own[2:4], mate[2:4], store)
        beneath[...] = complex_product(own[0:2], mate[0:2], store)


def over_kernel(spacing, near, far, own, mate, *refs):
    tail, _, out, store = refs

    @pl.when(lax.axis_index("slab") % (2 * spacing) == spacing)
    def _():
        load_vector(store, near[...], far[...])
        out[...] = complex_product(own[2:4], mate[2:4], store) + tail[...]


def top_kernel(spacing, near, far, own, mate, *refs):
    beneath, store = refs[-2:]

    @pl.when(lax.axis_index("slab") % (2 * spacing) == spacing)
    def _():
        load_vector(store, near[...], far[...])
        beneath[...] = complex_product(own[0:2], mate[0:2], store)


def pivot_kernel(spacing, near, far, own, mate, before, *refs):
    out, store = refs[-2:]
    active = lax.axis_index("slab") % (2 * spacing) == spacing

    @pl.when(active)
    def _():
        load_vector(store, near[...], far[...])
        out[...] = complex_product(own[4:6], mate[4:6], store)

    @pl.when(jnp.logical_not(active))
    def _():
        out[...] = before[...]


def root_kernel(count, *refs):
    near, far = refs[:2]
    shares = refs[2 : 2 + 2 * count]
    own, mate, before, out, store = refs[2 + 2 * count :]
    root = lax.axis_index("slab") == 0

    @pl.when(root)
    def _():
        whole = [near[...], far[...]]
        for n, share in enumerate(shares):
            whole[n % 2] = whole[n % 2] - share[...]
        load_vector(store, *whole)
        out[...] = complex_product(own[4:6], mate[4:6], store)

    @pl.when(jnp.logical_not(root))
    def _():
        out[...] = before[...]


def settle_kernel(spacing, part, near, far, own, mate, out, store):
    active = lax.axis_index("slab") % (2 * spacing) == spacing

    @pl.when(active)
    def _():
        load_vector(store, near[...], far[...])
        out[...] = part[...] - complex_product(own[6:8], mate[6:8], store)

    @pl.when(jnp.logical_not(active))
    def _():
        out[...] = part[...]


def side_term_kernel(slabs, lower, part, other, near, far, own, mate, out, store):
    s = lax.axis_index("slab")
    active = s % 2 == 1
    linked = (s + 1 < slabs) | lower
    first, last = (6, 8) if lower else (8, 10)

    @pl.when(active & linked)
    def _():
        load_vector(store, near[...], far[...])
        out[...] = part[...] - complex_product(own[first:last], mate[first:last], store)

    @pl.when(active & jnp.logical_not(linked))
    def _():
        out[...] = part[...]

    @pl.when(jnp.logical_not(active))
    def _():
        out[...] = other[...]


def both_kernel(slabs, spacing, count, part, other, *refs):
    vectors = refs[:4]
    early = refs[4:count]
    own, mate, out, lower, upper = refs[count:]
    s = lax.axis_index("slab")
    active = s % (2 * spacing) == spacing
    first = s % (4 * spacing) == spacing
    linked = s + spacing < slabs

    def pick(n, wanted):
        values = vectors[n][...]
        return jnp.where(wanted, early[n][...], values) if n < len(early) else values

    @pl.when(active)
    def _():
        load_vector(lower, pick(0, first), pick(1, first))
        out[...] = part[...] - complex_product(own[6:8], mate[6:8], lower)

    @pl.when(active & linked)
    def _():
        second = jnp.logical_not(first)
        load_vector(upper, pick(2, second), pick(3, second))
        out[...] -= complex_product(own[8:10], mate[8:10], upper)

    @pl.when(jnp.logical_not(active))
    def _():
        out[...] = other[...]


def call(
    kernel,
    *operands,
    outs=1,
    scratch=(),
    unused=(),
    shape=jax.ShapeDtypeStruct((Q, LANES), wide),
    flops=10**9,
):
    vmem = pl.BlockSpec(memory_space=pltpu.VMEM)
    return pl.pallas_call(
        kernel,
        out_shape=shape if outs == 1 else (shape,) * outs,
        in_specs=[vmem] * len(operands) + [pl.BlockSpec(memory_space=pl.ANY)] * len(unused),
        out_specs=vmem if outs == 1 else (vmem,) * outs,
        scratch_shapes=list(scratch),
        cost_estimate=pl.CostEstimate(flops=flops, bytes_accessed=1, transcendentals=0),
        compiler_params=pltpu.CompilerParams(vmem_limit_bytes=16 * 2**20),
    )(*operands, *unused)


def completed(route, count, cols):
    target = dict(route)
    taken = set(target.values())
    for a in [a for a in range(count) if a not in target and a not in taken]:
        target[a] = a ^ 1
        taken.add(a ^ 1)
    for a in range(count):
        if a not in target:
            target[a] = next(b for b in range(count) if b not in taken and b % cols == a % cols)
            taken.add(target[a])
    if sorted(target.values()) != list(range(count)):
        raise ValueError("no permutation")
    return sorted(target.items())


def per_device(slabs, cols, waves, energy, tunnel, pivots, below, above, back_lower, back_upper):
    everyone = range(cols)
    width = energy.shape[2]
    store = pltpu.VMEM((width, LANES), short)
    levels = slabs.bit_length() - 1
    every = range(slabs)

    def send(values, moves, flip=0):
        route = []
        for c in everyone:
            for a, b, *h in moves:
                route.append((a * cols + c, b * cols + (c ^ flip)))
                here = b * cols + (c ^ flip)
                for h in h:
                    route.append((here, h * cols + c))
                    here = h * cols + c
                if here != b * cols + (c ^ flip):
                    route.append((here, a * cols + c))
        return lax.ppermute(values, ("slab", "col"), completed(route, slabs * cols, cols))

    def both(values, near_moves, far_moves):
        return send(values, near_moves), send(values, far_moves, 2)

    def swap(values):
        return send(values, [(a, a) for a in every], 1)

    def exchange(values, chosen=every):
        return send(values, [(a, a) for a in chosen], 2)

    def kernel(body, *arguments):
        return functools.partial(body, *arguments)

    def stack(*arrays, after):
        depth = sum(v.shape[0] for v in arrays)
        shape = jax.ShapeDtypeStruct((depth, Q, width), wide)
        return call(stack_kernel, *arrays, unused=(after,), shape=shape, flops=1)

    mate_waves = swap(waves)
    t_pair = tunnel, swap(tunnel)
    e_pair = energy, swap(energy)
    side = call(side_kernel, shape=jax.ShapeDtypeStruct((8, LANES), jnp.int32))
    psi, up_near, up_far = call(
        open_kernel, waves, mate_waves, side, *t_pair, outs=3, scratch=[pltpu.VMEM((64, width), wide)]
    )
    up, crossing = call(cross_kernel, psi, up_near, exchange(up_far), outs=2, flops=1)
    psi_far = exchange(psi)
    between = [(a, b) for k in every[1:-1:2] for a, b in ((k, k + 1), (k + 1, k))]
    stepped = send(crossing, [(a, a ^ 1) for a in every])
    rest = call(
        kernel(ham_kernel, slabs),
        psi,
        psi_far,
        *both(psi, between, between),
        *e_pair,
        *t_pair,
        scratch=[store, store],
        unused=(up,),
    )
    near, crossing = call(near_kernel, rest, stepped, outs=2, flops=1)
    far = exchange(crossing)
    blocks = below[0], above[0], pivots[0], back_lower[0], back_upper[0]
    front = stack(*blocks, after=near)
    front = front, swap(front)
    back = front
    base = call(even_kernel, rest, stepped, far, *t_pair, scratch=[store])

    pivot = near
    for level in range(levels):
        d = 2**level
        if level == levels - 1:
            beneath = call(kernel(top_kernel, d), near, far, *front, scratch=[store])
            shares = both(beneath, [(d, 0, 1, d + 1)], [(d, 0, 1, d - 1)])
            pivot = call(kernel(pivot_kernel, d), near, far, *back, pivot, scratch=[store])
            pivot = call(
                kernel(root_kernel, len(shares) // 2),
                base,
                base_far,
                *shares,
                *back,
                pivot,
                scratch=[store],
            )
            break
        if level > 0:
            beneath, over = call(
                kernel(level_kernel, d), near, far, *front, outs=2, scratch=[store]
            )
        else:
            beneath = call(kernel(top_kernel, d), near, far, *front, scratch=[store])
            over = call(
                kernel(over_kernel, d), near, far, *front, up, scratch=[store], unused=(beneath,)
            )
        if level == 0:
            more = send(over, between)
            less = send(beneath, [(a, a ^ 1) for a in every])
            pivot = call(
                kernel(pivot_kernel, d),
                near,
                far,
                *back,
                pivot,
                scratch=[store],
                unused=(over,),
                flops=1,
            )
            base = near = call(kernel(join_kernel, d), base, more, less)
            base_far = far = exchange(near, every[::2])
            continue
        active = [a for a in every if a % (2 * d) == d]
        rising = [a for a in active if a + d < slabs]
        more = both(
            over, [(a, a + d, a + 1) for a in rising], [(a, a + d, a - 1) for a in rising]
        )
        less = both(
            beneath, [(a, a - d, a - 1) for a in active], [(a, a - d, a + 1) for a in active]
        )
        pivot = call(kernel(pivot_kernel, d), near, far, *back, pivot, scratch=[store])
        near = base = call(kernel(join_kernel, d), base, more[0], less[0])
        far = base_far = call(kernel(join_kernel, d), base_far, more[1], less[1])

    solved = pivot
    for level in reversed(range(levels)):
        d = 2**level
        sources = [a for a in every if a % (2 * d) == 0]
        upper = [a for a in sources if a > 0]
        if d == 1:
            low_near = send(solved, [(a, a ^ 1) for a in every])
            ways = [(a, a - 1) for a in upper] + [(a - 1, a) for a in upper]
            up_near = send(solved, ways)
            up_far = send(solved, ways, 2)
            low_far = exchange(low_near, [a + 1 for a in sources])
            vectors = low_near, low_far, up_near, up_far
        elif level == levels - 1:
            vectors = both(solved, [(0, d, d + 1, 1)], [(0, d, d + 1, 1)])
        else:
            sources = [a for a in every if a % (4 * d) == 2 * d]
            up_near = send(solved, [(a, a - d, a - d + 1, a + 1) for a in sources])
            up_far = send(solved, [(a, a - d, a - d + 1, a + 1) for a in sources], 2)
            low_far = send(solved, [(a, a + d, a + d + 1, a + 1) for a in sources], 2)
            low_near = send(solved, [(a, a + d, a + d + 1, a + 1) for a in sources])
            vectors = (low_near, low_far, up_near, up_far) + early
        if level > 1:
            half = d // 2
            sources = [a for a in every if a % (2 * d) == 0]
            ways = [(a, a + half, a + half + 1, a + 1) for a in sources]
            early = both(solved, ways, ways)
            if len(sources) > 1:
                ways = [(a, a - half, a - half + 1, a + 1) for a in sources if a > 0]
                early += both(solved, ways, ways)
        if level == levels - 1 and levels > 1:
            solved = call(kernel(settle_kernel, d), pivot, *vectors, *back, scratch=[store])
        elif d == 1:
            args = dict(scratch=[store], flops=1)
            part = call(
                kernel(side_term_kernel, slabs, False), pivot, solved, *vectors[2:], *back, **args
            )
            solved = call(
                kernel(side_term_kernel, slabs, True), part, solved, *vectors[:2], *back, **args
            )
        else:
            solved = call(
                kernel(both_kernel, slabs, d, len(vectors)),
                pivot,
                solved,
                *vectors,
                *back,
                scratch=[store, store],
            )
    out = call(regroup_kernel, solved, swap(solved))
    return out[None]


def solution(mesh):
    slabs, cols = mesh.shape["slab"], mesh.shape["col"]
    vector = P("slab", "col", None)
    block = P("slab", None, "col", None)
    return jax.shard_map(
        functools.partial(per_device, slabs, cols),
        mesh=mesh,
        in_specs=(vector,) * 3 + (block,) * 5,
        out_specs=vector,
        check_vma=False,
    )
```
